32 devices in a mesh: comp: 4 (over x, core), tile: 4 (over z), rep: 2 (over y).
Axes of the slice: x: 2, y: 2, z: 4, core: 2. Of those that a mesh axis runs over, the one named last changes fastest.
Arguments:
- retarded: bfloat16 [2, 16, 2, 192, 192], P(None, ('tile', 'rep')), may hold values from -0.3125 to 0.3125
- self_energy: bfloat16 [4, 16, 2, 192, 192], P('comp', ('tile', 'rep')), may hold values from -6 to 6
- energy_of: int32 [16], replicated, may hold values from 0 to 15, each once
Outputs:
- polar: float32 [4, 16, 2, 192, 192], P('comp', 'tile', None, 'rep')
The draws below stay inside these ranges and needn't reach their ends.
Inputs may be any that keep to these rules, and one draw needn't show every extreme that they name: `energy_of`: each of the 16 energy grid indices stands in exactly one slot.
All inputs are finite; a program needn't handle non-finite values.
Results may differ from the reference program's by a relative error of at most 0.0095.
Values may be sent and summed in bfloat16 or wider, within the bound.
A program may use at most 64 MiB of HBM per device.

```python
import math
import jax
import jax.numpy as jnp
from jax import lax

NB = 192
NE = 16


def block_scale(stream_key, shape, cuts, smallest, largest):
    factor_of = 1.0
    for dim, blocks in cuts:
        heights = jax.random.uniform(jax.random.fold_in(jax.random.fold_in(stream_key, 6), dim), (blocks,), jnp.float32, smallest / len(cuts), largest / len(cuts))
        factor_of = factor_of * jnp.repeat(jnp.exp(heights), shape[dim] // blocks).reshape((-1,) + (1,) * (len(shape) - 1 - dim))
    return factor_of


def scatter_about(own_key, dims, spread, bound, shards=(), held_as=jnp.bfloat16):
    result = jax.random.normal(own_key, dims, jnp.float32) * spread
    if len(shards) > 0:
        result = block_scale(own_key, dims, shards, -0.22, 0.18) * result
    return jnp.clip(result, min=-bound, max=bound).astype(held_as)


def setup_inputs(seed: int = 0) -> dict:
    key_list = jax.random.split(jax.random.key(seed), 4)
    retarded = scatter_about(key_list[0], (2, NE, 2, NB, NB), (2 * NB) ** -0.5, 0.3125, ((1, 8),))
    self_energy = scatter_about(key_list[1], (4, NE, 2, NB, NB), 1.0, 6.0, ((0, 4), (1, 8)))
    energy_of = jax.random.permutation(key_list[2], NE).astype(jnp.int32)
    return {"retarded": retarded, "self_energy": self_energy, "energy_of": energy_of}


def product(left_side, right_side):
    return jnp.dot(left_side, right_side, preferred_element_type=jnp.float32)

def triple(operands):
    green_matrix, sigma_matrix = operands
    green_re, green_im = (green_matrix[0], green_matrix[1])
    sigma_re, sigma_im = (sigma_matrix[0], sigma_matrix[1])
    left_re = (product(green_re, sigma_re) - product(green_im, sigma_im)).astype(jnp.bfloat16)
    left_im = (product(green_re, sigma_im) + product(green_im, sigma_re)).astype(jnp.bfloat16)
    out_re = product(left_re, green_re.T) + product(left_im, green_im.T)
    out_im = product(left_im, green_re.T) - product(left_re, green_im.T)
    return jnp.stack([out_re, out_im]).astype(jnp.bfloat16)

def reference(retarded, self_energy, energy_of):
    slot_count = energy_of.shape[0]
    freq_count = 2 * slot_count
    forward = []
    backward = []
    for component in range(4):
        green_all = lax.map(triple, (retarded[component // 2], self_energy[component]))
        if component % 2 == 1:
            green_all = jnp.swapaxes(green_all, 2, 3)
        ordered = jnp.zeros_like(green_all).at[energy_of].set(green_all)
        signal = ordered[:, 0].astype(jnp.float32) + 1j * ordered[:, 1].astype(jnp.float32)
        spectrum = jnp.fft.fft(signal, n=freq_count, axis=0)
        forward.append(spectrum)
        backward.append(jnp.concatenate([spectrum[:1], jnp.flip(spectrum[1:], axis=0)], axis=0))
    results = []
    for component in range(4):
        joint = forward[component] * backward[component ^ 1]
        joint_re = jnp.real(joint).astype(jnp.bfloat16).astype(jnp.float32)
        joint_im = jnp.imag(joint).astype(jnp.bfloat16).astype(jnp.float32)
        lagged = jnp.fft.ifft(joint_re + 1j * joint_im, axis=0)[:slot_count]
        polar_value = -1j * lagged / math.sqrt(slot_count)
        results.append(jnp.stack([jnp.real(polar_value), jnp.imag(polar_value)], axis=1))
    return jnp.stack(results).astype(jnp.float32)
```

```python
import functools
import math

import jax
import jax.numpy as jnp
from jax import lax
from jax.experimental import pallas as pl
from jax.experimental.pallas import tpu as pltpu
from jax.sharding import PartitionSpec as P


def from_partner(array, axis, distance):
    return lax.ppermute(array, axis, [(i, i ^ 1 << distance) for i in range(lax.axis_size(axis))])


def batched(left_side, right_side, pattern):
    return jnp.einsum(pattern, left_side, right_side, preferred_element_type=jnp.float32)


def phase_tables(row_values, col_values, modulus):
    phase_index = row_values[:, None] * col_values[None, :] % modulus
    phase_angle = phase_index.astype(jnp.float32) * (2.0 * math.pi / modulus)
    cos_full = jnp.cos(phase_angle)
    sin_full = jnp.sin(phase_angle)
    cos_high = cos_full.astype(jnp.bfloat16)
    sin_high = sin_full.astype(jnp.bfloat16)
    cos_low = (cos_full - cos_high.astype(jnp.float32)).astype(jnp.bfloat16)
    sin_low = (sin_full - sin_high.astype(jnp.float32)).astype(jnp.bfloat16)
    return ((cos_high, cos_low), (sin_high, sin_low))


def split_dot(table_pair, values):
    return jnp.dot(table_pair[0], values, preferred_element_type=jnp.float32) + jnp.dot(
        table_pair[1], values, preferred_element_type=jnp.float32
    )


def rotate(cos_table, sin_table, value_re, value_im, direction):
    part_re = split_dot(cos_table, value_re) - direction * split_dot(sin_table, value_im)
    part_im = split_dot(cos_table, value_im) + direction * split_dot(sin_table, value_re)
    return (part_re, part_im)


def body(retarded, self_energy, energy_of):
    component = lax.axis_index("comp")
    momentum = component // 2
    greater = component % 2
    tile_count = lax.axis_size("tile")
    rep_count = lax.axis_size("rep")
    green_matrix = lax.dynamic_index_in_dim(retarded, momentum, 0, keepdims=False)
    sigma_matrix = self_energy[0]
    green_re, green_im = (green_matrix[:, 0], green_matrix[:, 1])
    sigma_re, sigma_im = (sigma_matrix[:, 0], sigma_matrix[:, 1])
    left_re = (
        batched(green_re, sigma_re, "eik,ekj->eij") - batched(green_im, sigma_im, "eik,ekj->eij")
    ).astype(jnp.bfloat16)
    left_im = (
        batched(green_re, sigma_im, "eik,ekj->eij") + batched(green_im, sigma_re, "eik,ekj->eij")
    ).astype(jnp.bfloat16)
    out_re = batched(left_re, green_re, "eik,ejk->eij") + batched(left_im, green_im, "eik,ejk->eij")
    out_im = batched(left_im, green_re, "eik,ejk->eij") - batched(left_re, green_im, "eik,ejk->eij")
    stacked = jnp.stack([out_re, out_im]).astype(jnp.bfloat16)
    stacked = jnp.where(greater == 1, jnp.swapaxes(stacked, 2, 3), stacked)
    energy_dev = stacked.shape[1]
    block_order = stacked.shape[2]
    elem_count = block_order * block_order // (tile_count * rep_count)
    slot_count = energy_of.shape[0]
    blocks = stacked.reshape(2, energy_dev, rep_count, tile_count, elem_count)
    first_pass = lax.all_to_all(blocks, "rep", split_axis=2, concat_axis=1, tiled=True)
    gathered = lax.all_to_all(first_pass, "tile", split_axis=3, concat_axis=1, tiled=True)
    signal = gathered.reshape(2, slot_count, elem_count)
    freq_count = 2 * slot_count
    frequency = lax.iota(jnp.int32, freq_count)
    fwd_cos, fwd_sin = phase_tables(frequency, energy_of, freq_count)
    own_re, own_im = rotate(fwd_cos, fwd_sin, signal[0], signal[1], -1.0)
    partner = from_partner(signal, "comp", 0)
    other_re, other_im = rotate(fwd_cos, fwd_sin, partner[0], partner[1], 1.0)
    cross_re = (own_re * other_re - own_im * other_im).astype(jnp.bfloat16)
    cross_im = (own_re * other_im + own_im * other_re).astype(jnp.bfloat16)
    lag_index = lax.iota(jnp.int32, slot_count)
    inv_cos, inv_sin = phase_tables(lag_index, frequency, freq_count)
    back_re, back_im = rotate(inv_cos, inv_sin, cross_re, cross_im, 1.0)
    norm_factor = 1.0 / (freq_count * math.sqrt(slot_count))
    polar_parts = jnp.stack([back_im * norm_factor, -back_re * norm_factor], axis=1)
    regrouped = lax.all_to_all(
        polar_parts[:, :, None, :], "tile", split_axis=0, concat_axis=2, tiled=True
    )
    lag_count = slot_count // tile_count
    return regrouped.reshape(lag_count, 2, block_order // rep_count, block_order)[None]


LANES = 128
ROWS = 8


def matmul(left_side, right_side, contract):
    return lax.dot_general(
        left_side, right_side, (((1,), (contract,)), ((), ())), preferred_element_type=jnp.float32
    )


def rotated(values):
    return pltpu.roll(values, LANES // 2, axis=1)


def polar_kernel(
    axis_sizes,
    retarded,
    self_energy,
    energy_of,
    polar,
    green_in,
    sigma_in,
    energies,
    outgoing,
    ordered,
    lagged,
    arrived,
    load_sem,
    first_send,
    first_recv,
    second_send,
    second_recv,
    *gathered,
):
    tile_count, rep_count = axis_sizes
    component = lax.axis_index("comp")
    tile = lax.axis_index("tile")
    rep = lax.axis_index("rep")
    momentum = component // 2
    greater = component % 2
    energy_dev, block_order = green_in.shape[0], green_in.shape[2]
    slot_count = energies.shape[0]
    unit_count = arrived.shape[0]
    lag_count = arrived.shape[1]
    row_count = block_order // rep_count
    low_units = row_count // ROWS
    owner_count = 2 * tile_count
    peer_count = owner_count * rep_count
    base_units = unit_count // owner_count
    has_spare = unit_count % owner_count != 0

    place = (tile * 2 + greater) * rep_count + rep
    owner = tile * 2 + greater

    def first_unit(which):
        return which * unit_count // owner_count

    def takes_spare(which):
        return first_unit(which + 1) - first_unit(which) > base_units

    def device_of(which_owner, which_rep):
        return (momentum * 2 + which_owner % 2, which_owner // 2, which_rep)

    loads = []
    for energy in range(energy_dev):
        loads.append(
            (
                pltpu.make_async_copy(
                    retarded.at[momentum, energy], green_in.at[energy], load_sem.at[2 * energy]
                ),
                pltpu.make_async_copy(
                    self_energy.at[0, energy], sigma_in.at[energy], load_sem.at[2 * energy + 1]
                ),
            )
        )
        for load in loads[-1]:
            load.start()
    energy_load = pltpu.make_async_copy(energy_of, energies, load_sem.at[2 * energy_dev])
    energy_load.start()

    barrier = pltpu.get_barrier_semaphore()
    for step in range(1, peer_count):
        peer = (place + step) % peer_count
        pl.semaphore_signal(
            barrier,
            inc=1,
            device_id=device_of(peer // rep_count, peer % rep_count),
            device_id_type=pl.DeviceIdType.MESH,
        )

    def finish(energy, left, right, sign):
        low, high = slice(0, LANES), slice(LANES, block_order)
        right_re, right_im = right
        with_re = jnp.concatenate(
            [right_re[low], -sign * right_im[low], right_re[high], -sign * right_im[high]]
        )
        with_im = jnp.concatenate(
            [right_im[low], sign * right_re[low], right_im[high], sign * right_re[high]]
        )
        result = matmul(left[0], with_re, 1) + matmul(left[1], with_im, 1)
        is_low = lax.broadcasted_iota(jnp.int32, (row_count // 2, LANES), 1) < LANES // 2
        for part in range(rep_count):
            rows = slice(part * row_count, (part + 1) * row_count)
            mixed = result[rows, 2 * LANES :]
            upper, lower = mixed[: row_count // 2], mixed[row_count // 2 :]
            high_re = jnp.where(is_low, upper, rotated(lower))
            high_im = jnp.where(is_low, rotated(upper), lower)
            pieces_re = jnp.concatenate([result[rows, :LANES], high_re])
            pieces_im = jnp.concatenate([result[rows, LANES : 2 * LANES], high_im])
            packed = jnp.concatenate(
                [
                    pieces_re.reshape(unit_count, ROWS, LANES),
                    pieces_im.reshape(unit_count, ROWS, LANES),
                ],
                axis=1,
            )
            outgoing[part, :, energy] = packed.astype(jnp.bfloat16)

    for energy in range(energy_dev):
        for load in loads[energy]:
            load.wait()
        green_re, green_im = green_in[energy, 0], green_in[energy, 1]
        sigma_re, sigma_im = sigma_in[energy, 0], sigma_in[energy, 1]
        left_re = (matmul(green_re, sigma_re, 0) - matmul(green_im, sigma_im, 0)).astype(jnp.bfloat16)
        left_im = (matmul(green_re, sigma_im, 0) + matmul(green_im, sigma_re, 0)).astype(jnp.bfloat16)

        @pl.when(greater == 0)
        def _():
            finish(energy, (left_re, left_im), (green_re, green_im), 1)

        @pl.when(greater == 1)
        def _():
            finish(energy, (green_re, green_im), (left_re, left_im), -1)

    pl.semaphore_wait(barrier, peer_count - 1)

    my_slot = greater * slot_count + (tile * rep_count + rep) * energy_dev

    def send_first(unit, spare):
        for step in range(1, peer_count):
            peer = (place + step) % peer_count
            peer_owner, peer_rep = peer // rep_count, peer % rep_count
            copy = pltpu.make_async_remote_copy(
                src_ref=outgoing.at[peer_rep, first_unit(peer_owner) + unit],
                dst_ref=gathered[unit].at[pl.ds(my_slot, energy_dev)],
                send_sem=first_send.at[unit],
                recv_sem=first_recv.at[unit],
                device_id=device_of(peer_owner, peer_rep),
                device_id_type=pl.DeviceIdType.MESH,
            )
            if spare:
                pl.when(takes_spare(peer_owner))(copy.start)
            else:
                copy.start()

    def keep_own(unit):
        gathered[unit][pl.ds(my_slot, energy_dev)] = outgoing[rep, first_unit(owner) + unit]

    def wait_for(buffer, sem):
        pltpu.make_async_copy(buffer, buffer, sem).wait()

    for unit in range(base_units):
        send_first(unit, False)
    if has_spare:
        send_first(base_units, True)
    for unit in range(base_units):
        keep_own(unit)
    if has_spare:
        pl.when(takes_spare(owner))(functools.partial(keep_own, base_units))

    energy_load.wait()
    slots = []
    for energy in range(slot_count):
        slot = 0
        for candidate in range(slot_count):
            slot = jnp.where(energies[candidate] == energy, candidate, slot)
        slots.append(slot)

    norm_factor = 1.0 / math.sqrt(slot_count)

    def correlate(unit):
        wait_for(
            gathered[unit].at[pl.ds(0, (peer_count - 1) * energy_dev)], first_recv.at[unit]
        )
        for part in range(2):
            for energy in range(slot_count):
                ordered[part, energy] = gathered[unit][part * slot_count + slots[energy]].astype(
                    jnp.float32
                )
        for lag in range(slot_count):
            for part in range(2):
                own_re = ordered[part, lag:, :ROWS]
                own_im = ordered[part, lag:, ROWS:]
                other_re = ordered[1 - part, : slot_count - lag, :ROWS]
                other_im = ordered[1 - part, : slot_count - lag, ROWS:]
                sum_re = jnp.sum(own_re * other_re - own_im * other_im, axis=0)
                sum_im = jnp.sum(own_re * other_im + own_im * other_re, axis=0)
                lagged[unit, part, lag] = jnp.concatenate(
                    [sum_im * norm_factor, sum_re * -norm_factor]
                ).astype(jnp.bfloat16)
        my_unit = first_unit(owner) + unit
        for step in range(1, owner_count):
            peer = (owner + step) % owner_count
            pltpu.make_async_remote_copy(
                src_ref=lagged.at[unit, peer % 2, pl.ds(peer // 2 * lag_count, lag_count)],
                dst_ref=arrived.at[my_unit],
                send_sem=second_send.at[unit],
                recv_sem=second_recv.at[unit],
                device_id=device_of(peer, rep),
                device_id_type=pl.DeviceIdType.MESH,
            ).start()
        arrived[my_unit] = lagged[unit, greater, pl.ds(tile * lag_count, lag_count)]

    for unit in range(base_units):
        correlate(unit)
    if has_spare:
        pl.when(takes_spare(owner))(functools.partial(correlate, base_units))

    for unit in range(base_units):
        wait_for(
            gathered[unit].at[pl.ds(0, (peer_count - 1) * energy_dev)], first_send.at[unit]
        )
        wait_for(arrived.at[pl.ds(0, owner_count - 1)], second_send.at[unit])
        wait_for(arrived.at[pl.ds(0, owner_count - 1)], second_recv.at[unit])
    if has_spare:
        spare_units = unit_count % owner_count
        spares = spare_units * rep_count

        @pl.when(takes_spare(owner))
        def _():
            if spares > 1:
                wait_for(
                    gathered[base_units].at[pl.ds(0, (spares - 1) * energy_dev)],
                    first_send.at[base_units],
                )
            wait_for(arrived.at[pl.ds(0, owner_count - 1)], second_send.at[base_units])
            if spare_units > 1:
                wait_for(arrived.at[pl.ds(0, spare_units - 1)], second_recv.at[base_units])

        @pl.when(jnp.logical_not(takes_spare(owner)))
        def _():
            wait_for(
                gathered[base_units].at[pl.ds(0, spares * energy_dev)], first_send.at[base_units]
            )
            wait_for(arrived.at[pl.ds(0, spare_units)], second_recv.at[base_units])

    for lag in range(lag_count):
        for unit in range(unit_count):
            values = arrived[unit, lag].astype(jnp.float32)
            for part in range(2):
                block = values[part * ROWS : (part + 1) * ROWS]
                if unit < low_units:
                    polar[0, lag, part, unit * ROWS : (unit + 1) * ROWS, :LANES] = block
                else:
                    row = (unit - low_units) * ROWS
                    row_low = row + row_count // 2
                    polar[0, lag, part, row : row + ROWS, LANES:] = block[:, : LANES // 2]
                    polar[0, lag, part, row_low : row_low + ROWS, LANES:] = rotated(block)[
                        :, : LANES // 2
                    ]


def fits(sizes, energy_dev, block_order):
    comp_count, tile_count, rep_count = sizes
    return (
        comp_count % 2 == 0
        and block_order == LANES + LANES // 2
        and block_order % (2 * ROWS * 2 * rep_count) == 0
        and block_order * 3 // (4 * ROWS * rep_count) >= 2 * tile_count
        and tile_count * rep_count * energy_dev <= 4 * ROWS
    )


def fused(sizes, retarded, self_energy, energy_of):
    _, tile_count, rep_count = sizes
    energy_dev, block_order = retarded.shape[1], retarded.shape[-1]
    slot_count = energy_of.shape[0]
    lag_count = slot_count // tile_count
    row_count = block_order // rep_count
    unit_count = row_count * block_order // (ROWS * LANES)
    units_held = -(-unit_count // (2 * tile_count))
    packed = (2 * ROWS, LANES)
    return pl.pallas_call(
        functools.partial(polar_kernel, (tile_count, rep_count)),
        out_shape=jax.ShapeDtypeStruct((1, lag_count, 2, row_count, block_order), jnp.float32),
        in_specs=[pl.BlockSpec(memory_space=pl.ANY)] * 3,
        out_specs=pl.BlockSpec(memory_space=pltpu.VMEM),
        scratch_shapes=[
            pltpu.VMEM(retarded.shape[1:], jnp.bfloat16),
            pltpu.VMEM(self_energy.shape[1:], jnp.bfloat16),
            pltpu.SMEM((slot_count,), jnp.int32),
            pltpu.VMEM((rep_count, unit_count, energy_dev) + packed, jnp.bfloat16),
            pltpu.VMEM((2, slot_count) + packed, jnp.float32),
            pltpu.VMEM((units_held, 2, slot_count) + packed, jnp.bfloat16),
            pltpu.VMEM((unit_count, lag_count) + packed, jnp.bfloat16),
            pltpu.SemaphoreType.DMA((2 * energy_dev + 1,)),
            pltpu.SemaphoreType.DMA((units_held,)),
            pltpu.SemaphoreType.DMA((units_held,)),
            pltpu.SemaphoreType.DMA((units_held,)),
            pltpu.SemaphoreType.DMA((units_held,)),
        ]
        + [pltpu.VMEM((2 * slot_count,) + packed, jnp.bfloat16)] * units_held,
        compiler_params=pltpu.CompilerParams(
            collective_id=0, has_side_effects=True, vmem_limit_bytes=40 * 2**20
        ),
    )(retarded, self_energy, energy_of)


def solution(mesh):
    placed = (
        P(None, ("tile", "rep"), None, None, None),
        P("comp", ("tile", "rep"), None, None, None),
        P(),
    )
    sizes = tuple(mesh.shape[name] for name in ("comp", "tile", "rep"))

    def device_body(retarded, self_energy, energy_of):
        if fits(sizes, retarded.shape[1], retarded.shape[-1]):
            return fused(sizes, retarded, self_energy, energy_of)
        return body(retarded, self_energy, energy_of)

    return jax.shard_map(
        device_body,
        mesh=mesh,
        in_specs=placed,
        out_specs=P("comp", "tile", None, "rep", None),
        check_vma=False,
    )
```

```python
import functools
import math

import jax
import jax.numpy as jnp
from jax import lax
from jax.experimental import pallas as pl
from jax.experimental.pallas import tpu as pltpu
from jax.sharding import PartitionSpec as P


def from_partner(array, axis, distance):
    return lax.ppermute(array, axis, [(i, i ^ 1 << distance) for i in range(lax.axis_size(axis))])


def batched(left_side, right_side, pattern):
    return jnp.einsum(pattern, left_side, right_side, preferred_element_type=jnp.float32)


def phase_tables(row_values, col_values, modulus):
    phase_index = row_values[:, None] * col_values[None, :] % modulus
    phase_angle = phase_index.astype(jnp.float32) * (2.0 * math.pi / modulus)
    cos_full = jnp.cos(phase_angle)
    sin_full = jnp.sin(phase_angle)
    cos_high = cos_full.astype(jnp.bfloat16)
    sin_high = sin_full.astype(jnp.bfloat16)
    cos_low = (cos_full - cos_high.astype(jnp.float32)).astype(jnp.bfloat16)
    sin_low = (sin_full - sin_high.astype(jnp.float32)).astype(jnp.bfloat16)
    return ((cos_high, cos_low), (sin_high, sin_low))


def split_dot(table_pair, values):
    return jnp.dot(table_pair[0], values, preferred_element_type=jnp.float32) + jnp.dot(
        table_pair[1], values, preferred_element_type=jnp.float32
    )


def rotate(cos_table, sin_table, value_re, value_im, direction):
    part_re = split_dot(cos_table, value_re) - direction * split_dot(sin_table, value_im)
    part_im = split_dot(cos_table, value_im) + direction * split_dot(sin_table, value_re)
    return (part_re, part_im)


def body(retarded, self_energy, energy_of):
    component = lax.axis_index("comp")
    momentum = component // 2
    greater = component % 2
    tile_count = lax.axis_size("tile")
    rep_count = lax.axis_size("rep")
    green_matrix = lax.dynamic_index_in_dim(retarded, momentum, 0, keepdims=False)
    sigma_matrix = self_energy[0]
    green_re, green_im = (green_matrix[:, 0], green_matrix[:, 1])
    sigma_re, sigma_im = (sigma_matrix[:, 0], sigma_matrix[:, 1])
    left_re = (
        batched(green_re, sigma_re, "eik,ekj->eij") - batched(green_im, sigma_im, "eik,ekj->eij")
    ).astype(jnp.bfloat16)
    left_im = (
        batched(green_re, sigma_im, "eik,ekj->eij") + batched(green_im, sigma_re, "eik,ekj->eij")
    ).astype(jnp.bfloat16)
    out_re = batched(left_re, green_re, "eik,ejk->eij") + batched(left_im, green_im, "eik,ejk->eij")
    out_im = batched(left_im, green_re, "eik,ejk->eij") - batched(left_re, green_im, "eik,ejk->eij")
    stacked = jnp.stack([out_re, out_im]).astype(jnp.bfloat16)
    stacked = jnp.where(greater == 1, jnp.swapaxes(stacked, 2, 3), stacked)
    energy_dev = stacked.shape[1]
    block_order = stacked.shape[2]
    elem_count = block_order * block_order // (tile_count * rep_count)
    slot_count = energy_of.shape[0]
    blocks = stacked.reshape(2, energy_dev, rep_count, tile_count, elem_count)
    first_pass = lax.all_to_all(blocks, "rep", split_axis=2, concat_axis=1, tiled=True)
    gathered = lax.all_to_all(first_pass, "tile", split_axis=3, concat_axis=1, tiled=True)
    signal = gathered.reshape(2, slot_count, elem_count)
    freq_count = 2 * slot_count
    frequency = lax.iota(jnp.int32, freq_count)
    fwd_cos, fwd_sin = phase_tables(frequency, energy_of, freq_count)
    own_re, own_im = rotate(fwd_cos, fwd_sin, signal[0], signal[1], -1.0)
    partner = from_partner(signal, "comp", 0)
    other_re, other_im = rotate(fwd_cos, fwd_sin, partner[0], partner[1], 1.0)
    cross_re = (own_re * other_re - own_im * other_im).astype(jnp.bfloat16)
    cross_im = (own_re * other_im + own_im * other_re).astype(jnp.bfloat16)
    lag_index = lax.iota(jnp.int32, slot_count)
    inv_cos, inv_sin = phase_tables(lag_index, frequency, freq_count)
    back_re, back_im = rotate(inv_cos, inv_sin, cross_re, cross_im, 1.0)
    norm_factor = 1.0 / (freq_count * math.sqrt(slot_count))
    polar_parts = jnp.stack([back_im * norm_factor, -back_re * norm_factor], axis=1)
    regrouped = lax.all_to_all(
        polar_parts[:, :, None, :], "tile", split_axis=0, concat_axis=2, tiled=True
    )
    lag_count = slot_count // tile_count
    return regrouped.reshape(lag_count, 2, block_order // rep_count, block_order)[None]


LANES = 128
ROWS = 8


def matmul(left_side, right_side, contract):
    return lax.dot_general(
        left_side, right_side, (((1,), (contract,)), ((), ())), preferred_element_type=jnp.float32
    )


def rotated(values):
    return pltpu.roll(values, LANES // 2, axis=1)


def polar_kernel(
    axis_sizes,
    retarded,
    self_energy,
    energy_of,
    polar,
    green_in,
    sigma_in,
    energies,
    outgoing,
    ordered,
    lagged,
    arrived,
    load_sem,
    first_send,
    first_recv,
    second_send,
    second_recv,
    *gathered,
):
    tile_count, rep_count = axis_sizes
    component = lax.axis_index("comp")
    tile = lax.axis_index("tile")
    rep = lax.axis_index("rep")
    momentum = component // 2
    greater = component % 2
    energy_dev, block_order = green_in.shape[0], green_in.shape[2]
    slot_count = energies.shape[0]
    unit_count = arrived.shape[0]
    lag_count = arrived.shape[1]
    row_count = block_order // rep_count
    low_units = row_count // ROWS
    owner_count = 2 * tile_count
    peer_count = owner_count * rep_count
    base_units = unit_count // owner_count
    has_spare = unit_count % owner_count != 0

    owner = tile * 2 + greater

    def first_unit(which):
        return which * unit_count // owner_count

    def takes_spare(which):
        return first_unit(which + 1) - first_unit(which) > base_units

    tiles = [(tile + step) % tile_count for step in range(tile_count)]
    reps = [(rep + step) % rep_count for step in range(rep_count)]
    parts = [greater, 1 - greater]
    owners = [[tiles[i] * 2 + parts[j] for j in range(2)] for i in range(tile_count)]
    firsts = [[first_unit(owners[i][j]) for j in range(2)] for i in range(tile_count)]
    spares_at = [[takes_spare(owners[i][j]) for j in range(2)] for i in range(tile_count)]
    far_first = sorted(range(tile_count), key=lambda step: -min(step, tile_count - step))
    near_owners = [(i, j) for j in range(2) for i in far_first if (i, j) != (0, 0)]
    peers = [
        (i, j, k)
        for k in reversed(range(rep_count))
        for j in range(2)
        for i in far_first
        if (i, j, k) != (0, 0, 0)
    ]

    def device_of(i, j, k):
        return (momentum * 2 + parts[j], tiles[i], reps[k])

    loads = []
    for energy in range(energy_dev):
        loads.append(
            (
                pltpu.make_async_copy(
                    retarded.at[momentum, energy], green_in.at[energy], load_sem.at[2 * energy]
                ),
                pltpu.make_async_copy(
                    self_energy.at[0, energy], sigma_in.at[energy], load_sem.at[2 * energy + 1]
                ),
            )
        )
        for load in loads[-1]:
            load.start()
    energy_load = pltpu.make_async_copy(energy_of, energies, load_sem.at[2 * energy_dev])
    energy_load.start()

    barrier = pltpu.get_barrier_semaphore()
    for peer in peers:
        pl.semaphore_signal(
            barrier,
            inc=1,
            device_id=device_of(*peer),
            device_id_type=pl.DeviceIdType.MESH,
        )

    def finish(energy, left, right, sign):
        low, high = slice(0, LANES), slice(LANES, block_order)
        right_re, right_im = right
        with_re = jnp.concatenate(
            [right_re[low], -sign * right_im[low], right_re[high], -sign * right_im[high]]
        )
        with_im = jnp.concatenate(
            [right_im[low], sign * right_re[low], right_im[high], sign * right_re[high]]
        )
        result = matmul(left[0], with_re, 1) + matmul(left[1], with_im, 1)
        is_low = lax.broadcasted_iota(jnp.int32, (row_count // 2, LANES), 1) < LANES // 2
        for part in range(rep_count):
            rows = slice(part * row_count, (part + 1) * row_count)
            mixed = result[rows, 2 * LANES :]
            upper, lower = mixed[: row_count // 2], mixed[row_count // 2 :]
            high_re = jnp.where(is_low, upper, rotated(lower))
            high_im = jnp.where(is_low, rotated(upper), lower)
            pieces_re = jnp.concatenate([result[rows, :LANES], high_re])
            pieces_im = jnp.concatenate([result[rows, LANES : 2 * LANES], high_im])
            packed = jnp.concatenate(
                [
                    pieces_re.reshape(unit_count, ROWS, LANES),
                    pieces_im.reshape(unit_count, ROWS, LANES),
                ],
                axis=1,
            )
            outgoing[part, :, energy] = packed.astype(jnp.bfloat16)

    for energy in range(energy_dev):
        for load in loads[energy]:
            load.wait()
        green_re, green_im = green_in[energy, 0], green_in[energy, 1]
        sigma_re, sigma_im = sigma_in[energy, 0], sigma_in[energy, 1]
        left_re = (matmul(green_re, sigma_re, 0) - matmul(green_im, sigma_im, 0)).astype(jnp.bfloat16)
        left_im = (matmul(green_re, sigma_im, 0) + matmul(green_im, sigma_re, 0)).astype(jnp.bfloat16)

        @pl.when(greater == 0)
        def _():
            finish(energy, (left_re, left_im), (green_re, green_im), 1)

        @pl.when(greater == 1)
        def _():
            finish(energy, (green_re, green_im), (left_re, left_im), -1)

    pl.semaphore_wait(barrier, peer_count - 1)

    my_slot = greater * slot_count + (tile * rep_count + rep) * energy_dev

    def send_first(unit, spare):
        for i, j, k in peers:
            copy = pltpu.make_async_remote_copy(
                src_ref=outgoing.at[reps[k], firsts[i][j] + unit],
                dst_ref=gathered[unit].at[pl.ds(my_slot, energy_dev)],
                send_sem=first_send.at[unit],
                recv_sem=first_recv.at[unit],
                device_id=device_of(i, j, k),
                device_id_type=pl.DeviceIdType.MESH,
            )
            if spare:
                pl.when(spares_at[i][j])(copy.start)
            else:
                copy.start()

    def keep_own(unit):
        gathered[unit][pl.ds(my_slot, energy_dev)] = outgoing[rep, firsts[0][0] + unit]

    def wait_for(buffer, sem):
        pltpu.make_async_copy(buffer, buffer, sem).wait()

    for unit in range(base_units):
        send_first(unit, False)
    if has_spare:
        send_first(base_units, True)
    for unit in range(base_units):
        keep_own(unit)
    if has_spare:
        pl.when(spares_at[0][0])(functools.partial(keep_own, base_units))

    energy_load.wait()
    slots = []
    for energy in range(slot_count):
        slot = 0
        for candidate in range(slot_count):
            slot = jnp.where(energies[candidate] == energy, candidate, slot)
        slots.append(slot)

    norm_factor = 1.0 / math.sqrt(slot_count)

    def correlate(unit):
        wait_for(
            gathered[unit].at[pl.ds(0, (peer_count - 1) * energy_dev)], first_recv.at[unit]
        )
        for part in range(2):
            for energy in range(slot_count):
                ordered[part, energy] = gathered[unit][part * slot_count + slots[energy]].astype(
                    jnp.float32
                )
        for lag in range(slot_count):
            for part in range(2):
                own_re = ordered[part, lag:, :ROWS]
                own_im = ordered[part, lag:, ROWS:]
                other_re = ordered[1 - part, : slot_count - lag, :ROWS]
                other_im = ordered[1 - part, : slot_count - lag, ROWS:]
                sum_re = jnp.sum(own_re * other_re - own_im * other_im, axis=0)
                sum_im = jnp.sum(own_re * other_im + own_im * other_re, axis=0)
                lagged[unit, part, lag] = jnp.concatenate(
                    [sum_im * norm_factor, sum_re * -norm_factor]
                ).astype(jnp.bfloat16)
        my_unit = firsts[0][0] + unit
        for i, j in near_owners:
            pltpu.make_async_remote_copy(
                src_ref=lagged.at[unit, parts[j], pl.ds(tiles[i] * lag_count, lag_count)],
                dst_ref=arrived.at[my_unit],
                send_sem=second_send.at[unit],
                recv_sem=second_recv.at[unit],
                device_id=device_of(i, j, 0),
                device_id_type=pl.DeviceIdType.MESH,
            ).start()
        arrived[my_unit] = lagged[unit, greater, pl.ds(tile * lag_count, lag_count)]

    for unit in range(base_units):
        correlate(unit)
    if has_spare:
        pl.when(spares_at[0][0])(functools.partial(correlate, base_units))

    for unit in range(base_units):
        wait_for(
            gathered[unit].at[pl.ds(0, (peer_count - 1) * energy_dev)], first_send.at[unit]
        )
        wait_for(arrived.at[pl.ds(0, owner_count - 1)], second_send.at[unit])
        wait_for(arrived.at[pl.ds(0, owner_count - 1)], second_recv.at[unit])
    if has_spare:
        spare_units = unit_count % owner_count
        spares = spare_units * rep_count

        @pl.when(spares_at[0][0])
        def _():
            if spares > 1:
                wait_for(
                    gathered[base_units].at[pl.ds(0, (spares - 1) * energy_dev)],
                    first_send.at[base_units],
                )
            wait_for(arrived.at[pl.ds(0, owner_count - 1)], second_send.at[base_units])
            if spare_units > 1:
                wait_for(arrived.at[pl.ds(0, spare_units - 1)], second_recv.at[base_units])

        @pl.when(jnp.logical_not(spares_at[0][0]))
        def _():
            wait_for(
                gathered[base_units].at[pl.ds(0, spares * energy_dev)], first_send.at[base_units]
            )
            wait_for(arrived.at[pl.ds(0, spare_units)], second_recv.at[base_units])

    for lag in range(lag_count):
        for unit in range(unit_count):
            values = arrived[unit, lag].astype(jnp.float32)
            for part in range(2):
                block = values[part * ROWS : (part + 1) * ROWS]
                if unit < low_units:
                    polar[0, lag, part, unit * ROWS : (unit + 1) * ROWS, :LANES] = block
                else:
                    row = (unit - low_units) * ROWS
                    row_low = row + row_count // 2
                    polar[0, lag, part, row : row + ROWS, LANES:] = block[:, : LANES // 2]
                    polar[0, lag, part, row_low : row_low + ROWS, LANES:] = rotated(block)[
                        :, : LANES // 2
                    ]


def fits(sizes, energy_dev, block_order):
    comp_count, tile_count, rep_count = sizes
    return (
        comp_count % 2 == 0
        and block_order == LANES + LANES // 2
        and block_order % (2 * ROWS * 2 * rep_count) == 0
        and block_order * 3 // (4 * ROWS * rep_count) >= 2 * tile_count
        and tile_count * rep_count * energy_dev <= 4 * ROWS
    )


def fused(sizes, retarded, self_energy, energy_of):
    _, tile_count, rep_count = sizes
    energy_dev, block_order = retarded.shape[1], retarded.shape[-1]
    slot_count = energy_of.shape[0]
    lag_count = slot_count // tile_count
    row_count = block_order // rep_count
    unit_count = row_count * block_order // (ROWS * LANES)
    units_held = -(-unit_count // (2 * tile_count))
    packed = (2 * ROWS, LANES)
    return pl.pallas_call(
        functools.partial(polar_kernel, (tile_count, rep_count)),
        out_shape=jax.ShapeDtypeStruct((1, lag_count, 2, row_count, block_order), jnp.float32),
        in_specs=[pl.BlockSpec(memory_space=pl.ANY)] * 3,
        out_specs=pl.BlockSpec(memory_space=pltpu.VMEM),
        scratch_shapes=[
            pltpu.VMEM(retarded.shape[1:], jnp.bfloat16),
            pltpu.VMEM(self_energy.shape[1:], jnp.bfloat16),
            pltpu.SMEM((slot_count,), jnp.int32),
            pltpu.VMEM((rep_count, unit_count, energy_dev) + packed, jnp.bfloat16),
            pltpu.VMEM((2, slot_count) + packed, jnp.float32),
            pltpu.VMEM((units_held, 2, slot_count) + packed, jnp.bfloat16),
            pltpu.VMEM((unit_count, lag_count) + packed, jnp.bfloat16),
            pltpu.SemaphoreType.DMA((2 * energy_dev + 1,)),
            pltpu.SemaphoreType.DMA((units_held,)),
            pltpu.SemaphoreType.DMA((units_held,)),
            pltpu.SemaphoreType.DMA((units_held,)),
            pltpu.SemaphoreType.DMA((units_held,)),
        ]
        + [pltpu.VMEM((2 * slot_count,) + packed, jnp.bfloat16)] * units_held,
        compiler_params=pltpu.CompilerParams(
            collective_id=0, has_side_effects=True, vmem_limit_bytes=62 * 2**20
        ),
    )(retarded, self_energy, energy_of)


def solution(mesh):
    placed = (
        P(None, ("tile", "rep"), None, None, None),
        P("comp", ("tile", "rep"), None, None, None),
        P(),
    )
    sizes = tuple(mesh.shape[name] for name in ("comp", "tile", "rep"))

    def device_body(retarded, self_energy, energy_of):
        if fits(sizes, retarded.shape[1], retarded.shape[-1]):
            return fused(sizes, retarded, self_energy, energy_of)
        return body(retarded, self_energy, energy_of)

    return jax.shard_map(
        device_body,
        mesh=mesh,
        in_specs=placed,
        out_specs=P("comp", "tile", None, "rep", None),
        check_vma=False,
    )
```

```python
import functools
import math

import jax
import jax.numpy as jnp
from jax import lax
from jax.experimental import pallas as pl
from jax.experimental.pallas import tpu as pltpu
from jax.sharding import PartitionSpec as P


def from_partner(array, axis, distance):
    return lax.ppermute(array, axis, [(i, i ^ 1 << distance) for i in range(lax.axis_size(axis))])


def batched(left_side, right_side, pattern):
    return jnp.einsum(pattern, left_side, right_side, preferred_element_type=jnp.float32)


def phase_tables(row_values, col_values, modulus):
    phase_index = row_values[:, None] * col_values[None, :] % modulus
    phase_angle = phase_index.astype(jnp.float32) * (2.0 * math.pi / modulus)
    cos_full = jnp.cos(phase_angle)
    sin_full = jnp.sin(phase_angle)
    cos_high = cos_full.astype(jnp.bfloat16)
    sin_high = sin_full.astype(jnp.bfloat16)
    cos_low = (cos_full - cos_high.astype(jnp.float32)).astype(jnp.bfloat16)
    sin_low = (sin_full - sin_high.astype(jnp.float32)).astype(jnp.bfloat16)
    return ((cos_high, cos_low), (sin_high, sin_low))


def split_dot(table_pair, values):
    return jnp.dot(table_pair[0], values, preferred_element_type=jnp.float32) + jnp.dot(
        table_pair[1], values, preferred_element_type=jnp.float32
    )


def rotate(cos_table, sin_table, value_re, value_im, direction):
    part_re = split_dot(cos_table, value_re) - direction * split_dot(sin_table, value_im)
    part_im = split_dot(cos_table, value_im) + direction * split_dot(sin_table, value_re)
    return (part_re, part_im)


def body(retarded, self_energy, energy_of):
    component = lax.axis_index("comp")
    momentum = component // 2
    greater = component % 2
    tile_count = lax.axis_size("tile")
    rep_count = lax.axis_size("rep")
    green_matrix = lax.dynamic_index_in_dim(retarded, momentum, 0, keepdims=False)
    sigma_matrix = self_energy[0]
    green_re, green_im = (green_matrix[:, 0], green_matrix[:, 1])
    sigma_re, sigma_im = (sigma_matrix[:, 0], sigma_matrix[:, 1])
    left_re = (
        batched(green_re, sigma_re, "eik,ekj->eij") - batched(green_im, sigma_im, "eik,ekj->eij")
    ).astype(jnp.bfloat16)
    left_im = (
        batched(green_re, sigma_im, "eik,ekj->eij") + batched(green_im, sigma_re, "eik,ekj->eij")
    ).astype(jnp.bfloat16)
    out_re = batched(left_re, green_re, "eik,ejk->eij") + batched(left_im, green_im, "eik,ejk->eij")
    out_im = batched(left_im, green_re, "eik,ejk->eij") - batched(left_re, green_im, "eik,ejk->eij")
    stacked = jnp.stack([out_re, out_im]).astype(jnp.bfloat16)
    stacked = jnp.where(greater == 1, jnp.swapaxes(stacked, 2, 3), stacked)
    energy_dev = stacked.shape[1]
    block_order = stacked.shape[2]
    elem_count = block_order * block_order // (tile_count * rep_count)
    slot_count = energy_of.shape[0]
    blocks = stacked.reshape(2, energy_dev, rep_count, tile_count, elem_count)
    first_pass = lax.all_to_all(blocks, "rep", split_axis=2, concat_axis=1, tiled=True)
    gathered = lax.all_to_all(first_pass, "tile", split_axis=3, concat_axis=1, tiled=True)
    signal = gathered.reshape(2, slot_count, elem_count)
    freq_count = 2 * slot_count
    frequency = lax.iota(jnp.int32, freq_count)
    fwd_cos, fwd_sin = phase_tables(frequency, energy_of, freq_count)
    own_re, own_im = rotate(fwd_cos, fwd_sin, signal[0], signal[1], -1.0)
    partner = from_partner(signal, "comp", 0)
    other_re, other_im = rotate(fwd_cos, fwd_sin, partner[0], partner[1], 1.0)
    cross_re = (own_re * other_re - own_im * other_im).astype(jnp.bfloat16)
    cross_im = (own_re * other_im + own_im * other_re).astype(jnp.bfloat16)
    lag_index = lax.iota(jnp.int32, slot_count)
    inv_cos, inv_sin = phase_tables(lag_index, frequency, freq_count)
    back_re, back_im = rotate(inv_cos, inv_sin, cross_re, cross_im, 1.0)
    norm_factor = 1.0 / (freq_count * math.sqrt(slot_count))
    polar_parts = jnp.stack([back_im * norm_factor, -back_re * norm_factor], axis=1)
    regrouped = lax.all_to_all(
        polar_parts[:, :, None, :], "tile", split_axis=0, concat_axis=2, tiled=True
    )
    lag_count = slot_count // tile_count
    return regrouped.reshape(lag_count, 2, block_order // rep_count, block_order)[None]


LANES = 128
ROWS = 8
KERNEL_BYTES = 62 * 2**20


def matmul(left_side, right_side, contract):
    return lax.dot_general(
        left_side, right_side, (((1,), (contract,)), ((), ())), preferred_element_type=jnp.float32
    )


def rotated(values):
    return pltpu.roll(values, LANES // 2, axis=1)


def polar_kernel(
    axis_sizes,
    retarded,
    self_energy,
    energy_of,
    arrived,
    green_in,
    sigma_in,
    energies,
    outgoing,
    ordered,
    lagged,
    load_sem,
    first_send,
    first_recv,
    second_send,
    second_recv,
    keep_sem,
    *gathered,
):
    tile_count, rep_count = axis_sizes
    component = lax.axis_index("comp")
    tile = lax.axis_index("tile")
    rep = lax.axis_index("rep")
    momentum = component // 2
    greater = component % 2
    energy_dev, block_order = green_in.shape[0], green_in.shape[2]
    slot_count = energies.shape[0]
    unit_count = arrived.shape[0]
    lag_count = arrived.shape[1]
    row_count = block_order // rep_count
    low_units = row_count // ROWS
    owner_count = 2 * tile_count
    peer_count = owner_count * rep_count
    base_units = unit_count // owner_count
    has_spare = unit_count % owner_count != 0

    owner = tile * 2 + greater

    def first_unit(which):
        return which * unit_count // owner_count

    def takes_spare(which):
        return first_unit(which + 1) - first_unit(which) > base_units

    tiles = [(tile + step) % tile_count for step in range(tile_count)]
    reps = [(rep + step) % rep_count for step in range(rep_count)]
    parts = [greater, 1 - greater]
    owners = [[tiles[i] * 2 + parts[j] for j in range(2)] for i in range(tile_count)]
    firsts = [[first_unit(owners[i][j]) for j in range(2)] for i in range(tile_count)]
    spares_at = [[takes_spare(owners[i][j]) for j in range(2)] for i in range(tile_count)]
    far_first = sorted(range(tile_count), key=lambda step: -min(step, tile_count - step))
    near_owners = [(i, j) for j in range(2) for i in far_first if (i, j) != (0, 0)]
    peers = [
        (i, j, k)
        for k in reversed(range(rep_count))
        for j in range(2)
        for i in far_first
        if (i, j, k) != (0, 0, 0)
    ]

    def device_of(i, j, k):
        return (momentum * 2 + parts[j], tiles[i], reps[k])

    loads = []
    for energy in range(energy_dev):
        loads.append(
            (
                pltpu.make_async_copy(
                    retarded.at[momentum, energy], green_in.at[energy], load_sem.at[2 * energy]
                ),
                pltpu.make_async_copy(
                    self_energy.at[0, energy], sigma_in.at[energy], load_sem.at[2 * energy + 1]
                ),
            )
        )
        for load in loads[-1]:
            load.start()
    energy_load = pltpu.make_async_copy(energy_of, energies, load_sem.at[2 * energy_dev])
    energy_load.start()

    barrier = pltpu.get_barrier_semaphore()
    for peer in peers:
        pl.semaphore_signal(
            barrier,
            inc=1,
            device_id=device_of(*peer),
            device_id_type=pl.DeviceIdType.MESH,
        )

    def finish(energy, left, right, sign):
        low, high = slice(0, LANES), slice(LANES, block_order)
        right_re, right_im = right
        with_re = jnp.concatenate(
            [right_re[low], -sign * right_im[low], right_re[high], -sign * right_im[high]]
        )
        with_im = jnp.concatenate(
            [right_im[low], sign * right_re[low], right_im[high], sign * right_re[high]]
        )
        result = matmul(left[0], with_re, 1) + matmul(left[1], with_im, 1)
        is_low = lax.broadcasted_iota(jnp.int32, (row_count // 2, LANES), 1) < LANES // 2
        for part in range(rep_count):
            rows = slice(part * row_count, (part + 1) * row_count)
            mixed = result[rows, 2 * LANES :]
            upper, lower = mixed[: row_count // 2], mixed[row_count // 2 :]
            high_re = jnp.where(is_low, upper, rotated(lower))
            high_im = jnp.where(is_low, rotated(upper), lower)
            pieces_re = jnp.concatenate([result[rows, :LANES], high_re])
            pieces_im = jnp.concatenate([result[rows, LANES : 2 * LANES], high_im])
            packed = jnp.concatenate(
                [
                    pieces_re.reshape(unit_count, ROWS, LANES),
                    pieces_im.reshape(unit_count, ROWS, LANES),
                ],
                axis=1,
            )
            outgoing[part, :, energy] = packed.astype(jnp.bfloat16)

    for energy in range(energy_dev):
        for load in loads[energy]:
            load.wait()
        green_re, green_im = green_in[energy, 0], green_in[energy, 1]
        sigma_re, sigma_im = sigma_in[energy, 0], sigma_in[energy, 1]
        left_re = (matmul(green_re, sigma_re, 0) - matmul(green_im, sigma_im, 0)).astype(jnp.bfloat16)
        left_im = (matmul(green_re, sigma_im, 0) + matmul(green_im, sigma_re, 0)).astype(jnp.bfloat16)

        @pl.when(greater == 0)
        def _():
            finish(energy, (left_re, left_im), (green_re, green_im), 1)

        @pl.when(greater == 1)
        def _():
            finish(energy, (green_re, green_im), (left_re, left_im), -1)

    pl.semaphore_wait(barrier, peer_count - 1)

    my_slot = greater * slot_count + (tile * rep_count + rep) * energy_dev

    def send_first(unit, spare):
        for i, j, k in peers:
            copy = pltpu.make_async_remote_copy(
                src_ref=outgoing.at[reps[k], firsts[i][j] + unit],
                dst_ref=gathered[unit].at[pl.ds(my_slot, energy_dev)],
                send_sem=first_send.at[unit],
                recv_sem=first_recv.at[unit],
                device_id=device_of(i, j, k),
                device_id_type=pl.DeviceIdType.MESH,
            )
            if spare:
                pl.when(spares_at[i][j])(copy.start)
            else:
                copy.start()

    def keep_own(unit):
        gathered[unit][pl.ds(my_slot, energy_dev)] = outgoing[rep, firsts[0][0] + unit]

    def wait_for(buffer, sem):
        pltpu.make_async_copy(buffer, buffer, sem).wait()

    for unit in range(base_units):
        send_first(unit, False)
    if has_spare:
        send_first(base_units, True)
    for unit in range(base_units):
        keep_own(unit)
    if has_spare:
        pl.when(spares_at[0][0])(functools.partial(keep_own, base_units))

    energy_load.wait()
    slots = []
    for energy in range(slot_count):
        slot = 0
        for candidate in range(slot_count):
            slot = jnp.where(energies[candidate] == energy, candidate, slot)
        slots.append(slot)

    norm_factor = 1.0 / math.sqrt(slot_count)

    def keep_lags(unit):
        return pltpu.make_async_copy(
            lagged.at[unit, greater, pl.ds(tile * lag_count, lag_count)],
            arrived.at[firsts[0][0] + unit],
            keep_sem.at[unit],
        )

    def correlate(unit):
        wait_for(
            gathered[unit].at[pl.ds(0, (peer_count - 1) * energy_dev)], first_recv.at[unit]
        )
        for part in range(2):
            for energy in range(slot_count):
                ordered[part, energy] = gathered[unit][part * slot_count + slots[energy]].astype(
                    jnp.float32
                )
        for lag in range(slot_count):
            for part in range(2):
                own_re = ordered[part, lag:, :ROWS]
                own_im = ordered[part, lag:, ROWS:]
                other_re = ordered[1 - part, : slot_count - lag, :ROWS]
                other_im = ordered[1 - part, : slot_count - lag, ROWS:]
                sum_re = jnp.sum(own_re * other_re - own_im * other_im, axis=0)
                sum_im = jnp.sum(own_re * other_im + own_im * other_re, axis=0)
                lagged[unit, part, lag] = jnp.concatenate(
                    [sum_im * norm_factor, sum_re * -norm_factor]
                ).astype(jnp.bfloat16)
        my_unit = firsts[0][0] + unit
        for i, j in near_owners:
            pltpu.make_async_remote_copy(
                src_ref=lagged.at[unit, parts[j], pl.ds(tiles[i] * lag_count, lag_count)],
                dst_ref=arrived.at[my_unit],
                send_sem=second_send.at[unit],
                recv_sem=second_recv.at[unit],
                device_id=device_of(i, j, 0),
                device_id_type=pl.DeviceIdType.MESH,
            ).start()
        keep_lags(unit).start()

    for unit in range(base_units):
        correlate(unit)
    if has_spare:
        pl.when(spares_at[0][0])(functools.partial(correlate, base_units))

    for unit in range(base_units):
        wait_for(
            gathered[unit].at[pl.ds(0, (peer_count - 1) * energy_dev)], first_send.at[unit]
        )
        wait_for(arrived.at[pl.ds(0, owner_count - 1)], second_send.at[unit])
        wait_for(arrived.at[pl.ds(0, owner_count - 1)], second_recv.at[unit])
        keep_lags(unit).wait()
    if has_spare:
        spare_units = unit_count % owner_count
        spares = spare_units * rep_count

        @pl.when(spares_at[0][0])
        def _():
            if spares > 1:
                wait_for(
                    gathered[base_units].at[pl.ds(0, (spares - 1) * energy_dev)],
                    first_send.at[base_units],
                )
            wait_for(arrived.at[pl.ds(0, owner_count - 1)], second_send.at[base_units])
            keep_lags(base_units).wait()
            if spare_units > 1:
                wait_for(arrived.at[pl.ds(0, spare_units - 1)], second_recv.at[base_units])

        @pl.when(jnp.logical_not(spares_at[0][0]))
        def _():
            wait_for(
                gathered[base_units].at[pl.ds(0, spares * energy_dev)], first_send.at[base_units]
            )
            wait_for(arrived.at[pl.ds(0, spare_units)], second_recv.at[base_units])


def unpack_kernel(arrived, polar, packed, unpacked, load_sem, store_sem):
    unit_count, lag_count = arrived.shape[:2]
    row_count = polar.shape[3]
    low_units = row_count // ROWS
    loads = [
        pltpu.make_async_copy(arrived.at[:, lag], packed.at[lag], load_sem.at[lag])
        for lag in range(lag_count)
    ]
    stores = [
        pltpu.make_async_copy(unpacked.at[lag], polar.at[0, lag], store_sem.at[lag])
        for lag in range(lag_count)
    ]
    for load in loads:
        load.start()
    for lag in range(lag_count):
        loads[lag].wait()
        for unit in range(unit_count):
            values = packed[lag, unit].astype(jnp.float32)
            for part in range(2):
                block = values[part * ROWS : (part + 1) * ROWS]
                if unit < low_units:
                    unpacked[lag, part, unit * ROWS : (unit + 1) * ROWS, :LANES] = block
                else:
                    row = (unit - low_units) * ROWS
                    row_low = row + row_count // 2
                    unpacked[lag, part, row : row + ROWS, LANES:] = block[:, : LANES // 2]
                    unpacked[lag, part, row_low : row_low + ROWS, LANES:] = rotated(block)[
                        :, : LANES // 2
                    ]
        stores[lag].start()
    for store in stores:
        store.wait()


def fits(sizes, energy_dev, block_order):
    comp_count, tile_count, rep_count = sizes
    return (
        comp_count % 2 == 0
        and block_order == LANES + LANES // 2
        and block_order % (2 * ROWS * 2 * rep_count) == 0
        and block_order * 3 // (4 * ROWS * rep_count) >= 2 * tile_count
        and tile_count * rep_count * energy_dev <= 4 * ROWS
    )


def fused(sizes, retarded, self_energy, energy_of):
    _, tile_count, rep_count = sizes
    energy_dev, block_order = retarded.shape[1], retarded.shape[-1]
    slot_count = energy_of.shape[0]
    lag_count = slot_count // tile_count
    row_count = block_order // rep_count
    unit_count = row_count * block_order // (ROWS * LANES)
    units_held = -(-unit_count // (2 * tile_count))
    packed = (2 * ROWS, LANES)
    arrived = pl.pallas_call(
        functools.partial(polar_kernel, (tile_count, rep_count)),
        out_shape=jax.ShapeDtypeStruct((unit_count, lag_count) + packed, jnp.bfloat16),
        in_specs=[pl.BlockSpec(memory_space=pl.ANY)] * 3,
        out_specs=pl.BlockSpec(memory_space=pl.ANY),
        scratch_shapes=[
            pltpu.VMEM(retarded.shape[1:], jnp.bfloat16),
            pltpu.VMEM(self_energy.shape[1:], jnp.bfloat16),
            pltpu.SMEM((slot_count,), jnp.int32),
            pltpu.VMEM((rep_count, unit_count, energy_dev) + packed, jnp.bfloat16),
            pltpu.VMEM((2, slot_count) + packed, jnp.float32),
            pltpu.VMEM((units_held, 2, slot_count) + packed, jnp.bfloat16),
            pltpu.SemaphoreType.DMA((2 * energy_dev + 1,)),
            pltpu.SemaphoreType.DMA((units_held,)),
            pltpu.SemaphoreType.DMA((units_held,)),
            pltpu.SemaphoreType.DMA((units_held,)),
            pltpu.SemaphoreType.DMA((units_held,)),
            pltpu.SemaphoreType.DMA((units_held,)),
        ]
        + [pltpu.VMEM((2 * slot_count,) + packed, jnp.bfloat16)] * units_held,
        compiler_params=pltpu.CompilerParams(
            collective_id=0, has_side_effects=True, vmem_limit_bytes=KERNEL_BYTES
        ),
    )(retarded, self_energy, energy_of)
    return pl.pallas_call(
        unpack_kernel,
        out_shape=jax.ShapeDtypeStruct((1, lag_count, 2, row_count, block_order), jnp.float32),
        in_specs=[pl.BlockSpec(memory_space=pl.ANY)],
        out_specs=pl.BlockSpec(memory_space=pl.ANY),
        scratch_shapes=[
            pltpu.VMEM((lag_count, unit_count) + packed, jnp.bfloat16),
            pltpu.VMEM((lag_count, 2, row_count, block_order), jnp.float32),
            pltpu.SemaphoreType.DMA((lag_count,)),
            pltpu.SemaphoreType.DMA((lag_count,)),
        ],
        compiler_params=pltpu.CompilerParams(vmem_limit_bytes=KERNEL_BYTES),
    )(arrived)


def solution(mesh):
    placed = (
        P(None, ("tile", "rep"), None, None, None),
        P("comp", ("tile", "rep"), None, None, None),
        P(),
    )
    sizes = tuple(mesh.shape[name] for name in ("comp", "tile", "rep"))

    def device_body(retarded, self_energy, energy_of):
        if fits(sizes, retarded.shape[1], retarded.shape[-1]):
            return fused(sizes, retarded, self_energy, energy_of)
        return body(retarded, self_energy, energy_of)

    return jax.shard_map(
        device_body,
        mesh=mesh,
        in_specs=placed,
        out_specs=P("comp", "tile", None, "rep", None),
        check_vma=False,
    )
```

```python
import functools
import math

import jax
import jax.numpy as jnp
from jax import lax
from jax.experimental import pallas as pl
from jax.experimental.pallas import tpu as pltpu
from jax.sharding import PartitionSpec as P


def from_partner(array, axis, distance):
    return lax.ppermute(array, axis, [(i, i ^ 1 << distance) for i in range(lax.axis_size(axis))])


def batched(left_side, right_side, pattern):
    return jnp.einsum(pattern, left_side, right_side, preferred_element_type=jnp.float32)


def phase_tables(row_values, col_values, modulus):
    phase_index = row_values[:, None] * col_values[None, :] % modulus
    phase_angle = phase_index.astype(jnp.float32) * (2.0 * math.pi / modulus)
    cos_full = jnp.cos(phase_angle)
    sin_full = jnp.sin(phase_angle)
    cos_high = cos_full.astype(jnp.bfloat16)
    sin_high = sin_full.astype(jnp.bfloat16)
    cos_low = (cos_full - cos_high.astype(jnp.float32)).astype(jnp.bfloat16)
    sin_low = (sin_full - sin_high.astype(jnp.float32)).astype(jnp.bfloat16)
    return ((cos_high, cos_low), (sin_high, sin_low))


def split_dot(table_pair, values):
    return jnp.dot(table_pair[0], values, preferred_element_type=jnp.float32) + jnp.dot(
        table_pair[1], values, preferred_element_type=jnp.float32
    )


def rotate(cos_table, sin_table, value_re, value_im, direction):
    part_re = split_dot(cos_table, value_re) - direction * split_dot(sin_table, value_im)
    part_im = split_dot(cos_table, value_im) + direction * split_dot(sin_table, value_re)
    return (part_re, part_im)


def body(retarded, self_energy, energy_of):
    component = lax.axis_index("comp")
    momentum = component // 2
    greater = component % 2
    tile_count = lax.axis_size("tile")
    rep_count = lax.axis_size("rep")
    green_matrix = lax.dynamic_index_in_dim(retarded, momentum, 0, keepdims=False)
    sigma_matrix = self_energy[0]
    green_re, green_im = (green_matrix[:, 0], green_matrix[:, 1])
    sigma_re, sigma_im = (sigma_matrix[:, 0], sigma_matrix[:, 1])
    left_re = (
        batched(green_re, sigma_re, "eik,ekj->eij") - batched(green_im, sigma_im, "eik,ekj->eij")
    ).astype(jnp.bfloat16)
    left_im = (
        batched(green_re, sigma_im, "eik,ekj->eij") + batched(green_im, sigma_re, "eik,ekj->eij")
    ).astype(jnp.bfloat16)
    out_re = batched(left_re, green_re, "eik,ejk->eij") + batched(left_im, green_im, "eik,ejk->eij")
    out_im = batched(left_im, green_re, "eik,ejk->eij") - batched(left_re, green_im, "eik,ejk->eij")
    stacked = jnp.stack([out_re, out_im]).astype(jnp.bfloat16)
    stacked = jnp.where(greater == 1, jnp.swapaxes(stacked, 2, 3), stacked)
    energy_dev = stacked.shape[1]
    block_order = stacked.shape[2]
    elem_count = block_order * block_order // (tile_count * rep_count)
    slot_count = energy_of.shape[0]
    blocks = stacked.reshape(2, energy_dev, rep_count, tile_count, elem_count)
    first_pass = lax.all_to_all(blocks, "rep", split_axis=2, concat_axis=1, tiled=True)
    gathered = lax.all_to_all(first_pass, "tile", split_axis=3, concat_axis=1, tiled=True)
    signal = gathered.reshape(2, slot_count, elem_count)
    freq_count = 2 * slot_count
    frequency = lax.iota(jnp.int32, freq_count)
    fwd_cos, fwd_sin = phase_tables(frequency, energy_of, freq_count)
    own_re, own_im = rotate(fwd_cos, fwd_sin, signal[0], signal[1], -1.0)
    partner = from_partner(signal, "comp", 0)
    other_re, other_im = rotate(fwd_cos, fwd_sin, partner[0], partner[1], 1.0)
    cross_re = (own_re * other_re - own_im * other_im).astype(jnp.bfloat16)
    cross_im = (own_re * other_im + own_im * other_re).astype(jnp.bfloat16)
    lag_index = lax.iota(jnp.int32, slot_count)
    inv_cos, inv_sin = phase_tables(lag_index, frequency, freq_count)
    back_re, back_im = rotate(inv_cos, inv_sin, cross_re, cross_im, 1.0)
    norm_factor = 1.0 / (freq_count * math.sqrt(slot_count))
    polar_parts = jnp.stack([back_im * norm_factor, -back_re * norm_factor], axis=1)
    regrouped = lax.all_to_all(
        polar_parts[:, :, None, :], "tile", split_axis=0, concat_axis=2, tiled=True
    )
    lag_count = slot_count // tile_count
    return regrouped.reshape(lag_count, 2, block_order // rep_count, block_order)[None]


LANES = 128
ROWS = 8
KERNEL_BYTES = 62 * 2**20


def matmul(left_side, right_side, contract):
    return lax.dot_general(
        left_side, right_side, (((1,), (contract,)), ((), ())), preferred_element_type=jnp.float32
    )


def rotated(values):
    return pltpu.roll(values, LANES // 2, axis=1)


def polar_kernel(
    axis_sizes,
    retarded,
    self_energy,
    energy_of,
    arrived,
    green_in,
    sigma_in,
    energies,
    outgoing,
    ordered,
    lagged,
    load_sem,
    first_send,
    first_recv,
    second_send,
    second_recv,
    keep_sem,
    *gathered,
):
    tile_count, rep_count = axis_sizes
    component = lax.axis_index("comp")
    tile = lax.axis_index("tile")
    rep = lax.axis_index("rep")
    momentum = component // 2
    greater = component % 2
    energy_dev, block_order = green_in.shape[0], green_in.shape[2]
    slot_count = energies.shape[0]
    unit_count = arrived.shape[0]
    lag_count = arrived.shape[1]
    row_count = block_order // rep_count
    low_units = row_count // ROWS
    owner_count = 2 * tile_count
    peer_count = owner_count * rep_count
    base_units = unit_count // owner_count
    has_spare = unit_count % owner_count != 0

    owner = tile * 2 + greater

    def first_unit(which):
        return which * unit_count // owner_count

    def takes_spare(which):
        return first_unit(which + 1) - first_unit(which) > base_units

    half = tile_count // 2
    if tile_count % 2 == 0:
        own_half = tile // half * half
        other_half = (own_half + half) % tile_count
        tiles = [own_half + (tile + step) % half for step in range(half)]
        tiles += [other_half + (tile + step) % half for step in range(half)]
    else:
        tiles = [(tile + step) % tile_count for step in range(tile_count)]
    reps = [(rep + step) % rep_count for step in range(rep_count)]
    parts = [greater, 1 - greater]
    owners = [[tiles[i] * 2 + parts[j] for j in range(2)] for i in range(tile_count)]
    firsts = [[first_unit(owners[i][j]) for j in range(2)] for i in range(tile_count)]
    spares_at = [[takes_spare(owners[i][j]) for j in range(2)] for i in range(tile_count)]
    far_first = [(step + half) % tile_count for step in range(tile_count)]
    near_owners = [(i, j) for i in far_first for j in range(2) if (i, j) != (0, 0)]
    peers = [
        (i, j, k)
        for i in far_first
        for k in reversed(range(rep_count))
        for j in range(2)
        if (i, j, k) != (0, 0, 0)
    ]

    def device_of(i, j, k):
        return (momentum * 2 + parts[j], tiles[i], reps[k])

    loads = []
    for energy in range(energy_dev):
        loads.append(
            (
                pltpu.make_async_copy(
                    retarded.at[momentum, energy], green_in.at[energy], load_sem.at[2 * energy]
                ),
                pltpu.make_async_copy(
                    self_energy.at[0, energy], sigma_in.at[energy], load_sem.at[2 * energy + 1]
                ),
            )
        )
        for load in loads[-1]:
            load.start()
    energy_load = pltpu.make_async_copy(energy_of, energies, load_sem.at[2 * energy_dev])
    energy_load.start()

    barrier = pltpu.get_barrier_semaphore()
    for peer in peers:
        pl.semaphore_signal(
            barrier,
            inc=1,
            device_id=device_of(*peer),
            device_id_type=pl.DeviceIdType.MESH,
        )

    def finish(energy, left, right, sign):
        low, high = slice(0, LANES), slice(LANES, block_order)
        right_re, right_im = right
        with_re = jnp.concatenate(
            [right_re[low], -sign * right_im[low], right_re[high], -sign * right_im[high]]
        )
        with_im = jnp.concatenate(
            [right_im[low], sign * right_re[low], right_im[high], sign * right_re[high]]
        )
        result = matmul(left[0], with_re, 1) + matmul(left[1], with_im, 1)
        is_low = lax.broadcasted_iota(jnp.int32, (row_count // 2, LANES), 1) < LANES // 2
        for part in range(rep_count):
            rows = slice(part * row_count, (part + 1) * row_count)
            mixed = result[rows, 2 * LANES :]
            upper, lower = mixed[: row_count // 2], mixed[row_count // 2 :]
            high_re = jnp.where(is_low, upper, rotated(lower))
            high_im = jnp.where(is_low, rotated(upper), lower)
            pieces_re = jnp.concatenate([result[rows, :LANES], high_re])
            pieces_im = jnp.concatenate([result[rows, LANES : 2 * LANES], high_im])
            packed = jnp.concatenate(
                [
                    pieces_re.reshape(unit_count, ROWS, LANES),
                    pieces_im.reshape(unit_count, ROWS, LANES),
                ],
                axis=1,
            )
            outgoing[part, :, energy] = packed.astype(jnp.bfloat16)

    my_slot = greater * slot_count + (tile * rep_count + rep) * energy_dev

    def send_first(unit, energy):
        for i, j, k in peers:
            copy = pltpu.make_async_remote_copy(
                src_ref=outgoing.at[reps[k], firsts[i][j] + unit, energy],
                dst_ref=gathered[unit].at[my_slot + energy],
                send_sem=first_send.at[unit],
                recv_sem=first_recv.at[unit],
                device_id=device_of(i, j, k),
                device_id_type=pl.DeviceIdType.MESH,
            )
            if unit < base_units:
                copy.start()
            else:
                pl.when(spares_at[i][j])(copy.start)

    def keep_own(unit):
        gathered[unit][pl.ds(my_slot, energy_dev)] = outgoing[rep, firsts[0][0] + unit]

    for energy in range(energy_dev):
        for load in loads[energy]:
            load.wait()
        green_re, green_im = green_in[energy, 0], green_in[energy, 1]
        sigma_re, sigma_im = sigma_in[energy, 0], sigma_in[energy, 1]
        left_re = (matmul(green_re, sigma_re, 0) - matmul(green_im, sigma_im, 0)).astype(jnp.bfloat16)
        left_im = (matmul(green_re, sigma_im, 0) + matmul(green_im, sigma_re, 0)).astype(jnp.bfloat16)

        @pl.when(greater == 0)
        def _():
            finish(energy, (left_re, left_im), (green_re, green_im), 1)

        @pl.when(greater == 1)
        def _():
            finish(energy, (green_re, green_im), (left_re, left_im), -1)

        if energy == 0:
            pl.semaphore_wait(barrier, peer_count - 1)
        for unit in range(base_units + has_spare):
            send_first(unit, energy)

    def wait_for(buffer, sem):
        pltpu.make_async_copy(buffer, buffer, sem).wait()

    for unit in range(base_units):
        keep_own(unit)
    if has_spare:
        pl.when(spares_at[0][0])(functools.partial(keep_own, base_units))

    energy_load.wait()
    slots = []
    for energy in range(slot_count):
        slot = 0
        for candidate in range(slot_count):
            slot = jnp.where(energies[candidate] == energy, candidate, slot)
        slots.append(slot)

    norm_factor = 1.0 / math.sqrt(slot_count)

    def keep_lags(unit):
        return pltpu.make_async_copy(
            lagged.at[unit, greater, pl.ds(tile * lag_count, lag_count)],
            arrived.at[firsts[0][0] + unit],
            keep_sem.at[unit],
        )

    def correlate(unit):
        wait_for(
            gathered[unit].at[pl.ds(0, (peer_count - 1) * energy_dev)], first_recv.at[unit]
        )
        for part in range(2):
            for energy in range(slot_count):
                ordered[part, energy] = gathered[unit][part * slot_count + slots[energy]].astype(
                    jnp.float32
                )
        for lag in range(slot_count):
            for part in range(2):
                own_re = ordered[part, lag:, :ROWS]
                own_im = ordered[part, lag:, ROWS:]
                other_re = ordered[1 - part, : slot_count - lag, :ROWS]
                other_im = ordered[1 - part, : slot_count - lag, ROWS:]
                sum_re = jnp.sum(own_re * other_re - own_im * other_im, axis=0)
                sum_im = jnp.sum(own_re * other_im + own_im * other_re, axis=0)
                lagged[unit, part, lag] = jnp.concatenate(
                    [sum_im * norm_factor, sum_re * -norm_factor]
                ).astype(jnp.bfloat16)
        my_unit = firsts[0][0] + unit
        for i, j in near_owners:
            pltpu.make_async_remote_copy(
                src_ref=lagged.at[unit, parts[j], pl.ds(tiles[i] * lag_count, lag_count)],
                dst_ref=arrived.at[my_unit],
                send_sem=second_send.at[unit],
                recv_sem=second_recv.at[unit],
                device_id=device_of(i, j, 0),
                device_id_type=pl.DeviceIdType.MESH,
            ).start()
        keep_lags(unit).start()

    for unit in range(base_units):
        correlate(unit)
    if has_spare:
        pl.when(spares_at[0][0])(functools.partial(correlate, base_units))

    for unit in range(base_units):
        wait_for(
            gathered[unit].at[pl.ds(0, (peer_count - 1) * energy_dev)], first_send.at[unit]
        )
        wait_for(arrived.at[pl.ds(0, owner_count - 1)], second_send.at[unit])
        wait_for(arrived.at[pl.ds(0, owner_count - 1)], second_recv.at[unit])
        keep_lags(unit).wait()
    if has_spare:
        spare_units = unit_count % owner_count
        spares = spare_units * rep_count

        @pl.when(spares_at[0][0])
        def _():
            if spares > 1:
                wait_for(
                    gathered[base_units].at[pl.ds(0, (spares - 1) * energy_dev)],
                    first_send.at[base_units],
                )
            wait_for(arrived.at[pl.ds(0, owner_count - 1)], second_send.at[base_units])
            keep_lags(base_units).wait()
            if spare_units > 1:
                wait_for(arrived.at[pl.ds(0, spare_units - 1)], second_recv.at[base_units])

        @pl.when(jnp.logical_not(spares_at[0][0]))
        def _():
            wait_for(
                gathered[base_units].at[pl.ds(0, spares * energy_dev)], first_send.at[base_units]
            )
            wait_for(arrived.at[pl.ds(0, spare_units)], second_recv.at[base_units])


def unpack_kernel(arrived, polar, packed, unpacked, load_sem, store_sem):
    unit_count, lag_count = arrived.shape[:2]
    row_count = polar.shape[3]
    low_units = row_count // ROWS
    loads = [
        pltpu.make_async_copy(arrived.at[:, lag], packed.at[lag], load_sem.at[lag])
        for lag in range(lag_count)
    ]
    stores = [
        pltpu.make_async_copy(unpacked.at[lag], polar.at[0, lag], store_sem.at[lag])
        for lag in range(lag_count)
    ]
    for load in loads:
        load.start()
    for lag in range(lag_count):
        loads[lag].wait()
        for unit in range(unit_count):
            values = packed[lag, unit].astype(jnp.float32)
            for part in range(2):
                block = values[part * ROWS : (part + 1) * ROWS]
                if unit < low_units:
                    unpacked[lag, part, unit * ROWS : (unit + 1) * ROWS, :LANES] = block
                else:
                    row = (unit - low_units) * ROWS
                    row_low = row + row_count // 2
                    unpacked[lag, part, row : row + ROWS, LANES:] = block[:, : LANES // 2]
                    unpacked[lag, part, row_low : row_low + ROWS, LANES:] = rotated(block)[
                        :, : LANES // 2
                    ]
        stores[lag].start()
    for store in stores:
        store.wait()


def fits(sizes, energy_dev, block_order):
    comp_count, tile_count, rep_count = sizes
    return (
        comp_count % 2 == 0
        and block_order == LANES + LANES // 2
        and block_order % (2 * ROWS * 2 * rep_count) == 0
        and block_order * 3 // (4 * ROWS * rep_count) >= 2 * tile_count
        and tile_count * rep_count * energy_dev <= 4 * ROWS
    )


def fused(sizes, retarded, self_energy, energy_of):
    _, tile_count, rep_count = sizes
    energy_dev, block_order = retarded.shape[1], retarded.shape[-1]
    slot_count = energy_of.shape[0]
    lag_count = slot_count // tile_count
    row_count = block_order // rep_count
    unit_count = row_count * block_order // (ROWS * LANES)
    units_held = -(-unit_count // (2 * tile_count))
    packed = (2 * ROWS, LANES)
    arrived = pl.pallas_call(
        functools.partial(polar_kernel, (tile_count, rep_count)),
        out_shape=jax.ShapeDtypeStruct((unit_count, lag_count) + packed, jnp.bfloat16),
        in_specs=[pl.BlockSpec(memory_space=pl.ANY)] * 3,
        out_specs=pl.BlockSpec(memory_space=pl.ANY),
        scratch_shapes=[
            pltpu.VMEM(retarded.shape[1:], jnp.bfloat16),
            pltpu.VMEM(self_energy.shape[1:], jnp.bfloat16),
            pltpu.SMEM((slot_count,), jnp.int32),
            pltpu.VMEM((rep_count, unit_count, energy_dev) + packed, jnp.bfloat16),
            pltpu.VMEM((2, slot_count) + packed, jnp.float32),
            pltpu.VMEM((units_held, 2, slot_count) + packed, jnp.bfloat16),
            pltpu.SemaphoreType.DMA((2 * energy_dev + 1,)),
            pltpu.SemaphoreType.DMA((units_held,)),
            pltpu.SemaphoreType.DMA((units_held,)),
            pltpu.SemaphoreType.DMA((units_held,)),
            pltpu.SemaphoreType.DMA((units_held,)),
            pltpu.SemaphoreType.DMA((units_held,)),
        ]
        + [pltpu.VMEM((2 * slot_count,) + packed, jnp.bfloat16)] * units_held,
        compiler_params=pltpu.CompilerParams(
            collective_id=0, has_side_effects=True, vmem_limit_bytes=KERNEL_BYTES
        ),
    )(retarded, self_energy, energy_of)
    return pl.pallas_call(
        unpack_kernel,
        out_shape=jax.ShapeDtypeStruct((1, lag_count, 2, row_count, block_order), jnp.float32),
        in_specs=[pl.BlockSpec(memory_space=pl.ANY)],
        out_specs=pl.BlockSpec(memory_space=pl.ANY),
        scratch_shapes=[
            pltpu.VMEM((lag_count, unit_count) + packed, jnp.bfloat16),
            pltpu.VMEM((lag_count, 2, row_count, block_order), jnp.float32),
            pltpu.SemaphoreType.DMA((lag_count,)),
            pltpu.SemaphoreType.DMA((lag_count,)),
        ],
        compiler_params=pltpu.CompilerParams(vmem_limit_bytes=KERNEL_BYTES),
    )(arrived)


def solution(mesh):
    placed = (
        P(None, ("tile", "rep"), None, None, None),
        P("comp", ("tile", "rep"), None, None, None),
        P(),
    )
    sizes = tuple(mesh.shape[name] for name in ("comp", "tile", "rep"))

    def device_body(retarded, self_energy, energy_of):
        if fits(sizes, retarded.shape[1], retarded.shape[-1]):
            return fused(sizes, retarded, self_energy, energy_of)
        return body(retarded, self_energy, energy_of)

    return jax.shard_map(
        device_body,
        mesh=mesh,
        in_specs=placed,
        out_specs=P("comp", "tile", None, "rep", None),
        check_vma=False,
    )
```

```python
import functools
import math

import jax
import jax.numpy as jnp
from jax import lax
from jax.experimental import pallas as pl
from jax.experimental.pallas import tpu as pltpu
from jax.sharding import PartitionSpec as P


def from_partner(array, axis, distance):
    return lax.ppermute(array, axis, [(i, i ^ 1 << distance) for i in range(lax.axis_size(axis))])


def batched(left_side, right_side, pattern):
    return jnp.einsum(pattern, left_side, right_side, preferred_element_type=jnp.float32)


def phase_tables(row_values, col_values, modulus):
    phase_index = row_values[:, None] * col_values[None, :] % modulus
    phase_angle = phase_index.astype(jnp.float32) * (2.0 * math.pi / modulus)
    cos_full = jnp.cos(phase_angle)
    sin_full = jnp.sin(phase_angle)
    cos_high = cos_full.astype(jnp.bfloat16)
    sin_high = sin_full.astype(jnp.bfloat16)
    cos_low = (cos_full - cos_high.astype(jnp.float32)).astype(jnp.bfloat16)
    sin_low = (sin_full - sin_high.astype(jnp.float32)).astype(jnp.bfloat16)
    return ((cos_high, cos_low), (sin_high, sin_low))


def split_dot(table_pair, values):
    return jnp.dot(table_pair[0], values, preferred_element_type=jnp.float32) + jnp.dot(
        table_pair[1], values, preferred_element_type=jnp.float32
    )


def rotate(cos_table, sin_table, value_re, value_im, direction):
    part_re = split_dot(cos_table, value_re) - direction * split_dot(sin_table, value_im)
    part_im = split_dot(cos_table, value_im) + direction * split_dot(sin_table, value_re)
    return (part_re, part_im)


def body(retarded, self_energy, energy_of):
    component = lax.axis_index("comp")
    momentum = component // 2
    greater = component % 2
    tile_count = lax.axis_size("tile")
    rep_count = lax.axis_size("rep")
    green_matrix = lax.dynamic_index_in_dim(retarded, momentum, 0, keepdims=False)
    sigma_matrix = self_energy[0]
    green_re, green_im = (green_matrix[:, 0], green_matrix[:, 1])
    sigma_re, sigma_im = (sigma_matrix[:, 0], sigma_matrix[:, 1])
    left_re = (
        batched(green_re, sigma_re, "eik,ekj->eij") - batched(green_im, sigma_im, "eik,ekj->eij")
    ).astype(jnp.bfloat16)
    left_im = (
        batched(green_re, sigma_im, "eik,ekj->eij") + batched(green_im, sigma_re, "eik,ekj->eij")
    ).astype(jnp.bfloat16)
    out_re = batched(left_re, green_re, "eik,ejk->eij") + batched(left_im, green_im, "eik,ejk->eij")
    out_im = batched(left_im, green_re, "eik,ejk->eij") - batched(left_re, green_im, "eik,ejk->eij")
    stacked = jnp.stack([out_re, out_im]).astype(jnp.bfloat16)
    stacked = jnp.where(greater == 1, jnp.swapaxes(stacked, 2, 3), stacked)
    energy_dev = stacked.shape[1]
    block_order = stacked.shape[2]
    elem_count = block_order * block_order // (tile_count * rep_count)
    slot_count = energy_of.shape[0]
    blocks = stacked.reshape(2, energy_dev, rep_count, tile_count, elem_count)
    first_pass = lax.all_to_all(blocks, "rep", split_axis=2, concat_axis=1, tiled=True)
    gathered = lax.all_to_all(first_pass, "tile", split_axis=3, concat_axis=1, tiled=True)
    signal = gathered.reshape(2, slot_count, elem_count)
    freq_count = 2 * slot_count
    frequency = lax.iota(jnp.int32, freq_count)
    fwd_cos, fwd_sin = phase_tables(frequency, energy_of, freq_count)
    own_re, own_im = rotate(fwd_cos, fwd_sin, signal[0], signal[1], -1.0)
    partner = from_partner(signal, "comp", 0)
    other_re, other_im = rotate(fwd_cos, fwd_sin, partner[0], partner[1], 1.0)
    cross_re = (own_re * other_re - own_im * other_im).astype(jnp.bfloat16)
    cross_im = (own_re * other_im + own_im * other_re).astype(jnp.bfloat16)
    lag_index = lax.iota(jnp.int32, slot_count)
    inv_cos, inv_sin = phase_tables(lag_index, frequency, freq_count)
    back_re, back_im = rotate(inv_cos, inv_sin, cross_re, cross_im, 1.0)
    norm_factor = 1.0 / (freq_count * math.sqrt(slot_count))
    polar_parts = jnp.stack([back_im * norm_factor, -back_re * norm_factor], axis=1)
    regrouped = lax.all_to_all(
        polar_parts[:, :, None, :], "tile", split_axis=0, concat_axis=2, tiled=True
    )
    lag_count = slot_count // tile_count
    return regrouped.reshape(lag_count, 2, block_order // rep_count, block_order)[None]


LANES = 128
ROWS = 8
KERNEL_BYTES = 62 * 2**20


def matmul(left_side, right_side, contract):
    return lax.dot_general(
        left_side, right_side, (((1,), (contract,)), ((), ())), preferred_element_type=jnp.float32
    )


def rotated(values):
    return pltpu.roll(values, LANES // 2, axis=1)


def polar_kernel(
    axis_sizes,
    retarded,
    self_energy,
    energy_of,
    arrived,
    green_in,
    sigma_in,
    energies,
    outgoing,
    ordered,
    lagged,
    load_sem,
    first_send,
    first_recv,
    second_send,
    second_recv,
    keep_sem,
    *gathered,
):
    tile_count, rep_count = axis_sizes
    component = lax.axis_index("comp")
    tile = lax.axis_index("tile")
    rep = lax.axis_index("rep")
    momentum = component // 2
    greater = component % 2
    energy_dev, block_order = green_in.shape[0], green_in.shape[2]
    slot_count = energies.shape[0]
    unit_count = arrived.shape[0]
    lag_count = arrived.shape[1]
    row_count = block_order // rep_count
    low_units = row_count // ROWS
    owner_count = 2 * tile_count
    peer_count = owner_count * rep_count
    base_units = unit_count // owner_count
    has_spare = unit_count % owner_count != 0

    owner = tile * 2 + greater

    def first_unit(which):
        return which * unit_count // owner_count

    def takes_spare(which):
        return first_unit(which + 1) - first_unit(which) > base_units

    half = tile_count // 2
    if tile_count % 2 == 0:
        own_half = tile // half * half
        other_half = (own_half + half) % tile_count
        tiles = [own_half + (tile + step) % half for step in range(half)]
        tiles += [other_half + (tile + step) % half for step in range(half)]
    else:
        tiles = [(tile + step) % tile_count for step in range(tile_count)]
    reps = [(rep + step) % rep_count for step in range(rep_count)]
    parts = [greater, 1 - greater]
    owners = [[tiles[i] * 2 + parts[j] for j in range(2)] for i in range(tile_count)]
    firsts = [[first_unit(owners[i][j]) for j in range(2)] for i in range(tile_count)]
    spares_at = [[takes_spare(owners[i][j]) for j in range(2)] for i in range(tile_count)]
    far_first = [(step + half) % tile_count for step in range(tile_count)]
    near_owners = [(i, j) for i in far_first for j in range(2) if (i, j) != (0, 0)]
    peers = [
        (i, j, k)
        for i in far_first
        for k in reversed(range(rep_count))
        for j in range(2)
        if (i, j, k) != (0, 0, 0)
    ]

    def device_of(i, j, k):
        return (momentum * 2 + parts[j], tiles[i], reps[k])

    loads = []
    for energy in range(energy_dev):
        loads.append(
            (
                pltpu.make_async_copy(
                    retarded.at[momentum, energy], green_in.at[energy], load_sem.at[2 * energy]
                ),
                pltpu.make_async_copy(
                    self_energy.at[0, energy], sigma_in.at[energy], load_sem.at[2 * energy + 1]
                ),
            )
        )
        for load in loads[-1]:
            load.start()
    energy_load = pltpu.make_async_copy(energy_of, energies, load_sem.at[2 * energy_dev])
    energy_load.start()

    barrier = pltpu.get_barrier_semaphore()
    for peer in peers:
        pl.semaphore_signal(
            barrier,
            inc=1,
            device_id=device_of(*peer),
            device_id_type=pl.DeviceIdType.MESH,
        )

    def finish(energy, left, right, sign):
        low, high = slice(0, LANES), slice(LANES, block_order)
        right_re, right_im = right
        with_re = jnp.concatenate(
            [right_re[low], -sign * right_im[low], right_re[high], -sign * right_im[high]]
        )
        with_im = jnp.concatenate(
            [right_im[low], sign * right_re[low], right_im[high], sign * right_re[high]]
        )
        result = matmul(left[0], with_re, 1) + matmul(left[1], with_im, 1)
        is_low = lax.broadcasted_iota(jnp.int32, (row_count // 2, LANES), 1) < LANES // 2
        for part in range(rep_count):
            rows = slice(part * row_count, (part + 1) * row_count)
            mixed = result[rows, 2 * LANES :]
            upper, lower = mixed[: row_count // 2], mixed[row_count // 2 :]
            high_re = jnp.where(is_low, upper, rotated(lower))
            high_im = jnp.where(is_low, rotated(upper), lower)
            pieces_re = jnp.concatenate([result[rows, :LANES], high_re])
            pieces_im = jnp.concatenate([result[rows, LANES : 2 * LANES], high_im])
            packed = jnp.concatenate(
                [
                    pieces_re.reshape(unit_count, ROWS, LANES),
                    pieces_im.reshape(unit_count, ROWS, LANES),
                ],
                axis=1,
            )
            outgoing[part, :, energy] = packed.astype(jnp.bfloat16)

    my_slot = greater * slot_count + (tile * rep_count + rep) * energy_dev

    def send_first(unit):
        for i, j, k in peers:
            copy = pltpu.make_async_remote_copy(
                src_ref=outgoing.at[reps[k], firsts[i][j] + unit],
                dst_ref=gathered[unit].at[pl.ds(my_slot, energy_dev)],
                send_sem=first_send.at[unit],
                recv_sem=first_recv.at[unit],
                device_id=device_of(i, j, k),
                device_id_type=pl.DeviceIdType.MESH,
            )
            if unit < base_units:
                copy.start()
            else:
                pl.when(spares_at[i][j])(copy.start)

    def keep_own(unit):
        gathered[unit][pl.ds(my_slot, energy_dev)] = outgoing[rep, firsts[0][0] + unit]

    for energy in range(energy_dev):
        for load in loads[energy]:
            load.wait()
        green_re, green_im = green_in[energy, 0], green_in[energy, 1]
        sigma_re, sigma_im = sigma_in[energy, 0], sigma_in[energy, 1]
        left_re = (matmul(green_re, sigma_re, 0) - matmul(green_im, sigma_im, 0)).astype(jnp.bfloat16)
        left_im = (matmul(green_re, sigma_im, 0) + matmul(green_im, sigma_re, 0)).astype(jnp.bfloat16)

        @pl.when(greater == 0)
        def _():
            finish(energy, (left_re, left_im), (green_re, green_im), 1)

        @pl.when(greater == 1)
        def _():
            finish(energy, (green_re, green_im), (left_re, left_im), -1)

    pl.semaphore_wait(barrier, peer_count - 1)
    for unit in range(base_units + has_spare):
        send_first(unit)

    def wait_for(buffer, sem):
        pltpu.make_async_copy(buffer, buffer, sem).wait()

    for unit in range(base_units):
        keep_own(unit)
    if has_spare:
        pl.when(spares_at[0][0])(functools.partial(keep_own, base_units))

    energy_load.wait()
    slots = []
    for energy in range(slot_count):
        slot = 0
        for candidate in range(slot_count):
            slot = jnp.where(energies[candidate] == energy, candidate, slot)
        slots.append(slot)

    norm_factor = 1.0 / math.sqrt(slot_count)

    def keep_lags(unit):
        return pltpu.make_async_copy(
            lagged.at[unit, greater, pl.ds(tile * lag_count, lag_count)],
            arrived.at[firsts[0][0] + unit],
            keep_sem.at[unit],
        )

    def correlate(unit):
        wait_for(
            gathered[unit].at[pl.ds(0, (peer_count - 1) * energy_dev)], first_recv.at[unit]
        )
        for part in range(2):
            for energy in range(slot_count):
                ordered[part, energy] = gathered[unit][part * slot_count + slots[energy]].astype(
                    jnp.float32
                )
        for lag in range(slot_count):
            for part in range(2):
                own_re = ordered[part, lag:, :ROWS]
                own_im = ordered[part, lag:, ROWS:]
                other_re = ordered[1 - part, : slot_count - lag, :ROWS]
                other_im = ordered[1 - part, : slot_count - lag, ROWS:]
                sum_re = jnp.sum(own_re * other_re - own_im * other_im, axis=0)
                sum_im = jnp.sum(own_re * other_im + own_im * other_re, axis=0)
                lagged[unit, part, lag] = jnp.concatenate(
                    [sum_im * norm_factor, sum_re * -norm_factor]
                ).astype(jnp.bfloat16)
        my_unit = firsts[0][0] + unit
        for i, j in near_owners:
            pltpu.make_async_remote_copy(
                src_ref=lagged.at[unit, parts[j], pl.ds(tiles[i] * lag_count, lag_count)],
                dst_ref=arrived.at[my_unit],
                send_sem=second_send.at[unit],
                recv_sem=second_recv.at[unit],
                device_id=device_of(i, j, 0),
                device_id_type=pl.DeviceIdType.MESH,
            ).start()
        keep_lags(unit).start()

    for unit in range(base_units):
        correlate(unit)
    if has_spare:
        pl.when(spares_at[0][0])(functools.partial(correlate, base_units))

    for unit in range(base_units):
        wait_for(
            gathered[unit].at[pl.ds(0, (peer_count - 1) * energy_dev)], first_send.at[unit]
        )
        wait_for(arrived.at[pl.ds(0, owner_count - 1)], second_send.at[unit])
        wait_for(arrived.at[pl.ds(0, owner_count - 1)], second_recv.at[unit])
        keep_lags(unit).wait()
    if has_spare:
        spare_units = unit_count % owner_count
        spares = spare_units * rep_count

        @pl.when(spares_at[0][0])
        def _():
            if spares > 1:
                wait_for(
                    gathered[base_units].at[pl.ds(0, (spares - 1) * energy_dev)],
                    first_send.at[base_units],
                )
            wait_for(arrived.at[pl.ds(0, owner_count - 1)], second_send.at[base_units])
            keep_lags(base_units).wait()
            if spare_units > 1:
                wait_for(arrived.at[pl.ds(0, spare_units - 1)], second_recv.at[base_units])

        @pl.when(jnp.logical_not(spares_at[0][0]))
        def _():
            wait_for(
                gathered[base_units].at[pl.ds(0, spares * energy_dev)], first_send.at[base_units]
            )
            wait_for(arrived.at[pl.ds(0, spare_units)], second_recv.at[base_units])


def unpack_kernel(arrived, polar, packed, unpacked, load_sem, store_sem):
    unit_count, lag_count = arrived.shape[:2]
    row_count = polar.shape[3]
    low_units = row_count // ROWS
    loads = [
        pltpu.make_async_copy(arrived.at[:, lag], packed.at[lag], load_sem.at[lag])
        for lag in range(lag_count)
    ]
    stores = [
        pltpu.make_async_copy(unpacked.at[lag], polar.at[0, lag], store_sem.at[lag])
        for lag in range(lag_count)
    ]
    for load in loads:
        load.start()
    for lag in range(lag_count):
        loads[lag].wait()
        for unit in range(unit_count):
            values = packed[lag, unit].astype(jnp.float32)
            for part in range(2):
                block = values[part * ROWS : (part + 1) * ROWS]
                if unit < low_units:
                    unpacked[lag, part, unit * ROWS : (unit + 1) * ROWS, :LANES] = block
                else:
                    row = (unit - low_units) * ROWS
                    row_low = row + row_count // 2
                    unpacked[lag, part, row : row + ROWS, LANES:] = block[:, : LANES // 2]
                    unpacked[lag, part, row_low : row_low + ROWS, LANES:] = rotated(block)[
                        :, : LANES // 2
                    ]
        stores[lag].start()
    for store in stores:
        store.wait()


def fits(sizes, energy_dev, block_order):
    comp_count, tile_count, rep_count = sizes
    return (
        comp_count % 2 == 0
        and block_order == LANES + LANES // 2
        and block_order % (2 * ROWS * 2 * rep_count) == 0
        and block_order * 3 // (4 * ROWS * rep_count) >= 2 * tile_count
        and tile_count * rep_count * energy_dev <= 4 * ROWS
    )


def fused(sizes, retarded, self_energy, energy_of):
    _, tile_count, rep_count = sizes
    energy_dev, block_order = retarded.shape[1], retarded.shape[-1]
    slot_count = energy_of.shape[0]
    lag_count = slot_count // tile_count
    row_count = block_order // rep_count
    unit_count = row_count * block_order // (ROWS * LANES)
    units_held = -(-unit_count // (2 * tile_count))
    packed = (2 * ROWS, LANES)
    arrived = pl.pallas_call(
        functools.partial(polar_kernel, (tile_count, rep_count)),
        out_shape=jax.ShapeDtypeStruct((unit_count, lag_count) + packed, jnp.bfloat16),
        in_specs=[pl.BlockSpec(memory_space=pl.ANY)] * 3,
        out_specs=pl.BlockSpec(memory_space=pl.ANY),
        scratch_shapes=[
            pltpu.VMEM(retarded.shape[1:], jnp.bfloat16),
            pltpu.VMEM(self_energy.shape[1:], jnp.bfloat16),
            pltpu.SMEM((slot_count,), jnp.int32),
            pltpu.VMEM((rep_count, unit_count, energy_dev) + packed, jnp.bfloat16),
            pltpu.VMEM((2, slot_count) + packed, jnp.float32),
            pltpu.VMEM((units_held, 2, slot_count) + packed, jnp.bfloat16),
            pltpu.SemaphoreType.DMA((2 * energy_dev + 1,)),
            pltpu.SemaphoreType.DMA((units_held,)),
            pltpu.SemaphoreType.DMA((units_held,)),
            pltpu.SemaphoreType.DMA((units_held,)),
            pltpu.SemaphoreType.DMA((units_held,)),
            pltpu.SemaphoreType.DMA((units_held,)),
        ]
        + [pltpu.VMEM((2 * slot_count,) + packed, jnp.bfloat16)] * units_held,
        compiler_params=pltpu.CompilerParams(
            collective_id=0, has_side_effects=True, vmem_limit_bytes=KERNEL_BYTES
        ),
    )(retarded, self_energy, energy_of)
    return pl.pallas_call(
        unpack_kernel,
        out_shape=jax.ShapeDtypeStruct((1, lag_count, 2, row_count, block_order), jnp.float32),
        in_specs=[pl.BlockSpec(memory_space=pl.ANY)],
        out_specs=pl.BlockSpec(memory_space=pl.ANY),
        scratch_shapes=[
            pltpu.VMEM((lag_count, unit_count) + packed, jnp.bfloat16),
            pltpu.VMEM((lag_count, 2, row_count, block_order), jnp.float32),
            pltpu.SemaphoreType.DMA((lag_count,)),
            pltpu.SemaphoreType.DMA((lag_count,)),
        ],
        compiler_params=pltpu.CompilerParams(vmem_limit_bytes=KERNEL_BYTES),
    )(arrived)


def solution(mesh):
    placed = (
        P(None, ("tile", "rep"), None, None, None),
        P("comp", ("tile", "rep"), None, None, None),
        P(),
    )
    sizes = tuple(mesh.shape[name] for name in ("comp", "tile", "rep"))

    def device_body(retarded, self_energy, energy_of):
        if fits(sizes, retarded.shape[1], retarded.shape[-1]):
            return fused(sizes, retarded, self_energy, energy_of)
        return body(retarded, self_energy, energy_of)

    return jax.shard_map(
        device_body,
        mesh=mesh,
        in_specs=placed,
        out_specs=P("comp", "tile", None, "rep", None),
        check_vma=False,
    )
```

```python
import functools
import math

import jax
import jax.numpy as jnp
from jax import lax
from jax.experimental import pallas as pl
from jax.experimental.pallas import tpu as pltpu
from jax.sharding import PartitionSpec as P


def from_partner(array, axis, distance):
    return lax.ppermute(array, axis, [(i, i ^ 1 << distance) for i in range(lax.axis_size(axis))])


def batched(left_side, right_side, pattern):
    return jnp.einsum(pattern, left_side, right_side, preferred_element_type=jnp.float32)


def phase_tables(row_values, col_values, modulus):
    phase_index = row_values[:, None] * col_values[None, :] % modulus
    phase_angle = phase_index.astype(jnp.float32) * (2.0 * math.pi / modulus)
    cos_full = jnp.cos(phase_angle)
    sin_full = jnp.sin(phase_angle)
    cos_high = cos_full.astype(jnp.bfloat16)
    sin_high = sin_full.astype(jnp.bfloat16)
    cos_low = (cos_full - cos_high.astype(jnp.float32)).astype(jnp.bfloat16)
    sin_low = (sin_full - sin_high.astype(jnp.float32)).astype(jnp.bfloat16)
    return ((cos_high, cos_low), (sin_high, sin_low))


def split_dot(table_pair, values):
    return jnp.dot(table_pair[0], values, preferred_element_type=jnp.float32) + jnp.dot(
        table_pair[1], values, preferred_element_type=jnp.float32
    )


def rotate(cos_table, sin_table, value_re, value_im, direction):
    part_re = split_dot(cos_table, value_re) - direction * split_dot(sin_table, value_im)
    part_im = split_dot(cos_table, value_im) + direction * split_dot(sin_table, value_re)
    return (part_re, part_im)


def body(retarded, self_energy, energy_of):
    component = lax.axis_index("comp")
    momentum = component // 2
    greater = component % 2
    tile_count = lax.axis_size("tile")
    rep_count = lax.axis_size("rep")
    green_matrix = lax.dynamic_index_in_dim(retarded, momentum, 0, keepdims=False)
    sigma_matrix = self_energy[0]
    green_re, green_im = (green_matrix[:, 0], green_matrix[:, 1])
    sigma_re, sigma_im = (sigma_matrix[:, 0], sigma_matrix[:, 1])
    left_re = (
        batched(green_re, sigma_re, "eik,ekj->eij") - batched(green_im, sigma_im, "eik,ekj->eij")
    ).astype(jnp.bfloat16)
    left_im = (
        batched(green_re, sigma_im, "eik,ekj->eij") + batched(green_im, sigma_re, "eik,ekj->eij")
    ).astype(jnp.bfloat16)
    out_re = batched(left_re, green_re, "eik,ejk->eij") + batched(left_im, green_im, "eik,ejk->eij")
    out_im = batched(left_im, green_re, "eik,ejk->eij") - batched(left_re, green_im, "eik,ejk->eij")
    stacked = jnp.stack([out_re, out_im]).astype(jnp.bfloat16)
    stacked = jnp.where(greater == 1, jnp.swapaxes(stacked, 2, 3), stacked)
    energy_dev = stacked.shape[1]
    block_order = stacked.shape[2]
    elem_count = block_order * block_order // (tile_count * rep_count)
    slot_count = energy_of.shape[0]
    blocks = stacked.reshape(2, energy_dev, rep_count, tile_count, elem_count)
    first_pass = lax.all_to_all(blocks, "rep", split_axis=2, concat_axis=1, tiled=True)
    gathered = lax.all_to_all(first_pass, "tile", split_axis=3, concat_axis=1, tiled=True)
    signal = gathered.reshape(2, slot_count, elem_count)
    freq_count = 2 * slot_count
    frequency = lax.iota(jnp.int32, freq_count)
    fwd_cos, fwd_sin = phase_tables(frequency, energy_of, freq_count)
    own_re, own_im = rotate(fwd_cos, fwd_sin, signal[0], signal[1], -1.0)
    partner = from_partner(signal, "comp", 0)
    other_re, other_im = rotate(fwd_cos, fwd_sin, partner[0], partner[1], 1.0)
    cross_re = (own_re * other_re - own_im * other_im).astype(jnp.bfloat16)
    cross_im = (own_re * other_im + own_im * other_re).astype(jnp.bfloat16)
    lag_index = lax.iota(jnp.int32, slot_count)
    inv_cos, inv_sin = phase_tables(lag_index, frequency, freq_count)
    back_re, back_im = rotate(inv_cos, inv_sin, cross_re, cross_im, 1.0)
    norm_factor = 1.0 / (freq_count * math.sqrt(slot_count))
    polar_parts = jnp.stack([back_im * norm_factor, -back_re * norm_factor], axis=1)
    regrouped = lax.all_to_all(
        polar_parts[:, :, None, :], "tile", split_axis=0, concat_axis=2, tiled=True
    )
    lag_count = slot_count // tile_count
    return regrouped.reshape(lag_count, 2, block_order // rep_count, block_order)[None]


LANES = 128
ROWS = 8
KERNEL_BYTES = 62 * 2**20


def matmul(left_side, right_side, contract):
    return lax.dot_general(
        left_side, right_side, (((1,), (contract,)), ((), ())), preferred_element_type=jnp.float32
    )


def rotated(values):
    return pltpu.roll(values, LANES // 2, axis=1)


def polar_kernel(
    axis_sizes,
    retarded,
    self_energy,
    energy_of,
    arrived,
    green_in,
    sigma_in,
    energies,
    outgoing,
    ordered,
    lagged,
    load_sem,
    first_send,
    first_recv,
    second_send,
    second_recv,
    keep_sem,
    *gathered,
):
    tile_count, rep_count = axis_sizes
    component = lax.axis_index("comp")
    tile = lax.axis_index("tile")
    rep = lax.axis_index("rep")
    momentum = component // 2
    greater = component % 2
    energy_dev, block_order = green_in.shape[0], green_in.shape[2]
    slot_count = energies.shape[0]
    unit_count = arrived.shape[0]
    lag_count = arrived.shape[1]
    row_count = block_order // rep_count
    low_units = row_count // ROWS
    owner_count = 2 * tile_count
    peer_count = owner_count * rep_count
    base_units = unit_count // owner_count
    has_spare = unit_count % owner_count != 0

    owner = tile * 2 + greater

    def first_unit(which):
        return which * unit_count // owner_count

    def takes_spare(which):
        return first_unit(which + 1) - first_unit(which) > base_units

    half = tile_count // 2
    if tile_count % 2 == 0:
        own_half = tile // half * half
        other_half = (own_half + half) % tile_count
        tiles = [own_half + (tile + step) % half for step in range(half)]
        tiles += [other_half + (tile + step) % half for step in range(half)]
    else:
        tiles = [(tile + step) % tile_count for step in range(tile_count)]
    reps = [(rep + step) % rep_count for step in range(rep_count)]
    parts = [greater, 1 - greater]
    owners = [[tiles[i] * 2 + parts[j] for j in range(2)] for i in range(tile_count)]
    firsts = [[first_unit(owners[i][j]) for j in range(2)] for i in range(tile_count)]
    spares_at = [[takes_spare(owners[i][j]) for j in range(2)] for i in range(tile_count)]
    far_first = [(step + half) % tile_count for step in range(tile_count)]
    near_owners = [(i, j) for i in far_first for j in range(2) if (i, j) != (0, 0)]
    peers = [
        (i, j, k)
        for i in far_first
        for k in reversed(range(rep_count))
        for j in range(2)
        if (i, j, k) != (0, 0, 0)
    ]

    def device_of(i, j, k):
        return (momentum * 2 + parts[j], tiles[i], reps[k])

    loads = []
    for energy in range(energy_dev):
        loads.append(
            (
                pltpu.make_async_copy(
                    retarded.at[momentum, energy], green_in.at[energy], load_sem.at[2 * energy]
                ),
                pltpu.make_async_copy(
                    self_energy.at[0, energy], sigma_in.at[energy], load_sem.at[2 * energy + 1]
                ),
            )
        )
        for load in loads[-1]:
            load.start()
    energy_load = pltpu.make_async_copy(energy_of, energies, load_sem.at[2 * energy_dev])
    energy_load.start()

    barrier = pltpu.get_barrier_semaphore()
    for peer in peers:
        pl.semaphore_signal(
            barrier,
            inc=1,
            device_id=device_of(*peer),
            device_id_type=pl.DeviceIdType.MESH,
        )

    def finish(energy, left, right, sign):
        low, high = slice(0, LANES), slice(LANES, block_order)
        right_re, right_im = right
        with_re = jnp.concatenate(
            [right_re[low], -sign * right_im[low], right_re[high], -sign * right_im[high]]
        )
        with_im = jnp.concatenate(
            [right_im[low], sign * right_re[low], right_im[high], sign * right_re[high]]
        )
        result = matmul(left[0], with_re, 1) + matmul(left[1], with_im, 1)
        is_low = lax.broadcasted_iota(jnp.int32, (row_count // 2, LANES), 1) < LANES // 2
        for part in range(rep_count):
            rows = slice(part * row_count, (part + 1) * row_count)
            mixed = result[rows, 2 * LANES :]
            upper, lower = mixed[: row_count // 2], mixed[row_count // 2 :]
            high_re = jnp.where(is_low, upper, rotated(lower))
            high_im = jnp.where(is_low, rotated(upper), lower)
            pieces_re = jnp.concatenate([result[rows, :LANES], high_re])
            pieces_im = jnp.concatenate([result[rows, LANES : 2 * LANES], high_im])
            packed = jnp.concatenate(
                [
                    pieces_re.reshape(unit_count, ROWS, LANES),
                    pieces_im.reshape(unit_count, ROWS, LANES),
                ],
                axis=1,
            )
            outgoing[part, :, energy] = packed.astype(jnp.bfloat16)

    half_count = tile_count * rep_count
    my_place = greater * half_count + tile * rep_count + rep
    groups = [(0, base_units)] + [(base_units, 1)] * has_spare

    def send_first(group):
        start, size = groups[group]
        for i, j, k in peers:
            copy = pltpu.make_async_remote_copy(
                src_ref=outgoing.at[reps[k], pl.ds(firsts[i][j] + start, size)],
                dst_ref=gathered[group].at[my_place],
                send_sem=first_send.at[group],
                recv_sem=first_recv.at[group],
                device_id=device_of(i, j, k),
                device_id_type=pl.DeviceIdType.MESH,
            )
            if start == 0:
                copy.start()
            else:
                pl.when(spares_at[i][j])(copy.start)

    def keep_own(group):
        start, size = groups[group]
        gathered[group][my_place] = outgoing[rep, pl.ds(firsts[0][0] + start, size)]

    for energy in range(energy_dev):
        for load in loads[energy]:
            load.wait()
        green_re, green_im = green_in[energy, 0], green_in[energy, 1]
        sigma_re, sigma_im = sigma_in[energy, 0], sigma_in[energy, 1]
        left_re = (matmul(green_re, sigma_re, 0) - matmul(green_im, sigma_im, 0)).astype(jnp.bfloat16)
        left_im = (matmul(green_re, sigma_im, 0) + matmul(green_im, sigma_re, 0)).astype(jnp.bfloat16)

        @pl.when(greater == 0)
        def _():
            finish(energy, (left_re, left_im), (green_re, green_im), 1)

        @pl.when(greater == 1)
        def _():
            finish(energy, (green_re, green_im), (left_re, left_im), -1)

    pl.semaphore_wait(barrier, peer_count - 1)
    for group in range(len(groups)):
        send_first(group)

    def wait_for(buffer, sem):
        pltpu.make_async_copy(buffer, buffer, sem).wait()

    keep_own(0)
    if has_spare:
        pl.when(spares_at[0][0])(functools.partial(keep_own, 1))

    energy_load.wait()
    slots = []
    for energy in range(slot_count):
        source, local = 0, 0
        for candidate in range(slot_count):
            held = energies[candidate] == energy
            source = jnp.where(held, candidate // energy_dev, source)
            local = jnp.where(held, candidate % energy_dev, local)
        slots.append((source, local))

    norm_factor = 1.0 / math.sqrt(slot_count)

    def keep_lags(unit):
        return pltpu.make_async_copy(
            lagged.at[unit, greater, pl.ds(tile * lag_count, lag_count)],
            arrived.at[firsts[0][0] + unit],
            keep_sem.at[unit],
        )

    def correlate(unit):
        group = unit // base_units
        start, _ = groups[group]
        if unit == start:
            wait_for(gathered[group].at[pl.ds(0, peer_count - 1)], first_recv.at[group])
        for part in range(2):
            for energy, (source, local) in enumerate(slots):
                ordered[part, energy] = gathered[group][
                    part * half_count + source, unit - start, local
                ].astype(jnp.float32)
        for lag in range(slot_count):
            for part in range(2):
                own_re = ordered[part, lag:, :ROWS]
                own_im = ordered[part, lag:, ROWS:]
                other_re = ordered[1 - part, : slot_count - lag, :ROWS]
                other_im = ordered[1 - part, : slot_count - lag, ROWS:]
                sum_re = jnp.sum(own_re * other_re - own_im * other_im, axis=0)
                sum_im = jnp.sum(own_re * other_im + own_im * other_re, axis=0)
                lagged[unit, part, lag] = jnp.concatenate(
                    [sum_im * norm_factor, sum_re * -norm_factor]
                ).astype(jnp.bfloat16)
        my_unit = firsts[0][0] + unit
        for i, j in near_owners:
            pltpu.make_async_remote_copy(
                src_ref=lagged.at[unit, parts[j], pl.ds(tiles[i] * lag_count, lag_count)],
                dst_ref=arrived.at[my_unit],
                send_sem=second_send.at[unit],
                recv_sem=second_recv.at[unit],
                device_id=device_of(i, j, 0),
                device_id_type=pl.DeviceIdType.MESH,
            ).start()
        keep_lags(unit).start()

    for unit in range(base_units):
        correlate(unit)
    if has_spare:
        pl.when(spares_at[0][0])(functools.partial(correlate, base_units))

    wait_for(gathered[0].at[pl.ds(0, peer_count - 1)], first_send.at[0])
    for unit in range(base_units):
        wait_for(arrived.at[pl.ds(0, owner_count - 1)], second_send.at[unit])
        wait_for(arrived.at[pl.ds(0, owner_count - 1)], second_recv.at[unit])
        keep_lags(unit).wait()
    if has_spare:
        spare_units = unit_count % owner_count
        spares = spare_units * rep_count

        @pl.when(spares_at[0][0])
        def _():
            if spares > 1:
                wait_for(gathered[1].at[pl.ds(0, spares - 1)], first_send.at[1])
            wait_for(arrived.at[pl.ds(0, owner_count - 1)], second_send.at[base_units])
            keep_lags(base_units).wait()
            if spare_units > 1:
                wait_for(arrived.at[pl.ds(0, spare_units - 1)], second_recv.at[base_units])

        @pl.when(jnp.logical_not(spares_at[0][0]))
        def _():
            wait_for(gathered[1].at[pl.ds(0, spares)], first_send.at[1])
            wait_for(arrived.at[pl.ds(0, spare_units)], second_recv.at[base_units])


def unpack_kernel(arrived, polar, packed, unpacked, load_sem, store_sem):
    unit_count, lag_count = arrived.shape[:2]
    row_count = polar.shape[3]
    low_units = row_count // ROWS
    loads = [
        pltpu.make_async_copy(arrived.at[:, lag], packed.at[lag], load_sem.at[lag])
        for lag in range(lag_count)
    ]
    stores = [
        pltpu.make_async_copy(unpacked.at[lag], polar.at[0, lag], store_sem.at[lag])
        for lag in range(lag_count)
    ]
    for load in loads:
        load.start()
    for lag in range(lag_count):
        loads[lag].wait()
        for unit in range(unit_count):
            values = packed[lag, unit].astype(jnp.float32)
            for part in range(2):
                block = values[part * ROWS : (part + 1) * ROWS]
                if unit < low_units:
                    unpacked[lag, part, unit * ROWS : (unit + 1) * ROWS, :LANES] = block
                else:
                    row = (unit - low_units) * ROWS
                    row_low = row + row_count // 2
                    unpacked[lag, part, row : row + ROWS, LANES:] = block[:, : LANES // 2]
                    unpacked[lag, part, row_low : row_low + ROWS, LANES:] = rotated(block)[
                        :, : LANES // 2
                    ]
        stores[lag].start()
    for store in stores:
        store.wait()


def fits(sizes, energy_dev, block_order):
    comp_count, tile_count, rep_count = sizes
    return (
        comp_count % 2 == 0
        and block_order == LANES + LANES // 2
        and block_order % (2 * ROWS * 2 * rep_count) == 0
        and block_order * 3 // (4 * ROWS * rep_count) >= 2 * tile_count
        and tile_count * rep_count * energy_dev <= 4 * ROWS
    )


def fused(sizes, retarded, self_energy, energy_of):
    _, tile_count, rep_count = sizes
    energy_dev, block_order = retarded.shape[1], retarded.shape[-1]
    slot_count = energy_of.shape[0]
    lag_count = slot_count // tile_count
    row_count = block_order // rep_count
    unit_count = row_count * block_order // (ROWS * LANES)
    base_units = unit_count // (2 * tile_count)
    units_held = -(-unit_count // (2 * tile_count))
    group_sizes = [base_units] + [1] * (units_held - base_units)
    packed = (2 * ROWS, LANES)
    arrived = pl.pallas_call(
        functools.partial(polar_kernel, (tile_count, rep_count)),
        out_shape=jax.ShapeDtypeStruct((unit_count, lag_count) + packed, jnp.bfloat16),
        in_specs=[pl.BlockSpec(memory_space=pl.ANY)] * 3,
        out_specs=pl.BlockSpec(memory_space=pl.ANY),
        scratch_shapes=[
            pltpu.VMEM(retarded.shape[1:], jnp.bfloat16),
            pltpu.VMEM(self_energy.shape[1:], jnp.bfloat16),
            pltpu.SMEM((slot_count,), jnp.int32),
            pltpu.VMEM((rep_count, unit_count, energy_dev) + packed, jnp.bfloat16),
            pltpu.VMEM((2, slot_count) + packed, jnp.float32),
            pltpu.VMEM((units_held, 2, slot_count) + packed, jnp.bfloat16),
            pltpu.SemaphoreType.DMA((2 * energy_dev + 1,)),
            pltpu.SemaphoreType.DMA((units_held,)),
            pltpu.SemaphoreType.DMA((units_held,)),
            pltpu.SemaphoreType.DMA((units_held,)),
            pltpu.SemaphoreType.DMA((units_held,)),
            pltpu.SemaphoreType.DMA((units_held,)),
        ]
        + [
            pltpu.VMEM((2 * tile_count * rep_count, size, energy_dev) + packed, jnp.bfloat16)
            for size in group_sizes
        ],
        compiler_params=pltpu.CompilerParams(
            collective_id=0, has_side_effects=True, vmem_limit_bytes=KERNEL_BYTES
        ),
    )(retarded, self_energy, energy_of)
    return pl.pallas_call(
        unpack_kernel,
        out_shape=jax.ShapeDtypeStruct((1, lag_count, 2, row_count, block_order), jnp.float32),
        in_specs=[pl.BlockSpec(memory_space=pl.ANY)],
        out_specs=pl.BlockSpec(memory_space=pl.ANY),
        scratch_shapes=[
            pltpu.VMEM((lag_count, unit_count) + packed, jnp.bfloat16),
            pltpu.VMEM((lag_count, 2, row_count, block_order), jnp.float32),
            pltpu.SemaphoreType.DMA((lag_count,)),
            pltpu.SemaphoreType.DMA((lag_count,)),
        ],
        compiler_params=pltpu.CompilerParams(vmem_limit_bytes=KERNEL_BYTES),
    )(arrived)


def solution(mesh):
    placed = (
        P(None, ("tile", "rep"), None, None, None),
        P("comp", ("tile", "rep"), None, None, None),
        P(),
    )
    sizes = tuple(mesh.shape[name] for name in ("comp", "tile", "rep"))

    def device_body(retarded, self_energy, energy_of):
        if fits(sizes, retarded.shape[1], retarded.shape[-1]):
            return fused(sizes, retarded, self_energy, energy_of)
        return body(retarded, self_energy, energy_of)

    return jax.shard_map(
        device_body,
        mesh=mesh,
        in_specs=placed,
        out_specs=P("comp", "tile", None, "rep", None),
        check_vma=False,
    )
```

```python
import functools
import math

import jax
import jax.numpy as jnp
from jax import lax
from jax.experimental import pallas as pl
from jax.experimental.pallas import tpu as pltpu
from jax.sharding import PartitionSpec as P


def from_partner(array, axis, distance):
    return lax.ppermute(array, axis, [(i, i ^ 1 << distance) for i in range(lax.axis_size(axis))])


def batched(left_side, right_side, pattern):
    return jnp.einsum(pattern, left_side, right_side, preferred_element_type=jnp.float32)


def phase_tables(row_values, col_values, modulus):
    phase_index = row_values[:, None] * col_values[None, :] % modulus
    phase_angle = phase_index.astype(jnp.float32) * (2.0 * math.pi / modulus)
    cos_full = jnp.cos(phase_angle)
    sin_full = jnp.sin(phase_angle)
    cos_high = cos_full.astype(jnp.bfloat16)
    sin_high = sin_full.astype(jnp.bfloat16)
    cos_low = (cos_full - cos_high.astype(jnp.float32)).astype(jnp.bfloat16)
    sin_low = (sin_full - sin_high.astype(jnp.float32)).astype(jnp.bfloat16)
    return ((cos_high, cos_low), (sin_high, sin_low))


def split_dot(table_pair, values):
    return jnp.dot(table_pair[0], values, preferred_element_type=jnp.float32) + jnp.dot(
        table_pair[1], values, preferred_element_type=jnp.float32
    )


def rotate(cos_table, sin_table, value_re, value_im, direction):
    part_re = split_dot(cos_table, value_re) - direction * split_dot(sin_table, value_im)
    part_im = split_dot(cos_table, value_im) + direction * split_dot(sin_table, value_re)
    return (part_re, part_im)


def body(retarded, self_energy, energy_of):
    component = lax.axis_index("comp")
    momentum = component // 2
    greater = component % 2
    tile_count = lax.axis_size("tile")
    rep_count = lax.axis_size("rep")
    green_matrix = lax.dynamic_index_in_dim(retarded, momentum, 0, keepdims=False)
    sigma_matrix = self_energy[0]
    green_re, green_im = (green_matrix[:, 0], green_matrix[:, 1])
    sigma_re, sigma_im = (sigma_matrix[:, 0], sigma_matrix[:, 1])
    left_re = (
        batched(green_re, sigma_re, "eik,ekj->eij") - batched(green_im, sigma_im, "eik,ekj->eij")
    ).astype(jnp.bfloat16)
    left_im = (
        batched(green_re, sigma_im, "eik,ekj->eij") + batched(green_im, sigma_re, "eik,ekj->eij")
    ).astype(jnp.bfloat16)
    out_re = batched(left_re, green_re, "eik,ejk->eij") + batched(left_im, green_im, "eik,ejk->eij")
    out_im = batched(left_im, green_re, "eik,ejk->eij") - batched(left_re, green_im, "eik,ejk->eij")
    stacked = jnp.stack([out_re, out_im]).astype(jnp.bfloat16)
    stacked = jnp.where(greater == 1, jnp.swapaxes(stacked, 2, 3), stacked)
    energy_dev = stacked.shape[1]
    block_order = stacked.shape[2]
    elem_count = block_order * block_order // (tile_count * rep_count)
    slot_count = energy_of.shape[0]
    blocks = stacked.reshape(2, energy_dev, rep_count, tile_count, elem_count)
    first_pass = lax.all_to_all(blocks, "rep", split_axis=2, concat_axis=1, tiled=True)
    gathered = lax.all_to_all(first_pass, "tile", split_axis=3, concat_axis=1, tiled=True)
    signal = gathered.reshape(2, slot_count, elem_count)
    freq_count = 2 * slot_count
    frequency = lax.iota(jnp.int32, freq_count)
    fwd_cos, fwd_sin = phase_tables(frequency, energy_of, freq_count)
    own_re, own_im = rotate(fwd_cos, fwd_sin, signal[0], signal[1], -1.0)
    partner = from_partner(signal, "comp", 0)
    other_re, other_im = rotate(fwd_cos, fwd_sin, partner[0], partner[1], 1.0)
    cross_re = (own_re * other_re - own_im * other_im).astype(jnp.bfloat16)
    cross_im = (own_re * other_im + own_im * other_re).astype(jnp.bfloat16)
    lag_index = lax.iota(jnp.int32, slot_count)
    inv_cos, inv_sin = phase_tables(lag_index, frequency, freq_count)
    back_re, back_im = rotate(inv_cos, inv_sin, cross_re, cross_im, 1.0)
    norm_factor = 1.0 / (freq_count * math.sqrt(slot_count))
    polar_parts = jnp.stack([back_im * norm_factor, -back_re * norm_factor], axis=1)
    regrouped = lax.all_to_all(
        polar_parts[:, :, None, :], "tile", split_axis=0, concat_axis=2, tiled=True
    )
    lag_count = slot_count // tile_count
    return regrouped.reshape(lag_count, 2, block_order // rep_count, block_order)[None]


LANES = 128
ROWS = 8
KERNEL_BYTES = 62 * 2**20


def matmul(left_side, right_side, contract):
    return lax.dot_general(
        left_side, right_side, (((1,), (contract,)), ((), ())), preferred_element_type=jnp.float32
    )


def rotated(values):
    return pltpu.roll(values, LANES // 2, axis=1)


def polar_kernel(
    axis_sizes,
    retarded,
    self_energy,
    energy_of,
    arrived,
    green_in,
    sigma_in,
    energies,
    outgoing,
    ordered,
    lagged,
    load_sem,
    first_send,
    first_recv,
    second_send,
    second_recv,
    keep_sem,
    *gathered,
):
    tile_count, rep_count = axis_sizes
    component = lax.axis_index("comp")
    tile = lax.axis_index("tile")
    rep = lax.axis_index("rep")
    momentum = component // 2
    greater = component % 2
    energy_dev, block_order = green_in.shape[0], green_in.shape[2]
    slot_count = energies.shape[0]
    unit_count = arrived.shape[0]
    lag_count = arrived.shape[1]
    row_count = block_order // rep_count
    low_units = row_count // ROWS
    owner_count = 2 * tile_count
    peer_count = owner_count * rep_count
    base_units = unit_count // owner_count
    has_spare = unit_count % owner_count != 0

    owner = tile * 2 + greater

    def first_unit(which):
        return which * unit_count // owner_count

    def takes_spare(which):
        return first_unit(which + 1) - first_unit(which) > base_units

    half = tile_count // 2
    if tile_count % 2 == 0:
        own_half = tile // half * half
        other_half = (own_half + half) % tile_count
        tiles = [own_half + (tile + step) % half for step in range(half)]
        tiles += [other_half + (tile + step) % half for step in range(half)]
    else:
        tiles = [(tile + step) % tile_count for step in range(tile_count)]
    reps = [(rep + step) % rep_count for step in range(rep_count)]
    parts = [greater, 1 - greater]
    owners = [[tiles[i] * 2 + parts[j] for j in range(2)] for i in range(tile_count)]
    firsts = [[first_unit(owners[i][j]) for j in range(2)] for i in range(tile_count)]
    spares_at = [[takes_spare(owners[i][j]) for j in range(2)] for i in range(tile_count)]
    far_first = [(step + half) % tile_count for step in range(tile_count)]
    peers = [
        (i, j, k)
        for i in far_first
        for k in reversed(range(rep_count))
        for j in range(2)
        if (i, j, k) != (0, 0, 0)
    ]

    def device_of(i, j, k):
        return (momentum * 2 + parts[j], tiles[i], reps[k])

    loads = []
    for energy in range(energy_dev):
        loads.append(
            (
                pltpu.make_async_copy(
                    retarded.at[momentum, energy], green_in.at[energy], load_sem.at[2 * energy]
                ),
                pltpu.make_async_copy(
                    self_energy.at[0, energy], sigma_in.at[energy], load_sem.at[2 * energy + 1]
                ),
            )
        )
        for load in loads[-1]:
            load.start()
    energy_load = pltpu.make_async_copy(energy_of, energies, load_sem.at[2 * energy_dev])
    energy_load.start()

    barrier = pltpu.get_barrier_semaphore()
    for peer in peers:
        pl.semaphore_signal(
            barrier,
            inc=1,
            device_id=device_of(*peer),
            device_id_type=pl.DeviceIdType.MESH,
        )

    def finish(energy, left, right, sign):
        low, high = slice(0, LANES), slice(LANES, block_order)
        right_re, right_im = right
        with_re = jnp.concatenate(
            [right_re[low], -sign * right_im[low], right_re[high], -sign * right_im[high]]
        )
        with_im = jnp.concatenate(
            [right_im[low], sign * right_re[low], right_im[high], sign * right_re[high]]
        )
        result = matmul(left[0], with_re, 1) + matmul(left[1], with_im, 1)
        is_low = lax.broadcasted_iota(jnp.int32, (row_count // 2, LANES), 1) < LANES // 2
        for part in range(rep_count):
            rows = slice(part * row_count, (part + 1) * row_count)
            mixed = result[rows, 2 * LANES :]
            upper, lower = mixed[: row_count // 2], mixed[row_count // 2 :]
            high_re = jnp.where(is_low, upper, rotated(lower))
            high_im = jnp.where(is_low, rotated(upper), lower)
            pieces_re = jnp.concatenate([result[rows, :LANES], high_re])
            pieces_im = jnp.concatenate([result[rows, LANES : 2 * LANES], high_im])
            packed = jnp.concatenate(
                [
                    pieces_re.reshape(unit_count, ROWS, LANES),
                    pieces_im.reshape(unit_count, ROWS, LANES),
                ],
                axis=1,
            )
            outgoing[part, :, energy] = packed.astype(jnp.bfloat16)

    my_slot = greater * slot_count + (tile * rep_count + rep) * energy_dev

    def send_first(unit):
        for i, j, k in peers:
            copy = pltpu.make_async_remote_copy(
                src_ref=outgoing.at[reps[k], firsts[i][j] + unit],
                dst_ref=gathered[unit].at[pl.ds(my_slot, energy_dev)],
                send_sem=first_send.at[unit],
                recv_sem=first_recv.at[unit],
                device_id=device_of(i, j, k),
                device_id_type=pl.DeviceIdType.MESH,
            )
            if unit < base_units:
                copy.start()
            else:
                pl.when(spares_at[i][j])(copy.start)

    def keep_own(unit):
        gathered[unit][pl.ds(my_slot, energy_dev)] = outgoing[rep, firsts[0][0] + unit]

    greens, lefts = [], []
    for energy in range(energy_dev):
        for load in loads[energy]:
            load.wait()
        green_re, green_im = green_in[energy, 0], green_in[energy, 1]
        sigma_re, sigma_im = sigma_in[energy, 0], sigma_in[energy, 1]
        left_re = (matmul(green_re, sigma_re, 0) - matmul(green_im, sigma_im, 0)).astype(jnp.bfloat16)
        left_im = (matmul(green_re, sigma_im, 0) + matmul(green_im, sigma_re, 0)).astype(jnp.bfloat16)
        greens.append((green_re, green_im))
        lefts.append((left_re, left_im))

    @pl.when(greater == 0)
    def _():
        for energy in range(energy_dev):
            finish(energy, lefts[energy], greens[energy], 1)

    @pl.when(greater == 1)
    def _():
        for energy in range(energy_dev):
            finish(energy, greens[energy], lefts[energy], -1)

    pl.semaphore_wait(barrier, peer_count - 1)
    for unit in range(base_units + has_spare):
        send_first(unit)

    def wait_for(buffer, sem):
        pltpu.make_async_copy(buffer, buffer, sem).wait()

    for unit in range(base_units):
        keep_own(unit)
    if has_spare:
        pl.when(spares_at[0][0])(functools.partial(keep_own, base_units))

    energy_load.wait()
    slots = []
    for energy in range(slot_count):
        slot = 0
        for candidate in range(slot_count):
            slot = jnp.where(energies[candidate] == energy, candidate, slot)
        slots.append(slot)

    norm_factor = 1.0 / math.sqrt(slot_count)

    def keep_lags(unit):
        return pltpu.make_async_copy(
            lagged.at[unit, greater, pl.ds(tile * lag_count, lag_count)],
            arrived.at[firsts[0][0] + unit],
            keep_sem.at[unit],
        )

    def correlate(unit):
        wait_for(
            gathered[unit].at[pl.ds(0, (peer_count - 1) * energy_dev)], first_recv.at[unit]
        )
        for part in range(2):
            for energy in range(slot_count):
                ordered[part, energy] = gathered[unit][part * slot_count + slots[energy]].astype(
                    jnp.float32
                )
        for block in reversed(range(tile_count)):
            for lag in range(block * lag_count, (block + 1) * lag_count):
                for part in range(2):
                    own_re = ordered[part, lag:, :ROWS]
                    own_im = ordered[part, lag:, ROWS:]
                    other_re = ordered[1 - part, : slot_count - lag, :ROWS]
                    other_im = ordered[1 - part, : slot_count - lag, ROWS:]
                    sum_re = jnp.sum(own_re * other_re - own_im * other_im, axis=0)
                    sum_im = jnp.sum(own_re * other_im + own_im * other_re, axis=0)
                    lagged[unit, part, lag] = jnp.concatenate(
                        [sum_im * norm_factor, sum_re * -norm_factor]
                    ).astype(jnp.bfloat16)
            for part in range(2):
                copy = pltpu.make_async_remote_copy(
                    src_ref=lagged.at[unit, part, pl.ds(block * lag_count, lag_count)],
                    dst_ref=arrived.at[firsts[0][0] + unit],
                    send_sem=second_send.at[unit],
                    recv_sem=second_recv.at[unit],
                    device_id=(momentum * 2 + part, block, rep),
                    device_id_type=pl.DeviceIdType.MESH,
                )
                here = owner == block * 2 + part
                pl.when(jnp.logical_not(here))(copy.start)
                pl.when(here)(keep_lags(unit).start)

    for unit in range(base_units):
        correlate(unit)
    if has_spare:
        pl.when(spares_at[0][0])(functools.partial(correlate, base_units))

    for unit in range(base_units):
        wait_for(
            gathered[unit].at[pl.ds(0, (peer_count - 1) * energy_dev)], first_send.at[unit]
        )
        wait_for(arrived.at[pl.ds(0, owner_count - 1)], second_send.at[unit])
        wait_for(arrived.at[pl.ds(0, owner_count - 1)], second_recv.at[unit])
        keep_lags(unit).wait()
    if has_spare:
        spare_units = unit_count % owner_count
        spares = spare_units * rep_count

        @pl.when(spares_at[0][0])
        def _():
            if spares > 1:
                wait_for(
                    gathered[base_units].at[pl.ds(0, (spares - 1) * energy_dev)],
                    first_send.at[base_units],
                )
            wait_for(arrived.at[pl.ds(0, owner_count - 1)], second_send.at[base_units])
            keep_lags(base_units).wait()
            if spare_units > 1:
                wait_for(arrived.at[pl.ds(0, spare_units - 1)], second_recv.at[base_units])

        @pl.when(jnp.logical_not(spares_at[0][0]))
        def _():
            wait_for(
                gathered[base_units].at[pl.ds(0, spares * energy_dev)], first_send.at[base_units]
            )
            wait_for(arrived.at[pl.ds(0, spare_units)], second_recv.at[base_units])


def unpack_kernel(arrived, polar, packed, unpacked, load_sem, store_sem):
    unit_count, lag_count = arrived.shape[:2]
    row_count = polar.shape[3]
    low_units = row_count // ROWS
    loads = [
        pltpu.make_async_copy(arrived.at[:, lag], packed.at[lag], load_sem.at[lag])
        for lag in range(lag_count)
    ]
    stores = [
        pltpu.make_async_copy(unpacked.at[lag], polar.at[0, lag], store_sem.at[lag])
        for lag in range(lag_count)
    ]
    for load in loads:
        load.start()
    for lag in range(lag_count):
        loads[lag].wait()
        for unit in range(unit_count):
            values = packed[lag, unit].astype(jnp.float32)
            for part in range(2):
                block = values[part * ROWS : (part + 1) * ROWS]
                if unit < low_units:
                    unpacked[lag, part, unit * ROWS : (unit + 1) * ROWS, :LANES] = block
                else:
                    row = (unit - low_units) * ROWS
                    row_low = row + row_count // 2
                    unpacked[lag, part, row : row + ROWS, LANES:] = block[:, : LANES // 2]
                    unpacked[lag, part, row_low : row_low + ROWS, LANES:] = rotated(block)[
                        :, : LANES // 2
                    ]
        stores[lag].start()
    for store in stores:
        store.wait()


def fits(sizes, energy_dev, block_order):
    comp_count, tile_count, rep_count = sizes
    return (
        comp_count % 2 == 0
        and block_order == LANES + LANES // 2
        and block_order % (2 * ROWS * 2 * rep_count) == 0
        and block_order * 3 // (4 * ROWS * rep_count) >= 2 * tile_count
        and tile_count * rep_count * energy_dev <= 4 * ROWS
    )


def fused(sizes, retarded, self_energy, energy_of):
    _, tile_count, rep_count = sizes
    energy_dev, block_order = retarded.shape[1], retarded.shape[-1]
    slot_count = energy_of.shape[0]
    lag_count = slot_count // tile_count
    row_count = block_order // rep_count
    unit_count = row_count * block_order // (ROWS * LANES)
    units_held = -(-unit_count // (2 * tile_count))
    packed = (2 * ROWS, LANES)
    arrived = pl.pallas_call(
        functools.partial(polar_kernel, (tile_count, rep_count)),
        out_shape=jax.ShapeDtypeStruct((unit_count, lag_count) + packed, jnp.bfloat16),
        in_specs=[pl.BlockSpec(memory_space=pl.ANY)] * 3,
        out_specs=pl.BlockSpec(memory_space=pl.ANY),
        scratch_shapes=[
            pltpu.VMEM(retarded.shape[1:], jnp.bfloat16),
            pltpu.VMEM(self_energy.shape[1:], jnp.bfloat16),
            pltpu.SMEM((slot_count,), jnp.int32),
            pltpu.VMEM((rep_count, unit_count, energy_dev) + packed, jnp.bfloat16),
            pltpu.VMEM((2, slot_count) + packed, jnp.float32),
            pltpu.VMEM((units_held, 2, slot_count) + packed, jnp.bfloat16),
            pltpu.SemaphoreType.DMA((2 * energy_dev + 1,)),
            pltpu.SemaphoreType.DMA((units_held,)),
            pltpu.SemaphoreType.DMA((units_held,)),
            pltpu.SemaphoreType.DMA((units_held,)),
            pltpu.SemaphoreType.DMA((units_held,)),
            pltpu.SemaphoreType.DMA((units_held,)),
        ]
        + [pltpu.VMEM((2 * slot_count,) + packed, jnp.bfloat16)] * units_held,
        compiler_params=pltpu.CompilerParams(
            collective_id=0, has_side_effects=True, vmem_limit_bytes=KERNEL_BYTES
        ),
    )(retarded, self_energy, energy_of)
    return pl.pallas_call(
        unpack_kernel,
        out_shape=jax.ShapeDtypeStruct((1, lag_count, 2, row_count, block_order), jnp.float32),
        in_specs=[pl.BlockSpec(memory_space=pl.ANY)],
        out_specs=pl.BlockSpec(memory_space=pl.ANY),
        scratch_shapes=[
            pltpu.VMEM((lag_count, unit_count) + packed, jnp.bfloat16),
            pltpu.VMEM((lag_count, 2, row_count, block_order), jnp.float32),
            pltpu.SemaphoreType.DMA((lag_count,)),
            pltpu.SemaphoreType.DMA((lag_count,)),
        ],
        compiler_params=pltpu.CompilerParams(vmem_limit_bytes=KERNEL_BYTES),
    )(arrived)


def solution(mesh):
    placed = (
        P(None, ("tile", "rep"), None, None, None),
        P("comp", ("tile", "rep"), None, None, None),
        P(),
    )
    sizes = tuple(mesh.shape[name] for name in ("comp", "tile", "rep"))

    def device_body(retarded, self_energy, energy_of):
        if fits(sizes, retarded.shape[1], retarded.shape[-1]):
            return fused(sizes, retarded, self_energy, energy_of)
        return body(retarded, self_energy, energy_of)

    return jax.shard_map(
        device_body,
        mesh=mesh,
        in_specs=placed,
        out_specs=P("comp", "tile", None, "rep", None),
        check_vma=False,
    )
```

```python
import functools
import math

import jax
import jax.numpy as jnp
from jax import lax
from jax.experimental import pallas as pl
from jax.experimental.pallas import tpu as pltpu
from jax.sharding import PartitionSpec as P


def from_partner(array, axis, distance):
    return lax.ppermute(array, axis, [(i, i ^ 1 << distance) for i in range(lax.axis_size(axis))])


def batched(left_side, right_side, pattern):
    return jnp.einsum(pattern, left_side, right_side, preferred_element_type=jnp.float32)


def phase_tables(row_values, col_values, modulus):
    phase_index = row_values[:, None] * col_values[None, :] % modulus
    phase_angle = phase_index.astype(jnp.float32) * (2.0 * math.pi / modulus)
    cos_full = jnp.cos(phase_angle)
    sin_full = jnp.sin(phase_angle)
    cos_high = cos_full.astype(jnp.bfloat16)
    sin_high = sin_full.astype(jnp.bfloat16)
    cos_low = (cos_full - cos_high.astype(jnp.float32)).astype(jnp.bfloat16)
    sin_low = (sin_full - sin_high.astype(jnp.float32)).astype(jnp.bfloat16)
    return ((cos_high, cos_low), (sin_high, sin_low))


def split_dot(table_pair, values):
    return jnp.dot(table_pair[0], values, preferred_element_type=jnp.float32) + jnp.dot(
        table_pair[1], values, preferred_element_type=jnp.float32
    )


def rotate(cos_table, sin_table, value_re, value_im, direction):
    part_re = split_dot(cos_table, value_re) - direction * split_dot(sin_table, value_im)
    part_im = split_dot(cos_table, value_im) + direction * split_dot(sin_table, value_re)
    return (part_re, part_im)


def body(retarded, self_energy, energy_of):
    component = lax.axis_index("comp")
    momentum = component // 2
    greater = component % 2
    tile_count = lax.axis_size("tile")
    rep_count = lax.axis_size("rep")
    green_matrix = lax.dynamic_index_in_dim(retarded, momentum, 0, keepdims=False)
    sigma_matrix = self_energy[0]
    green_re, green_im = (green_matrix[:, 0], green_matrix[:, 1])
    sigma_re, sigma_im = (sigma_matrix[:, 0], sigma_matrix[:, 1])
    left_re = (
        batched(green_re, sigma_re, "eik,ekj->eij") - batched(green_im, sigma_im, "eik,ekj->eij")
    ).astype(jnp.bfloat16)
    left_im = (
        batched(green_re, sigma_im, "eik,ekj->eij") + batched(green_im, sigma_re, "eik,ekj->eij")
    ).astype(jnp.bfloat16)
    out_re = batched(left_re, green_re, "eik,ejk->eij") + batched(left_im, green_im, "eik,ejk->eij")
    out_im = batched(left_im, green_re, "eik,ejk->eij") - batched(left_re, green_im, "eik,ejk->eij")
    stacked = jnp.stack([out_re, out_im]).astype(jnp.bfloat16)
    stacked = jnp.where(greater == 1, jnp.swapaxes(stacked, 2, 3), stacked)
    energy_dev = stacked.shape[1]
    block_order = stacked.shape[2]
    elem_count = block_order * block_order // (tile_count * rep_count)
    slot_count = energy_of.shape[0]
    blocks = stacked.reshape(2, energy_dev, rep_count, tile_count, elem_count)
    first_pass = lax.all_to_all(blocks, "rep", split_axis=2, concat_axis=1, tiled=True)
    gathered = lax.all_to_all(first_pass, "tile", split_axis=3, concat_axis=1, tiled=True)
    signal = gathered.reshape(2, slot_count, elem_count)
    freq_count = 2 * slot_count
    frequency = lax.iota(jnp.int32, freq_count)
    fwd_cos, fwd_sin = phase_tables(frequency, energy_of, freq_count)
    own_re, own_im = rotate(fwd_cos, fwd_sin, signal[0], signal[1], -1.0)
    partner = from_partner(signal, "comp", 0)
    other_re, other_im = rotate(fwd_cos, fwd_sin, partner[0], partner[1], 1.0)
    cross_re = (own_re * other_re - own_im * other_im).astype(jnp.bfloat16)
    cross_im = (own_re * other_im + own_im * other_re).astype(jnp.bfloat16)
    lag_index = lax.iota(jnp.int32, slot_count)
    inv_cos, inv_sin = phase_tables(lag_index, frequency, freq_count)
    back_re, back_im = rotate(inv_cos, inv_sin, cross_re, cross_im, 1.0)
    norm_factor = 1.0 / (freq_count * math.sqrt(slot_count))
    polar_parts = jnp.stack([back_im * norm_factor, -back_re * norm_factor], axis=1)
    regrouped = lax.all_to_all(
        polar_parts[:, :, None, :], "tile", split_axis=0, concat_axis=2, tiled=True
    )
    lag_count = slot_count // tile_count
    return regrouped.reshape(lag_count, 2, block_order // rep_count, block_order)[None]


LANES = 128
ROWS = 8
KERNEL_BYTES = 62 * 2**20


def matmul(left_side, right_side, contract):
    return lax.dot_general(
        left_side, right_side, (((1,), (contract,)), ((), ())), preferred_element_type=jnp.float32
    )


def rotated(values):
    return pltpu.roll(values, LANES // 2, axis=1)


def polar_kernel(
    axis_sizes,
    retarded,
    self_energy,
    energy_of,
    arrived,
    green_in,
    sigma_in,
    energies,
    outgoing,
    ordered,
    lagged,
    load_sem,
    first_send,
    first_recv,
    second_send,
    second_recv,
    keep_sem,
    *gathered,
):
    tile_count, rep_count = axis_sizes
    component = lax.axis_index("comp")
    tile = lax.axis_index("tile")
    rep = lax.axis_index("rep")
    momentum = component // 2
    greater = component % 2
    energy_dev, block_order = green_in.shape[0], green_in.shape[2]
    slot_count = energies.shape[0]
    unit_count = arrived.shape[0]
    lag_count = arrived.shape[1]
    row_count = block_order // rep_count
    low_units = row_count // ROWS
    owner_count = 2 * tile_count
    peer_count = owner_count * rep_count
    base_units = unit_count // owner_count
    has_spare = unit_count % owner_count != 0

    owner = tile * 2 + greater

    def first_unit(which):
        return which * unit_count // owner_count

    def takes_spare(which):
        return first_unit(which + 1) - first_unit(which) > base_units

    half = tile_count // 2
    if tile_count % 2 == 0:
        own_half = tile // half * half
        other_half = (own_half + half) % tile_count
        tiles = [own_half + (tile + step) % half for step in range(half)]
        tiles += [other_half + (tile + step) % half for step in range(half)]
    else:
        tiles = [(tile + step) % tile_count for step in range(tile_count)]
    reps = [(rep + step) % rep_count for step in range(rep_count)]
    parts = [greater, 1 - greater]
    owners = [[tiles[i] * 2 + parts[j] for j in range(2)] for i in range(tile_count)]
    firsts = [[first_unit(owners[i][j]) for j in range(2)] for i in range(tile_count)]
    spares_at = [[takes_spare(owners[i][j]) for j in range(2)] for i in range(tile_count)]
    far_first = [(step + half) % tile_count for step in range(tile_count)]
    near_owners = [(i, j) for i in far_first for j in range(2) if (i, j) != (0, 0)]
    peers = [
        (i, j, k)
        for i in far_first
        for k in reversed(range(rep_count))
        for j in range(2)
        if (i, j, k) != (0, 0, 0)
    ]

    def device_of(i, j, k):
        return (momentum * 2 + parts[j], tiles[i], reps[k])

    loads = []
    for energy in range(energy_dev):
        loads.append(
            (
                pltpu.make_async_copy(
                    retarded.at[momentum, energy], green_in.at[energy], load_sem.at[2 * energy]
                ),
                pltpu.make_async_copy(
                    self_energy.at[0, energy], sigma_in.at[energy], load_sem.at[2 * energy + 1]
                ),
            )
        )
        for load in loads[-1]:
            load.start()
    energy_load = pltpu.make_async_copy(energy_of, energies, load_sem.at[2 * energy_dev])
    energy_load.start()

    barrier = pltpu.get_barrier_semaphore()
    for peer in peers:
        pl.semaphore_signal(
            barrier,
            inc=1,
            device_id=device_of(*peer),
            device_id_type=pl.DeviceIdType.MESH,
        )

    def finish(energy, left, right, sign):
        low, high = slice(0, LANES), slice(LANES, block_order)
        right_re, right_im = right
        with_re = jnp.concatenate(
            [right_re[low], -sign * right_im[low], right_re[high], -sign * right_im[high]]
        )
        with_im = jnp.concatenate(
            [right_im[low], sign * right_re[low], right_im[high], sign * right_re[high]]
        )
        result = matmul(left[0], with_re, 1) + matmul(left[1], with_im, 1)
        is_low = lax.broadcasted_iota(jnp.int32, (row_count // 2, LANES), 1) < LANES // 2
        for part in range(rep_count):
            rows = slice(part * row_count, (part + 1) * row_count)
            mixed = result[rows, 2 * LANES :]
            upper, lower = mixed[: row_count // 2], mixed[row_count // 2 :]
            high_re = jnp.where(is_low, upper, rotated(lower))
            high_im = jnp.where(is_low, rotated(upper), lower)
            pieces_re = jnp.concatenate([result[rows, :LANES], high_re])
            pieces_im = jnp.concatenate([result[rows, LANES : 2 * LANES], high_im])
            packed = jnp.concatenate(
                [
                    pieces_re.reshape(unit_count, ROWS, LANES),
                    pieces_im.reshape(unit_count, ROWS, LANES),
                ],
                axis=1,
            )
            outgoing[part, :, energy] = packed.astype(jnp.bfloat16)

    my_slot = greater * slot_count + (tile * rep_count + rep) * energy_dev

    def send_first(unit):
        for i, j, k in peers:
            copy = pltpu.make_async_remote_copy(
                src_ref=outgoing.at[reps[k], firsts[i][j] + unit],
                dst_ref=gathered[unit].at[pl.ds(my_slot, energy_dev)],
                send_sem=first_send.at[unit],
                recv_sem=first_recv.at[unit],
                device_id=device_of(i, j, k),
                device_id_type=pl.DeviceIdType.MESH,
            )
            if unit < base_units:
                copy.start()
            else:
                pl.when(spares_at[i][j])(copy.start)

    def keep_own(unit):
        gathered[unit][pl.ds(my_slot, energy_dev)] = outgoing[rep, firsts[0][0] + unit]

    greens, lefts = [], []
    for energy in range(energy_dev):
        for load in loads[energy]:
            load.wait()
        green_re, green_im = green_in[energy, 0], green_in[energy, 1]
        sigma_re, sigma_im = sigma_in[energy, 0], sigma_in[energy, 1]
        left_re = (matmul(green_re, sigma_re, 0) - matmul(green_im, sigma_im, 0)).astype(jnp.bfloat16)
        left_im = (matmul(green_re, sigma_im, 0) + matmul(green_im, sigma_re, 0)).astype(jnp.bfloat16)
        greens.append((green_re, green_im))
        lefts.append((left_re, left_im))

    @pl.when(greater == 0)
    def _():
        for energy in range(energy_dev):
            finish(energy, lefts[energy], greens[energy], 1)

    @pl.when(greater == 1)
    def _():
        for energy in range(energy_dev):
            finish(energy, greens[energy], lefts[energy], -1)

    pl.semaphore_wait(barrier, peer_count - 1)
    for unit in range(base_units + has_spare):
        send_first(unit)

    def wait_for(buffer, sem):
        pltpu.make_async_copy(buffer, buffer, sem).wait()

    for unit in range(base_units):
        keep_own(unit)
    if has_spare:
        pl.when(spares_at[0][0])(functools.partial(keep_own, base_units))

    energy_load.wait()
    slots = []
    for energy in range(slot_count):
        slot = 0
        for candidate in range(slot_count):
            slot = jnp.where(energies[candidate] == energy, candidate, slot)
        slots.append(slot)

    norm_factor = 1.0 / math.sqrt(slot_count)

    def keep_lags(unit):
        return pltpu.make_async_copy(
            lagged.at[unit, greater, pl.ds(tile * lag_count, lag_count)],
            arrived.at[firsts[0][0] + unit],
            keep_sem.at[unit],
        )

    def correlate(unit):
        wait_for(
            gathered[unit].at[pl.ds(0, (peer_count - 1) * energy_dev)], first_recv.at[unit]
        )
        for part in range(2):
            for energy in range(slot_count):
                ordered[part, energy] = gathered[unit][part * slot_count + slots[energy]].astype(
                    jnp.float32
                )
        for lag in range(slot_count):
            for part in range(2):
                own_re = ordered[part, lag:, :ROWS]
                own_im = ordered[part, lag:, ROWS:]
                other_re = ordered[1 - part, : slot_count - lag, :ROWS]
                other_im = ordered[1 - part, : slot_count - lag, ROWS:]
                sum_re = jnp.sum(own_re * other_re - own_im * other_im, axis=0)
                sum_im = jnp.sum(own_re * other_im + own_im * other_re, axis=0)
                lagged[unit, part, lag] = jnp.concatenate(
                    [sum_im * norm_factor, sum_re * -norm_factor]
                ).astype(jnp.bfloat16)
        my_unit = firsts[0][0] + unit
        for i, j in near_owners:
            pltpu.make_async_remote_copy(
                src_ref=lagged.at[unit, parts[j], pl.ds(tiles[i] * lag_count, lag_count)],
                dst_ref=arrived.at[my_unit],
                send_sem=second_send.at[unit],
                recv_sem=second_recv.at[unit],
                device_id=device_of(i, j, 0),
                device_id_type=pl.DeviceIdType.MESH,
            ).start()
        keep_lags(unit).start()

    for unit in range(base_units):
        correlate(unit)
    if has_spare:
        pl.when(spares_at[0][0])(functools.partial(correlate, base_units))

    for unit in range(base_units):
        wait_for(
            gathered[unit].at[pl.ds(0, (peer_count - 1) * energy_dev)], first_send.at[unit]
        )
        wait_for(arrived.at[pl.ds(0, owner_count - 1)], second_send.at[unit])
        wait_for(arrived.at[pl.ds(0, owner_count - 1)], second_recv.at[unit])
        keep_lags(unit).wait()
    if has_spare:
        spare_units = unit_count % owner_count
        spares = spare_units * rep_count

        @pl.when(spares_at[0][0])
        def _():
            if spares > 1:
                wait_for(
                    gathered[base_units].at[pl.ds(0, (spares - 1) * energy_dev)],
                    first_send.at[base_units],
                )
            wait_for(arrived.at[pl.ds(0, owner_count - 1)], second_send.at[base_units])
            keep_lags(base_units).wait()
            if spare_units > 1:
                wait_for(arrived.at[pl.ds(0, spare_units - 1)], second_recv.at[base_units])

        @pl.when(jnp.logical_not(spares_at[0][0]))
        def _():
            wait_for(
                gathered[base_units].at[pl.ds(0, spares * energy_dev)], first_send.at[base_units]
            )
            wait_for(arrived.at[pl.ds(0, spare_units)], second_recv.at[base_units])


def unpack_kernel(arrived, polar, packed, unpacked, load_sem, store_sem):
    unit_count, lag_count = arrived.shape[:2]
    row_count = polar.shape[3]
    low_units = row_count // ROWS
    loads = [
        pltpu.make_async_copy(arrived.at[:, lag], packed.at[lag], load_sem.at[lag])
        for lag in range(lag_count)
    ]
    stores = [
        pltpu.make_async_copy(unpacked.at[lag], polar.at[0, lag], store_sem.at[lag])
        for lag in range(lag_count)
    ]
    for load in loads:
        load.start()
    for lag in range(lag_count):
        loads[lag].wait()
        for unit in range(unit_count):
            values = packed[lag, unit].astype(jnp.float32)
            for part in range(2):
                block = values[part * ROWS : (part + 1) * ROWS]
                if unit < low_units:
                    unpacked[lag, part, unit * ROWS : (unit + 1) * ROWS, :LANES] = block
                else:
                    row = (unit - low_units) * ROWS
                    row_low = row + row_count // 2
                    unpacked[lag, part, row : row + ROWS, LANES:] = block[:, : LANES // 2]
                    unpacked[lag, part, row_low : row_low + ROWS, LANES:] = rotated(block)[
                        :, : LANES // 2
                    ]
        stores[lag].start()
    for store in stores:
        store.wait()


def fits(sizes, energy_dev, block_order):
    comp_count, tile_count, rep_count = sizes
    return (
        comp_count % 2 == 0
        and block_order == LANES + LANES // 2
        and block_order % (2 * ROWS * 2 * rep_count) == 0
        and block_order * 3 // (4 * ROWS * rep_count) >= 2 * tile_count
        and tile_count * rep_count * energy_dev <= 4 * ROWS
    )


def fused(sizes, retarded, self_energy, energy_of):
    _, tile_count, rep_count = sizes
    energy_dev, block_order = retarded.shape[1], retarded.shape[-1]
    slot_count = energy_of.shape[0]
    lag_count = slot_count // tile_count
    row_count = block_order // rep_count
    unit_count = row_count * block_order // (ROWS * LANES)
    units_held = -(-unit_count // (2 * tile_count))
    packed = (2 * ROWS, LANES)
    arrived = pl.pallas_call(
        functools.partial(polar_kernel, (tile_count, rep_count)),
        out_shape=jax.ShapeDtypeStruct((unit_count, lag_count) + packed, jnp.bfloat16),
        in_specs=[pl.BlockSpec(memory_space=pl.ANY)] * 3,
        out_specs=pl.BlockSpec(memory_space=pl.ANY),
        scratch_shapes=[
            pltpu.VMEM(retarded.shape[1:], jnp.bfloat16),
            pltpu.VMEM(self_energy.shape[1:], jnp.bfloat16),
            pltpu.SMEM((slot_count,), jnp.int32),
            pltpu.VMEM((rep_count, unit_count, energy_dev) + packed, jnp.bfloat16),
            pltpu.VMEM((2, slot_count) + packed, jnp.float32),
            pltpu.VMEM((units_held, 2, slot_count) + packed, jnp.bfloat16),
            pltpu.SemaphoreType.DMA((2 * energy_dev + 1,)),
            pltpu.SemaphoreType.DMA((units_held,)),
            pltpu.SemaphoreType.DMA((units_held,)),
            pltpu.SemaphoreType.DMA((units_held,)),
            pltpu.SemaphoreType.DMA((units_held,)),
            pltpu.SemaphoreType.DMA((units_held,)),
        ]
        + [pltpu.VMEM((2 * slot_count,) + packed, jnp.bfloat16)] * units_held,
        compiler_params=pltpu.CompilerParams(
            collective_id=0, has_side_effects=True, vmem_limit_bytes=KERNEL_BYTES
        ),
    )(retarded, self_energy, energy_of)
    return pl.pallas_call(
        unpack_kernel,
        out_shape=jax.ShapeDtypeStruct((1, lag_count, 2, row_count, block_order), jnp.float32),
        in_specs=[pl.BlockSpec(memory_space=pl.ANY)],
        out_specs=pl.BlockSpec(memory_space=pl.ANY),
        scratch_shapes=[
            pltpu.VMEM((lag_count, unit_count) + packed, jnp.bfloat16),
            pltpu.VMEM((lag_count, 2, row_count, block_order), jnp.float32),
            pltpu.SemaphoreType.DMA((lag_count,)),
            pltpu.SemaphoreType.DMA((lag_count,)),
        ],
        compiler_params=pltpu.CompilerParams(vmem_limit_bytes=KERNEL_BYTES),
    )(arrived)


def solution(mesh):
    placed = (
        P(None, ("tile", "rep"), None, None, None),
        P("comp", ("tile", "rep"), None, None, None),
        P(),
    )
    sizes = tuple(mesh.shape[name] for name in ("comp", "tile", "rep"))

    def device_body(retarded, self_energy, energy_of):
        if fits(sizes, retarded.shape[1], retarded.shape[-1]):
            return fused(sizes, retarded, self_energy, energy_of)
        return body(retarded, self_energy, energy_of)

    return jax.shard_map(
        device_body,
        mesh=mesh,
        in_specs=placed,
        out_specs=P("comp", "tile", None, "rep", None),
        check_vma=False,
    )
```

```python
import functools
import math

import jax
import jax.numpy as jnp
from jax import lax
from jax.experimental import pallas as pl
from jax.experimental.pallas import tpu as pltpu
from jax.sharding import PartitionSpec as P


def from_partner(array, axis, distance):
    return lax.ppermute(array, axis, [(i, i ^ 1 << distance) for i in range(lax.axis_size(axis))])


def batched(left_side, right_side, pattern):
    return jnp.einsum(pattern, left_side, right_side, preferred_element_type=jnp.float32)


def phase_tables(row_values, col_values, modulus):
    phase_index = row_values[:, None] * col_values[None, :] % modulus
    phase_angle = phase_index.astype(jnp.float32) * (2.0 * math.pi / modulus)
    cos_full = jnp.cos(phase_angle)
    sin_full = jnp.sin(phase_angle)
    cos_high = cos_full.astype(jnp.bfloat16)
    sin_high = sin_full.astype(jnp.bfloat16)
    cos_low = (cos_full - cos_high.astype(jnp.float32)).astype(jnp.bfloat16)
    sin_low = (sin_full - sin_high.astype(jnp.float32)).astype(jnp.bfloat16)
    return ((cos_high, cos_low), (sin_high, sin_low))


def split_dot(table_pair, values):
    return jnp.dot(table_pair[0], values, preferred_element_type=jnp.float32) + jnp.dot(
        table_pair[1], values, preferred_element_type=jnp.float32
    )


def rotate(cos_table, sin_table, value_re, value_im, direction):
    part_re = split_dot(cos_table, value_re) - direction * split_dot(sin_table, value_im)
    part_im = split_dot(cos_table, value_im) + direction * split_dot(sin_table, value_re)
    return (part_re, part_im)


def body(retarded, self_energy, energy_of):
    component = lax.axis_index("comp")
    momentum = component // 2
    greater = component % 2
    tile_count = lax.axis_size("tile")
    rep_count = lax.axis_size("rep")
    green_matrix = lax.dynamic_index_in_dim(retarded, momentum, 0, keepdims=False)
    sigma_matrix = self_energy[0]
    green_re, green_im = (green_matrix[:, 0], green_matrix[:, 1])
    sigma_re, sigma_im = (sigma_matrix[:, 0], sigma_matrix[:, 1])
    left_re = (
        batched(green_re, sigma_re, "eik,ekj->eij") - batched(green_im, sigma_im, "eik,ekj->eij")
    ).astype(jnp.bfloat16)
    left_im = (
        batched(green_re, sigma_im, "eik,ekj->eij") + batched(green_im, sigma_re, "eik,ekj->eij")
    ).astype(jnp.bfloat16)
    out_re = batched(left_re, green_re, "eik,ejk->eij") + batched(left_im, green_im, "eik,ejk->eij")
    out_im = batched(left_im, green_re, "eik,ejk->eij") - batched(left_re, green_im, "eik,ejk->eij")
    stacked = jnp.stack([out_re, out_im]).astype(jnp.bfloat16)
    stacked = jnp.where(greater == 1, jnp.swapaxes(stacked, 2, 3), stacked)
    energy_dev = stacked.shape[1]
    block_order = stacked.shape[2]
    elem_count = block_order * block_order // (tile_count * rep_count)
    slot_count = energy_of.shape[0]
    blocks = stacked.reshape(2, energy_dev, rep_count, tile_count, elem_count)
    first_pass = lax.all_to_all(blocks, "rep", split_axis=2, concat_axis=1, tiled=True)
    gathered = lax.all_to_all(first_pass, "tile", split_axis=3, concat_axis=1, tiled=True)
    signal = gathered.reshape(2, slot_count, elem_count)
    freq_count = 2 * slot_count
    frequency = lax.iota(jnp.int32, freq_count)
    fwd_cos, fwd_sin = phase_tables(frequency, energy_of, freq_count)
    own_re, own_im = rotate(fwd_cos, fwd_sin, signal[0], signal[1], -1.0)
    partner = from_partner(signal, "comp", 0)
    other_re, other_im = rotate(fwd_cos, fwd_sin, partner[0], partner[1], 1.0)
    cross_re = (own_re * other_re - own_im * other_im).astype(jnp.bfloat16)
    cross_im = (own_re * other_im + own_im * other_re).astype(jnp.bfloat16)
    lag_index = lax.iota(jnp.int32, slot_count)
    inv_cos, inv_sin = phase_tables(lag_index, frequency, freq_count)
    back_re, back_im = rotate(inv_cos, inv_sin, cross_re, cross_im, 1.0)
    norm_factor = 1.0 / (freq_count * math.sqrt(slot_count))
    polar_parts = jnp.stack([back_im * norm_factor, -back_re * norm_factor], axis=1)
    regrouped = lax.all_to_all(
        polar_parts[:, :, None, :], "tile", split_axis=0, concat_axis=2, tiled=True
    )
    lag_count = slot_count // tile_count
    return regrouped.reshape(lag_count, 2, block_order // rep_count, block_order)[None]


LANES = 128
ROWS = 8
KERNEL_BYTES = 62 * 2**20


def matmul(left_side, right_side, contract):
    return lax.dot_general(
        left_side, right_side, (((1,), (contract,)), ((), ())), preferred_element_type=jnp.float32
    )


def rotated(values):
    return pltpu.roll(values, LANES // 2, axis=1)


def polar_kernel(
    axis_sizes,
    retarded,
    self_energy,
    energy_of,
    arrived,
    green_in,
    sigma_in,
    energies,
    outgoing,
    ordered,
    lagged,
    load_sem,
    first_send,
    first_recv,
    second_send,
    second_recv,
    keep_sem,
    *gathered,
):
    tile_count, rep_count = axis_sizes
    component = lax.axis_index("comp")
    tile = lax.axis_index("tile")
    rep = lax.axis_index("rep")
    momentum = component // 2
    greater = component % 2
    energy_dev, block_order = green_in.shape[0], green_in.shape[2]
    slot_count = energies.shape[0]
    unit_count = arrived.shape[0]
    lag_count = arrived.shape[1]
    row_count = block_order // rep_count
    low_units = row_count // ROWS
    owner_count = 2 * tile_count
    peer_count = owner_count * rep_count
    base_units = unit_count // owner_count
    has_spare = unit_count % owner_count != 0

    owner = tile * 2 + greater

    def first_unit(which):
        return which * unit_count // owner_count

    def takes_spare(which):
        return first_unit(which + 1) - first_unit(which) > base_units

    half = tile_count // 2
    if tile_count % 2 == 0:
        own_half = tile // half * half
        other_half = (own_half + half) % tile_count
        tiles = [own_half + (tile + step) % half for step in range(half)]
        tiles += [other_half + (tile + step) % half for step in range(half)]
    else:
        tiles = [(tile + step) % tile_count for step in range(tile_count)]
    reps = [(rep + step) % rep_count for step in range(rep_count)]
    parts = [greater, 1 - greater]
    owners = [[tiles[i] * 2 + parts[j] for j in range(2)] for i in range(tile_count)]
    firsts = [[first_unit(owners[i][j]) for j in range(2)] for i in range(tile_count)]
    spares_at = [[takes_spare(owners[i][j]) for j in range(2)] for i in range(tile_count)]
    far_first = [(step + half) % tile_count for step in range(tile_count)]
    near_owners = [(i, j) for i in far_first for j in range(2) if (i, j) != (0, 0)]
    peers = [
        (i, j, k)
        for i in far_first
        for k in reversed(range(rep_count))
        for j in range(2)
        if (i, j, k) != (0, 0, 0)
    ]

    def device_of(i, j, k):
        return (momentum * 2 + parts[j], tiles[i], reps[k])

    loads = []
    for energy in range(energy_dev):
        loads.append(
            (
                pltpu.make_async_copy(
                    retarded.at[momentum, energy], green_in.at[energy], load_sem.at[2 * energy]
                ),
                pltpu.make_async_copy(
                    self_energy.at[0, energy], sigma_in.at[energy], load_sem.at[2 * energy + 1]
                ),
            )
        )
        for load in loads[-1]:
            load.start()
    energy_load = pltpu.make_async_copy(energy_of, energies, load_sem.at[2 * energy_dev])
    energy_load.start()

    barrier = pltpu.get_barrier_semaphore()
    for peer in peers:
        pl.semaphore_signal(
            barrier,
            inc=1,
            device_id=device_of(*peer),
            device_id_type=pl.DeviceIdType.MESH,
        )

    def finish(energy, left, right, sign):
        low, high = slice(0, LANES), slice(LANES, block_order)
        right_re, right_im = right
        with_re = jnp.concatenate(
            [right_re[low], -sign * right_im[low], right_re[high], -sign * right_im[high]]
        )
        with_im = jnp.concatenate(
            [right_im[low], sign * right_re[low], right_im[high], sign * right_re[high]]
        )
        result = matmul(left[0], with_re, 1) + matmul(left[1], with_im, 1)
        is_low = lax.broadcasted_iota(jnp.int32, (row_count // 2, LANES), 1) < LANES // 2
        for part in range(rep_count):
            rows = slice(part * row_count, (part + 1) * row_count)
            mixed = result[rows, 2 * LANES :]
            upper, lower = mixed[: row_count // 2], mixed[row_count // 2 :]
            high_re = jnp.where(is_low, upper, rotated(lower))
            high_im = jnp.where(is_low, rotated(upper), lower)
            pieces_re = jnp.concatenate([result[rows, :LANES], high_re])
            pieces_im = jnp.concatenate([result[rows, LANES : 2 * LANES], high_im])
            packed = jnp.concatenate(
                [
                    pieces_re.reshape(unit_count, ROWS, LANES),
                    pieces_im.reshape(unit_count, ROWS, LANES),
                ],
                axis=1,
            )
            outgoing[part, :, energy] = packed.astype(jnp.bfloat16)

    my_slot = greater * slot_count + (tile * rep_count + rep) * energy_dev

    def send_first(unit):
        for i, j, k in peers:
            copy = pltpu.make_async_remote_copy(
                src_ref=outgoing.at[reps[k], firsts[i][j] + unit],
                dst_ref=gathered[unit].at[pl.ds(my_slot, energy_dev)],
                send_sem=first_send.at[unit],
                recv_sem=first_recv.at[unit],
                device_id=device_of(i, j, k),
                device_id_type=pl.DeviceIdType.MESH,
            )
            if unit < base_units:
                copy.start()
            else:
                pl.when(spares_at[i][j])(copy.start)

    def keep_own(unit):
        gathered[unit][pl.ds(my_slot, energy_dev)] = outgoing[rep, firsts[0][0] + unit]

    for energy in range(energy_dev):
        for load in loads[energy]:
            load.wait()
        green_re, green_im = green_in[energy, 0], green_in[energy, 1]
        sigma_re, sigma_im = sigma_in[energy, 0], sigma_in[energy, 1]
        left_re = (matmul(green_re, sigma_re, 0) - matmul(green_im, sigma_im, 0)).astype(jnp.bfloat16)
        left_im = (matmul(green_re, sigma_im, 0) + matmul(green_im, sigma_re, 0)).astype(jnp.bfloat16)

        @pl.when(greater == 0)
        def _():
            finish(energy, (left_re, left_im), (green_re, green_im), 1)

        @pl.when(greater == 1)
        def _():
            finish(energy, (green_re, green_im), (left_re, left_im), -1)

    pl.semaphore_wait(barrier, peer_count - 1)
    unit_order = [0] + [base_units] * has_spare + list(range(1, base_units))
    for unit in unit_order:
        send_first(unit)

    def wait_for(buffer, sem):
        pltpu.make_async_copy(buffer, buffer, sem).wait()

    for unit in range(base_units):
        keep_own(unit)
    if has_spare:
        pl.when(spares_at[0][0])(functools.partial(keep_own, base_units))

    energy_load.wait()
    slots = []
    for energy in range(slot_count):
        slot = 0
        for candidate in range(slot_count):
            slot = jnp.where(energies[candidate] == energy, candidate, slot)
        slots.append(slot)

    norm_factor = 1.0 / math.sqrt(slot_count)

    def keep_lags(unit):
        return pltpu.make_async_copy(
            lagged.at[unit, greater, pl.ds(tile * lag_count, lag_count)],
            arrived.at[firsts[0][0] + unit],
            keep_sem.at[unit],
        )

    def correlate(unit):
        wait_for(
            gathered[unit].at[pl.ds(0, (peer_count - 1) * energy_dev)], first_recv.at[unit]
        )
        for part in range(2):
            for energy in range(slot_count):
                ordered[part, energy] = gathered[unit][part * slot_count + slots[energy]].astype(
                    jnp.float32
                )
        for lag in range(slot_count):
            for part in range(2):
                own_re = ordered[part, lag:, :ROWS]
                own_im = ordered[part, lag:, ROWS:]
                other_re = ordered[1 - part, : slot_count - lag, :ROWS]
                other_im = ordered[1 - part, : slot_count - lag, ROWS:]
                sum_re = jnp.sum(own_re * other_re - own_im * other_im, axis=0)
                sum_im = jnp.sum(own_re * other_im + own_im * other_re, axis=0)
                lagged[unit, part, lag] = jnp.concatenate(
                    [sum_im * norm_factor, sum_re * -norm_factor]
                ).astype(jnp.bfloat16)
        my_unit = firsts[0][0] + unit
        for i, j in near_owners:
            pltpu.make_async_remote_copy(
                src_ref=lagged.at[unit, parts[j], pl.ds(tiles[i] * lag_count, lag_count)],
                dst_ref=arrived.at[my_unit],
                send_sem=second_send.at[unit],
                recv_sem=second_recv.at[unit],
                device_id=device_of(i, j, 0),
                device_id_type=pl.DeviceIdType.MESH,
            ).start()
        keep_lags(unit).start()

    for unit in unit_order:
        if unit < base_units:
            correlate(unit)
        else:
            pl.when(spares_at[0][0])(functools.partial(correlate, unit))

    for unit in range(base_units):
        wait_for(
            gathered[unit].at[pl.ds(0, (peer_count - 1) * energy_dev)], first_send.at[unit]
        )
        wait_for(arrived.at[pl.ds(0, owner_count - 1)], second_send.at[unit])
        wait_for(arrived.at[pl.ds(0, owner_count - 1)], second_recv.at[unit])
        keep_lags(unit).wait()
    if has_spare:
        spare_units = unit_count % owner_count
        spares = spare_units * rep_count

        @pl.when(spares_at[0][0])
        def _():
            if spares > 1:
                wait_for(
                    gathered[base_units].at[pl.ds(0, (spares - 1) * energy_dev)],
                    first_send.at[base_units],
                )
            wait_for(arrived.at[pl.ds(0, owner_count - 1)], second_send.at[base_units])
            keep_lags(base_units).wait()
            if spare_units > 1:
                wait_for(arrived.at[pl.ds(0, spare_units - 1)], second_recv.at[base_units])

        @pl.when(jnp.logical_not(spares_at[0][0]))
        def _():
            wait_for(
                gathered[base_units].at[pl.ds(0, spares * energy_dev)], first_send.at[base_units]
            )
            wait_for(arrived.at[pl.ds(0, spare_units)], second_recv.at[base_units])


def unpack_kernel(arrived, polar, packed, unpacked, load_sem, store_sem):
    unit_count, lag_count = arrived.shape[:2]
    row_count = polar.shape[3]
    low_units = row_count // ROWS
    load = pltpu.make_async_copy(arrived, packed, load_sem)
    stores = [
        pltpu.make_async_copy(unpacked.at[lag], polar.at[0, lag], store_sem.at[lag])
        for lag in range(lag_count)
    ]
    load.start()
    load.wait()
    for lag in range(lag_count):
        for unit in range(unit_count):
            values = packed[unit, lag].astype(jnp.float32)
            for part in range(2):
                block = values[part * ROWS : (part + 1) * ROWS]
                if unit < low_units:
                    unpacked[lag, part, unit * ROWS : (unit + 1) * ROWS, :LANES] = block
                else:
                    row = (unit - low_units) * ROWS
                    row_low = row + row_count // 2
                    unpacked[lag, part, row : row + ROWS, LANES:] = block[:, : LANES // 2]
                    unpacked[lag, part, row_low : row_low + ROWS, LANES:] = rotated(block)[
                        :, : LANES // 2
                    ]
        stores[lag].start()
    for store in stores:
        store.wait()


def fits(sizes, energy_dev, block_order):
    comp_count, tile_count, rep_count = sizes
    return (
        comp_count % 2 == 0
        and block_order == LANES + LANES // 2
        and block_order % (2 * ROWS * 2 * rep_count) == 0
        and block_order * 3 // (4 * ROWS * rep_count) >= 2 * tile_count
        and tile_count * rep_count * energy_dev <= 4 * ROWS
    )


def fused(sizes, retarded, self_energy, energy_of):
    _, tile_count, rep_count = sizes
    energy_dev, block_order = retarded.shape[1], retarded.shape[-1]
    slot_count = energy_of.shape[0]
    lag_count = slot_count // tile_count
    row_count = block_order // rep_count
    unit_count = row_count * block_order // (ROWS * LANES)
    units_held = -(-unit_count // (2 * tile_count))
    packed = (2 * ROWS, LANES)
    arrived = pl.pallas_call(
        functools.partial(polar_kernel, (tile_count, rep_count)),
        out_shape=jax.ShapeDtypeStruct((unit_count, lag_count) + packed, jnp.bfloat16),
        in_specs=[pl.BlockSpec(memory_space=pl.ANY)] * 3,
        out_specs=pl.BlockSpec(memory_space=pl.ANY),
        scratch_shapes=[
            pltpu.VMEM(retarded.shape[1:], jnp.bfloat16),
            pltpu.VMEM(self_energy.shape[1:], jnp.bfloat16),
            pltpu.SMEM((slot_count,), jnp.int32),
            pltpu.VMEM((rep_count, unit_count, energy_dev) + packed, jnp.bfloat16),
            pltpu.VMEM((2, slot_count) + packed, jnp.float32),
            pltpu.VMEM((units_held, 2, slot_count) + packed, jnp.bfloat16),
            pltpu.SemaphoreType.DMA((2 * energy_dev + 1,)),
            pltpu.SemaphoreType.DMA((units_held,)),
            pltpu.SemaphoreType.DMA((units_held,)),
            pltpu.SemaphoreType.DMA((units_held,)),
            pltpu.SemaphoreType.DMA((units_held,)),
            pltpu.SemaphoreType.DMA((units_held,)),
        ]
        + [pltpu.VMEM((2 * slot_count,) + packed, jnp.bfloat16)] * units_held,
        compiler_params=pltpu.CompilerParams(
            collective_id=0, has_side_effects=True, vmem_limit_bytes=KERNEL_BYTES
        ),
    )(retarded, self_energy, energy_of)
    return pl.pallas_call(
        unpack_kernel,
        out_shape=jax.ShapeDtypeStruct((1, lag_count, 2, row_count, block_order), jnp.float32),
        in_specs=[pl.BlockSpec(memory_space=pl.ANY)],
        out_specs=pl.BlockSpec(memory_space=pl.ANY),
        scratch_shapes=[
            pltpu.VMEM((unit_count, lag_count) + packed, jnp.bfloat16),
            pltpu.VMEM((lag_count, 2, row_count, block_order), jnp.float32),
            pltpu.SemaphoreType.DMA,
            pltpu.SemaphoreType.DMA((lag_count,)),
        ],
        compiler_params=pltpu.CompilerParams(vmem_limit_bytes=KERNEL_BYTES),
    )(arrived)


def solution(mesh):
    placed = (
        P(None, ("tile", "rep"), None, None, None),
        P("comp", ("tile", "rep"), None, None, None),
        P(),
    )
    sizes = tuple(mesh.shape[name] for name in ("comp", "tile", "rep"))

    def device_body(retarded, self_energy, energy_of):
        if fits(sizes, retarded.shape[1], retarded.shape[-1]):
            return fused(sizes, retarded, self_energy, energy_of)
        return body(retarded, self_energy, energy_of)

    return jax.shard_map(
        device_body,
        mesh=mesh,
        in_specs=placed,
        out_specs=P("comp", "tile", None, "rep", None),
        check_vma=False,
    )
```

```python
import functools
import math

import jax
import jax.numpy as jnp
from jax import lax
from jax.experimental import pallas as pl
from jax.experimental.pallas import tpu as pltpu
from jax.sharding import PartitionSpec as P


def from_partner(array, axis, distance):
    return lax.ppermute(array, axis, [(i, i ^ 1 << distance) for i in range(lax.axis_size(axis))])


def batched(left_side, right_side, pattern):
    return jnp.einsum(pattern, left_side, right_side, preferred_element_type=jnp.float32)


def phase_tables(row_values, col_values, modulus):
    phase_index = row_values[:, None] * col_values[None, :] % modulus
    phase_angle = phase_index.astype(jnp.float32) * (2.0 * math.pi / modulus)
    cos_full = jnp.cos(phase_angle)
    sin_full = jnp.sin(phase_angle)
    cos_high = cos_full.astype(jnp.bfloat16)
    sin_high = sin_full.astype(jnp.bfloat16)
    cos_low = (cos_full - cos_high.astype(jnp.float32)).astype(jnp.bfloat16)
    sin_low = (sin_full - sin_high.astype(jnp.float32)).astype(jnp.bfloat16)
    return ((cos_high, cos_low), (sin_high, sin_low))


def split_dot(table_pair, values):
    return jnp.dot(table_pair[0], values, preferred_element_type=jnp.float32) + jnp.dot(
        table_pair[1], values, preferred_element_type=jnp.float32
    )


def rotate(cos_table, sin_table, value_re, value_im, direction):
    part_re = split_dot(cos_table, value_re) - direction * split_dot(sin_table, value_im)
    part_im = split_dot(cos_table, value_im) + direction * split_dot(sin_table, value_re)
    return (part_re, part_im)


def body(retarded, self_energy, energy_of):
    component = lax.axis_index("comp")
    momentum = component // 2
    greater = component % 2
    tile_count = lax.axis_size("tile")
    rep_count = lax.axis_size("rep")
    green_matrix = lax.dynamic_index_in_dim(retarded, momentum, 0, keepdims=False)
    sigma_matrix = self_energy[0]
    green_re, green_im = (green_matrix[:, 0], green_matrix[:, 1])
    sigma_re, sigma_im = (sigma_matrix[:, 0], sigma_matrix[:, 1])
    left_re = (
        batched(green_re, sigma_re, "eik,ekj->eij") - batched(green_im, sigma_im, "eik,ekj->eij")
    ).astype(jnp.bfloat16)
    left_im = (
        batched(green_re, sigma_im, "eik,ekj->eij") + batched(green_im, sigma_re, "eik,ekj->eij")
    ).astype(jnp.bfloat16)
    out_re = batched(left_re, green_re, "eik,ejk->eij") + batched(left_im, green_im, "eik,ejk->eij")
    out_im = batched(left_im, green_re, "eik,ejk->eij") - batched(left_re, green_im, "eik,ejk->eij")
    stacked = jnp.stack([out_re, out_im]).astype(jnp.bfloat16)
    stacked = jnp.where(greater == 1, jnp.swapaxes(stacked, 2, 3), stacked)
    energy_dev = stacked.shape[1]
    block_order = stacked.shape[2]
    elem_count = block_order * block_order // (tile_count * rep_count)
    slot_count = energy_of.shape[0]
    blocks = stacked.reshape(2, energy_dev, rep_count, tile_count, elem_count)
    first_pass = lax.all_to_all(blocks, "rep", split_axis=2, concat_axis=1, tiled=True)
    gathered = lax.all_to_all(first_pass, "tile", split_axis=3, concat_axis=1, tiled=True)
    signal = gathered.reshape(2, slot_count, elem_count)
    freq_count = 2 * slot_count
    frequency = lax.iota(jnp.int32, freq_count)
    fwd_cos, fwd_sin = phase_tables(frequency, energy_of, freq_count)
    own_re, own_im = rotate(fwd_cos, fwd_sin, signal[0], signal[1], -1.0)
    partner = from_partner(signal, "comp", 0)
    other_re, other_im = rotate(fwd_cos, fwd_sin, partner[0], partner[1], 1.0)
    cross_re = (own_re * other_re - own_im * other_im).astype(jnp.bfloat16)
    cross_im = (own_re * other_im + own_im * other_re).astype(jnp.bfloat16)
    lag_index = lax.iota(jnp.int32, slot_count)
    inv_cos, inv_sin = phase_tables(lag_index, frequency, freq_count)
    back_re, back_im = rotate(inv_cos, inv_sin, cross_re, cross_im, 1.0)
    norm_factor = 1.0 / (freq_count * math.sqrt(slot_count))
    polar_parts = jnp.stack([back_im * norm_factor, -back_re * norm_factor], axis=1)
    regrouped = lax.all_to_all(
        polar_parts[:, :, None, :], "tile", split_axis=0, concat_axis=2, tiled=True
    )
    lag_count = slot_count // tile_count
    return regrouped.reshape(lag_count, 2, block_order // rep_count, block_order)[None]


LANES = 128
ROWS = 8
KERNEL_BYTES = 62 * 2**20


def matmul(left_side, right_side, contract):
    return lax.dot_general(
        left_side, right_side, (((1,), (contract,)), ((), ())), preferred_element_type=jnp.float32
    )


def rotated(values):
    return pltpu.roll(values, LANES // 2, axis=1)


def polar_kernel(
    axis_sizes,
    retarded,
    self_energy,
    energy_of,
    arrived,
    green_in,
    sigma_in,
    energies,
    outgoing,
    ordered,
    lagged,
    load_sem,
    first_send,
    first_recv,
    second_send,
    second_recv,
    keep_sem,
    *gathered,
):
    tile_count, rep_count = axis_sizes
    component = lax.axis_index("comp")
    tile = lax.axis_index("tile")
    rep = lax.axis_index("rep")
    momentum = component // 2
    greater = component % 2
    energy_dev, block_order = green_in.shape[0], green_in.shape[2]
    slot_count = energies.shape[0]
    unit_count = arrived.shape[0]
    lag_count = arrived.shape[1]
    row_count = block_order // rep_count
    low_units = row_count // ROWS
    owner_count = 2 * tile_count
    peer_count = owner_count * rep_count
    base_units = unit_count // owner_count
    has_spare = unit_count % owner_count != 0

    owner = tile * 2 + greater

    def first_unit(which):
        return which * unit_count // owner_count

    def takes_spare(which):
        return first_unit(which + 1) - first_unit(which) > base_units

    half = tile_count // 2
    if tile_count % 2 == 0:
        own_half = tile // half * half
        other_half = (own_half + half) % tile_count
        tiles = [own_half + (tile + step) % half for step in range(half)]
        tiles += [other_half + (tile + step) % half for step in range(half)]
    else:
        tiles = [(tile + step) % tile_count for step in range(tile_count)]
    reps = [(rep + step) % rep_count for step in range(rep_count)]
    parts = [greater, 1 - greater]
    owners = [[tiles[i] * 2 + parts[j] for j in range(2)] for i in range(tile_count)]
    firsts = [[first_unit(owners[i][j]) for j in range(2)] for i in range(tile_count)]
    spares_at = [[takes_spare(owners[i][j]) for j in range(2)] for i in range(tile_count)]
    far_first = [(step + half) % tile_count for step in range(tile_count)]
    near_owners = [(i, j) for i in far_first for j in range(2) if (i, j) != (0, 0)]
    peers = [
        (i, j, k)
        for i in far_first
        for k in reversed(range(rep_count))
        for j in range(2)
        if (i, j, k) != (0, 0, 0)
    ]

    def device_of(i, j, k):
        return (momentum * 2 + parts[j], tiles[i], reps[k])

    loads = []
    for energy in range(energy_dev):
        loads.append(
            (
                pltpu.make_async_copy(
                    retarded.at[momentum, energy], green_in.at[energy], load_sem.at[2 * energy]
                ),
                pltpu.make_async_copy(
                    self_energy.at[0, energy], sigma_in.at[energy], load_sem.at[2 * energy + 1]
                ),
            )
        )
        for load in loads[-1]:
            load.start()
    energy_load = pltpu.make_async_copy(energy_of, energies, load_sem.at[2 * energy_dev])
    energy_load.start()

    barrier = pltpu.get_barrier_semaphore()
    for peer in peers:
        pl.semaphore_signal(
            barrier,
            inc=1,
            device_id=device_of(*peer),
            device_id_type=pl.DeviceIdType.MESH,
        )

    def finish(energy, left, right, sign):
        low, high = slice(0, LANES), slice(LANES, block_order)
        right_re, right_im = right
        with_re = jnp.concatenate(
            [right_re[low], -sign * right_im[low], right_re[high], -sign * right_im[high]]
        )
        with_im = jnp.concatenate(
            [right_im[low], sign * right_re[low], right_im[high], sign * right_re[high]]
        )
        result = matmul(left[0], with_re, 1) + matmul(left[1], with_im, 1)
        is_low = lax.broadcasted_iota(jnp.int32, (row_count // 2, LANES), 1) < LANES // 2
        for part in range(rep_count):
            rows = slice(part * row_count, (part + 1) * row_count)
            mixed = result[rows, 2 * LANES :]
            upper, lower = mixed[: row_count // 2], mixed[row_count // 2 :]
            high_re = jnp.where(is_low, upper, rotated(lower))
            high_im = jnp.where(is_low, rotated(upper), lower)
            pieces_re = jnp.concatenate([result[rows, :LANES], high_re])
            pieces_im = jnp.concatenate([result[rows, LANES : 2 * LANES], high_im])
            packed = jnp.concatenate(
                [
                    pieces_re.reshape(unit_count, ROWS, LANES),
                    pieces_im.reshape(unit_count, ROWS, LANES),
                ],
                axis=1,
            )
            outgoing[part, :, energy] = packed.astype(jnp.bfloat16)

    my_slot = greater * slot_count + (tile * rep_count + rep) * energy_dev

    def send_first(unit):
        for i, j, k in peers:
            copy = pltpu.make_async_remote_copy(
                src_ref=outgoing.at[reps[k], firsts[i][j] + unit],
                dst_ref=gathered[unit].at[pl.ds(my_slot, energy_dev)],
                send_sem=first_send.at[unit],
                recv_sem=first_recv.at[unit],
                device_id=device_of(i, j, k),
                device_id_type=pl.DeviceIdType.MESH,
            )
            if unit < base_units:
                copy.start()
            else:
                pl.when(spares_at[i][j])(copy.start)

    def keep_own(unit):
        gathered[unit][pl.ds(my_slot, energy_dev)] = outgoing[rep, firsts[0][0] + unit]

    for energy in range(energy_dev):
        for load in loads[energy]:
            load.wait()
        green_re, green_im = green_in[energy, 0], green_in[energy, 1]
        both = jnp.concatenate([green_re, green_im])
        by_re = matmul(both, sigma_in[energy, 0], 0)
        by_im = matmul(both, sigma_in[energy, 1], 0)
        left_re = (by_re[:block_order] - by_im[block_order:]).astype(jnp.bfloat16)
        left_im = (by_im[:block_order] + by_re[block_order:]).astype(jnp.bfloat16)

        @pl.when(greater == 0)
        def _():
            finish(energy, (left_re, left_im), (green_re, green_im), 1)

        @pl.when(greater == 1)
        def _():
            finish(energy, (green_re, green_im), (left_re, left_im), -1)

    pl.semaphore_wait(barrier, peer_count - 1)
    unit_order = [0] + [base_units] * has_spare + list(range(1, base_units))
    for unit in unit_order:
        send_first(unit)

    def wait_for(buffer, sem):
        pltpu.make_async_copy(buffer, buffer, sem).wait()

    for unit in range(base_units):
        keep_own(unit)
    if has_spare:
        pl.when(spares_at[0][0])(functools.partial(keep_own, base_units))

    energy_load.wait()
    slots = []
    for energy in range(slot_count):
        slot = 0
        for candidate in range(slot_count):
            slot = jnp.where(energies[candidate] == energy, candidate, slot)
        slots.append(slot)

    norm_factor = 1.0 / math.sqrt(slot_count)

    def keep_lags(unit):
        return pltpu.make_async_copy(
            lagged.at[unit, greater, pl.ds(tile * lag_count, lag_count)],
            arrived.at[firsts[0][0] + unit],
            keep_sem.at[unit],
        )

    def correlate(unit):
        wait_for(
            gathered[unit].at[pl.ds(0, (peer_count - 1) * energy_dev)], first_recv.at[unit]
        )
        for part in range(2):
            for energy in range(slot_count):
                ordered[part, energy] = gathered[unit][part * slot_count + slots[energy]].astype(
                    jnp.float32
                )
        for lag in range(slot_count):
            for part in range(2):
                own_re = ordered[part, lag:, :ROWS]
                own_im = ordered[part, lag:, ROWS:]
                other_re = ordered[1 - part, : slot_count - lag, :ROWS]
                other_im = ordered[1 - part, : slot_count - lag, ROWS:]
                sum_re = jnp.sum(own_re * other_re - own_im * other_im, axis=0)
                sum_im = jnp.sum(own_re * other_im + own_im * other_re, axis=0)
                lagged[unit, part, lag] = jnp.concatenate(
                    [sum_im * norm_factor, sum_re * -norm_factor]
                ).astype(jnp.bfloat16)
        my_unit = firsts[0][0] + unit
        for i, j in near_owners:
            pltpu.make_async_remote_copy(
                src_ref=lagged.at[unit, parts[j], pl.ds(tiles[i] * lag_count, lag_count)],
                dst_ref=arrived.at[my_unit],
                send_sem=second_send.at[unit],
                recv_sem=second_recv.at[unit],
                device_id=device_of(i, j, 0),
                device_id_type=pl.DeviceIdType.MESH,
            ).start()
        keep_lags(unit).start()

    for unit in unit_order:
        if unit < base_units:
            correlate(unit)
        else:
            pl.when(spares_at[0][0])(functools.partial(correlate, unit))

    for unit in range(base_units):
        wait_for(
            gathered[unit].at[pl.ds(0, (peer_count - 1) * energy_dev)], first_send.at[unit]
        )
        wait_for(arrived.at[pl.ds(0, owner_count - 1)], second_send.at[unit])
        wait_for(arrived.at[pl.ds(0, owner_count - 1)], second_recv.at[unit])
        keep_lags(unit).wait()
    if has_spare:
        spare_units = unit_count % owner_count
        spares = spare_units * rep_count

        @pl.when(spares_at[0][0])
        def _():
            if spares > 1:
                wait_for(
                    gathered[base_units].at[pl.ds(0, (spares - 1) * energy_dev)],
                    first_send.at[base_units],
                )
            wait_for(arrived.at[pl.ds(0, owner_count - 1)], second_send.at[base_units])
            keep_lags(base_units).wait()
            if spare_units > 1:
                wait_for(arrived.at[pl.ds(0, spare_units - 1)], second_recv.at[base_units])

        @pl.when(jnp.logical_not(spares_at[0][0]))
        def _():
            wait_for(
                gathered[base_units].at[pl.ds(0, spares * energy_dev)], first_send.at[base_units]
            )
            wait_for(arrived.at[pl.ds(0, spare_units)], second_recv.at[base_units])


def unpack_kernel(arrived, polar, packed, unpacked, load_sem, store_sem):
    unit_count, lag_count = arrived.shape[:2]
    row_count = polar.shape[3]
    low_units = row_count // ROWS
    load = pltpu.make_async_copy(arrived, packed, load_sem)
    stores = [
        pltpu.make_async_copy(unpacked.at[lag], polar.at[0, lag], store_sem.at[lag])
        for lag in range(lag_count)
    ]
    load.start()
    load.wait()
    for lag in range(lag_count):
        for unit in range(unit_count):
            values = packed[unit, lag].astype(jnp.float32)
            for part in range(2):
                block = values[part * ROWS : (part + 1) * ROWS]
                if unit < low_units:
                    unpacked[lag, part, unit * ROWS : (unit + 1) * ROWS, :LANES] = block
                else:
                    row = (unit - low_units) * ROWS
                    row_low = row + row_count // 2
                    unpacked[lag, part, row : row + ROWS, LANES:] = block[:, : LANES // 2]
                    unpacked[lag, part, row_low : row_low + ROWS, LANES:] = rotated(block)[
                        :, : LANES // 2
                    ]
        stores[lag].start()
    for store in stores:
        store.wait()


def fits(sizes, energy_dev, block_order):
    comp_count, tile_count, rep_count = sizes
    return (
        comp_count % 2 == 0
        and block_order == LANES + LANES // 2
        and block_order % (2 * ROWS * 2 * rep_count) == 0
        and block_order * 3 // (4 * ROWS * rep_count) >= 2 * tile_count
        and tile_count * rep_count * energy_dev <= 4 * ROWS
    )


def fused(sizes, retarded, self_energy, energy_of):
    _, tile_count, rep_count = sizes
    energy_dev, block_order = retarded.shape[1], retarded.shape[-1]
    slot_count = energy_of.shape[0]
    lag_count = slot_count // tile_count
    row_count = block_order // rep_count
    unit_count = row_count * block_order // (ROWS * LANES)
    units_held = -(-unit_count // (2 * tile_count))
    packed = (2 * ROWS, LANES)
    arrived = pl.pallas_call(
        functools.partial(polar_kernel, (tile_count, rep_count)),
        out_shape=jax.ShapeDtypeStruct((unit_count, lag_count) + packed, jnp.bfloat16),
        in_specs=[pl.BlockSpec(memory_space=pl.ANY)] * 3,
        out_specs=pl.BlockSpec(memory_space=pl.ANY),
        scratch_shapes=[
            pltpu.VMEM(retarded.shape[1:], jnp.bfloat16),
            pltpu.VMEM(self_energy.shape[1:], jnp.bfloat16),
            pltpu.SMEM((slot_count,), jnp.int32),
            pltpu.VMEM((rep_count, unit_count, energy_dev) + packed, jnp.bfloat16),
            pltpu.VMEM((2, slot_count) + packed, jnp.float32),
            pltpu.VMEM((units_held, 2, slot_count) + packed, jnp.bfloat16),
            pltpu.SemaphoreType.DMA((2 * energy_dev + 1,)),
            pltpu.SemaphoreType.DMA((units_held,)),
            pltpu.SemaphoreType.DMA((units_held,)),
            pltpu.SemaphoreType.DMA((units_held,)),
            pltpu.SemaphoreType.DMA((units_held,)),
            pltpu.SemaphoreType.DMA((units_held,)),
        ]
        + [pltpu.VMEM((2 * slot_count,) + packed, jnp.bfloat16)] * units_held,
        compiler_params=pltpu.CompilerParams(
            collective_id=0, has_side_effects=True, vmem_limit_bytes=KERNEL_BYTES
        ),
    )(retarded, self_energy, energy_of)
    return pl.pallas_call(
        unpack_kernel,
        out_shape=jax.ShapeDtypeStruct((1, lag_count, 2, row_count, block_order), jnp.float32),
        in_specs=[pl.BlockSpec(memory_space=pl.ANY)],
        out_specs=pl.BlockSpec(memory_space=pl.ANY),
        scratch_shapes=[
            pltpu.VMEM((unit_count, lag_count) + packed, jnp.bfloat16),
            pltpu.VMEM((lag_count, 2, row_count, block_order), jnp.float32),
            pltpu.SemaphoreType.DMA,
            pltpu.SemaphoreType.DMA((lag_count,)),
        ],
        compiler_params=pltpu.CompilerParams(vmem_limit_bytes=KERNEL_BYTES),
    )(arrived)


def solution(mesh):
    placed = (
        P(None, ("tile", "rep"), None, None, None),
        P("comp", ("tile", "rep"), None, None, None),
        P(),
    )
    sizes = tuple(mesh.shape[name] for name in ("comp", "tile", "rep"))

    def device_body(retarded, self_energy, energy_of):
        if fits(sizes, retarded.shape[1], retarded.shape[-1]):
            return fused(sizes, retarded, self_energy, energy_of)
        return body(retarded, self_energy, energy_of)

    return jax.shard_map(
        device_body,
        mesh=mesh,
        in_specs=placed,
        out_specs=P("comp", "tile", None, "rep", None),
        check_vma=False,
    )
```

```python
import functools
import math

import jax
import jax.numpy as jnp
from jax import lax
from jax.experimental import pallas as pl
from jax.experimental.pallas import tpu as pltpu
from jax.sharding import PartitionSpec as P


def from_partner(array, axis, distance):
    return lax.ppermute(array, axis, [(i, i ^ 1 << distance) for i in range(lax.axis_size(axis))])


def batched(left_side, right_side, pattern):
    return jnp.einsum(pattern, left_side, right_side, preferred_element_type=jnp.float32)


def phase_tables(row_values, col_values, modulus):
    phase_index = row_values[:, None] * col_values[None, :] % modulus
    phase_angle = phase_index.astype(jnp.float32) * (2.0 * math.pi / modulus)
    cos_full = jnp.cos(phase_angle)
    sin_full = jnp.sin(phase_angle)
    cos_high = cos_full.astype(jnp.bfloat16)
    sin_high = sin_full.astype(jnp.bfloat16)
    cos_low = (cos_full - cos_high.astype(jnp.float32)).astype(jnp.bfloat16)
    sin_low = (sin_full - sin_high.astype(jnp.float32)).astype(jnp.bfloat16)
    return ((cos_high, cos_low), (sin_high, sin_low))


def split_dot(table_pair, values):
    return jnp.dot(table_pair[0], values, preferred_element_type=jnp.float32) + jnp.dot(
        table_pair[1], values, preferred_element_type=jnp.float32
    )


def rotate(cos_table, sin_table, value_re, value_im, direction):
    part_re = split_dot(cos_table, value_re) - direction * split_dot(sin_table, value_im)
    part_im = split_dot(cos_table, value_im) + direction * split_dot(sin_table, value_re)
    return (part_re, part_im)


def body(retarded, self_energy, energy_of):
    component = lax.axis_index("comp")
    momentum = component // 2
    greater = component % 2
    tile_count = lax.axis_size("tile")
    rep_count = lax.axis_size("rep")
    green_matrix = lax.dynamic_index_in_dim(retarded, momentum, 0, keepdims=False)
    sigma_matrix = self_energy[0]
    green_re, green_im = (green_matrix[:, 0], green_matrix[:, 1])
    sigma_re, sigma_im = (sigma_matrix[:, 0], sigma_matrix[:, 1])
    left_re = (
        batched(green_re, sigma_re, "eik,ekj->eij") - batched(green_im, sigma_im, "eik,ekj->eij")
    ).astype(jnp.bfloat16)
    left_im = (
        batched(green_re, sigma_im, "eik,ekj->eij") + batched(green_im, sigma_re, "eik,ekj->eij")
    ).astype(jnp.bfloat16)
    out_re = batched(left_re, green_re, "eik,ejk->eij") + batched(left_im, green_im, "eik,ejk->eij")
    out_im = batched(left_im, green_re, "eik,ejk->eij") - batched(left_re, green_im, "eik,ejk->eij")
    stacked = jnp.stack([out_re, out_im]).astype(jnp.bfloat16)
    stacked = jnp.where(greater == 1, jnp.swapaxes(stacked, 2, 3), stacked)
    energy_dev = stacked.shape[1]
    block_order = stacked.shape[2]
    elem_count = block_order * block_order // (tile_count * rep_count)
    slot_count = energy_of.shape[0]
    blocks = stacked.reshape(2, energy_dev, rep_count, tile_count, elem_count)
    first_pass = lax.all_to_all(blocks, "rep", split_axis=2, concat_axis=1, tiled=True)
    gathered = lax.all_to_all(first_pass, "tile", split_axis=3, concat_axis=1, tiled=True)
    signal = gathered.reshape(2, slot_count, elem_count)
    freq_count = 2 * slot_count
    frequency = lax.iota(jnp.int32, freq_count)
    fwd_cos, fwd_sin = phase_tables(frequency, energy_of, freq_count)
    own_re, own_im = rotate(fwd_cos, fwd_sin, signal[0], signal[1], -1.0)
    partner = from_partner(signal, "comp", 0)
    other_re, other_im = rotate(fwd_cos, fwd_sin, partner[0], partner[1], 1.0)
    cross_re = (own_re * other_re - own_im * other_im).astype(jnp.bfloat16)
    cross_im = (own_re * other_im + own_im * other_re).astype(jnp.bfloat16)
    lag_index = lax.iota(jnp.int32, slot_count)
    inv_cos, inv_sin = phase_tables(lag_index, frequency, freq_count)
    back_re, back_im = rotate(inv_cos, inv_sin, cross_re, cross_im, 1.0)
    norm_factor = 1.0 / (freq_count * math.sqrt(slot_count))
    polar_parts = jnp.stack([back_im * norm_factor, -back_re * norm_factor], axis=1)
    regrouped = lax.all_to_all(
        polar_parts[:, :, None, :], "tile", split_axis=0, concat_axis=2, tiled=True
    )
    lag_count = slot_count // tile_count
    return regrouped.reshape(lag_count, 2, block_order // rep_count, block_order)[None]


LANES = 128
ROWS = 8
KERNEL_BYTES = 62 * 2**20


def matmul(left_side, right_side, contract):
    return lax.dot_general(
        left_side, right_side, (((1,), (contract,)), ((), ())), preferred_element_type=jnp.float32
    )


def rotated(values):
    return pltpu.roll(values, LANES // 2, axis=1)


def polar_kernel(
    axis_sizes,
    retarded,
    self_energy,
    energy_of,
    arrived,
    green_in,
    sigma_in,
    energies,
    outgoing,
    ordered,
    lagged,
    load_sem,
    first_send,
    first_recv,
    second_send,
    second_recv,
    keep_sem,
    *gathered,
):
    tile_count, rep_count = axis_sizes
    component = lax.axis_index("comp")
    tile = lax.axis_index("tile")
    rep = lax.axis_index("rep")
    momentum = component // 2
    greater = component % 2
    energy_dev, block_order = green_in.shape[0], green_in.shape[2]
    slot_count = energies.shape[0]
    unit_count = arrived.shape[0]
    lag_count = arrived.shape[1]
    row_count = block_order // rep_count
    low_units = row_count // ROWS
    owner_count = 2 * tile_count
    peer_count = owner_count * rep_count
    base_units = unit_count // owner_count
    has_spare = unit_count % owner_count != 0

    owner = tile * 2 + greater

    def first_unit(which):
        return which * unit_count // owner_count

    def takes_spare(which):
        return first_unit(which + 1) - first_unit(which) > base_units

    half = tile_count // 2
    if tile_count % 2 == 0:
        own_half = tile // half * half
        other_half = (own_half + half) % tile_count
        tiles = [own_half + (tile + step) % half for step in range(half)]
        tiles += [other_half + (tile + step) % half for step in range(half)]
    else:
        tiles = [(tile + step) % tile_count for step in range(tile_count)]
    reps = [(rep + step) % rep_count for step in range(rep_count)]
    parts = [greater, 1 - greater]
    owners = [[tiles[i] * 2 + parts[j] for j in range(2)] for i in range(tile_count)]
    firsts = [[first_unit(owners[i][j]) for j in range(2)] for i in range(tile_count)]
    spares_at = [[takes_spare(owners[i][j]) for j in range(2)] for i in range(tile_count)]
    far_first = [(step + half) % tile_count for step in range(tile_count)]
    peers = [
        (i, j, k)
        for i in far_first
        for k in reversed(range(rep_count))
        for j in range(2)
        if (i, j, k) != (0, 0, 0)
    ]

    def device_of(i, j, k):
        return (momentum * 2 + parts[j], tiles[i], reps[k])

    loads = []
    for energy in range(energy_dev):
        loads.append(
            (
                pltpu.make_async_copy(
                    retarded.at[momentum, energy], green_in.at[energy], load_sem.at[2 * energy]
                ),
                pltpu.make_async_copy(
                    self_energy.at[0, energy], sigma_in.at[energy], load_sem.at[2 * energy + 1]
                ),
            )
        )
        for load in loads[-1]:
            load.start()
    energy_load = pltpu.make_async_copy(energy_of, energies, load_sem.at[2 * energy_dev])
    energy_load.start()

    barrier = pltpu.get_barrier_semaphore()
    for peer in peers:
        pl.semaphore_signal(
            barrier,
            inc=1,
            device_id=device_of(*peer),
            device_id_type=pl.DeviceIdType.MESH,
        )

    def finish(energy, left, right, sign):
        low, high = slice(0, LANES), slice(LANES, block_order)
        right_re, right_im = right
        with_re = jnp.concatenate(
            [right_re[low], -sign * right_im[low], right_re[high], -sign * right_im[high]]
        )
        with_im = jnp.concatenate(
            [right_im[low], sign * right_re[low], right_im[high], sign * right_re[high]]
        )
        result = matmul(left[0], with_re, 1) + matmul(left[1], with_im, 1)
        is_low = lax.broadcasted_iota(jnp.int32, (row_count // 2, LANES), 1) < LANES // 2
        for part in range(rep_count):
            rows = slice(part * row_count, (part + 1) * row_count)
            mixed = result[rows, 2 * LANES :]
            upper, lower = mixed[: row_count // 2], mixed[row_count // 2 :]
            high_re = jnp.where(is_low, upper, rotated(lower))
            high_im = jnp.where(is_low, rotated(upper), lower)
            pieces_re = jnp.concatenate([result[rows, :LANES], high_re])
            pieces_im = jnp.concatenate([result[rows, LANES : 2 * LANES], high_im])
            packed = jnp.concatenate(
                [
                    pieces_re.reshape(unit_count, ROWS, LANES),
                    pieces_im.reshape(unit_count, ROWS, LANES),
                ],
                axis=1,
            )
            outgoing[part, :, energy] = packed.astype(jnp.bfloat16)

    my_slot = greater * slot_count + (tile * rep_count + rep) * energy_dev

    def send_first(unit):
        for i, j, k in peers:
            copy = pltpu.make_async_remote_copy(
                src_ref=outgoing.at[reps[k], firsts[i][j] + unit],
                dst_ref=gathered[unit].at[pl.ds(my_slot, energy_dev)],
                send_sem=first_send.at[unit],
                recv_sem=first_recv.at[unit],
                device_id=device_of(i, j, k),
                device_id_type=pl.DeviceIdType.MESH,
            )
            if unit < base_units:
                copy.start()
            else:
                pl.when(spares_at[i][j])(copy.start)

    def keep_own(unit):
        gathered[unit][pl.ds(my_slot, energy_dev)] = outgoing[rep, firsts[0][0] + unit]

    for energy in range(energy_dev):
        for load in loads[energy]:
            load.wait()
        green_re, green_im = green_in[energy, 0], green_in[energy, 1]
        both = jnp.concatenate([green_re, green_im])
        by_re = matmul(both, sigma_in[energy, 0], 0)
        by_im = matmul(both, sigma_in[energy, 1], 0)
        left_re = (by_re[:block_order] - by_im[block_order:]).astype(jnp.bfloat16)
        left_im = (by_im[:block_order] + by_re[block_order:]).astype(jnp.bfloat16)

        @pl.when(greater == 0)
        def _():
            finish(energy, (left_re, left_im), (green_re, green_im), 1)

        @pl.when(greater == 1)
        def _():
            finish(energy, (green_re, green_im), (left_re, left_im), -1)

    pl.semaphore_wait(barrier, peer_count - 1)
    unit_order = [0] + [base_units] * has_spare + list(range(1, base_units))
    for unit in unit_order:
        send_first(unit)

    def wait_for(buffer, sem):
        pltpu.make_async_copy(buffer, buffer, sem).wait()

    for unit in range(base_units):
        keep_own(unit)
    if has_spare:
        pl.when(spares_at[0][0])(functools.partial(keep_own, base_units))

    energy_load.wait()
    slots = []
    for energy in range(slot_count):
        slot = 0
        for candidate in range(slot_count):
            slot = jnp.where(energies[candidate] == energy, candidate, slot)
        slots.append(slot)

    norm_factor = 1.0 / math.sqrt(slot_count)

    def keep_lags(unit):
        return pltpu.make_async_copy(
            lagged.at[unit, greater, pl.ds(tile * lag_count, lag_count)],
            arrived.at[firsts[0][0] + unit],
            keep_sem.at[unit],
        )

    def correlate(unit):
        wait_for(
            gathered[unit].at[pl.ds(0, (peer_count - 1) * energy_dev)], first_recv.at[unit]
        )
        for part in range(2):
            for energy in range(slot_count):
                ordered[part, energy] = gathered[unit][part * slot_count + slots[energy]].astype(
                    jnp.float32
                )
        def sum_lags(block):
            for lag in range(block * lag_count, (block + 1) * lag_count):
                for part in range(2):
                    own_re = ordered[part, lag:, :ROWS]
                    own_im = ordered[part, lag:, ROWS:]
                    other_re = ordered[1 - part, : slot_count - lag, :ROWS]
                    other_im = ordered[1 - part, : slot_count - lag, ROWS:]
                    sum_re = jnp.sum(own_re * other_re - own_im * other_im, axis=0)
                    sum_im = jnp.sum(own_re * other_im + own_im * other_re, axis=0)
                    lagged[unit, part, lag] = jnp.concatenate(
                        [sum_im * norm_factor, sum_re * -norm_factor]
                    ).astype(jnp.bfloat16)
            for part in range(2):
                copy = pltpu.make_async_remote_copy(
                    src_ref=lagged.at[unit, part, pl.ds(block * lag_count, lag_count)],
                    dst_ref=arrived.at[firsts[0][0] + unit],
                    send_sem=second_send.at[unit],
                    recv_sem=second_recv.at[unit],
                    device_id=(momentum * 2 + part, block, rep),
                    device_id_type=pl.DeviceIdType.MESH,
                )
                here = owner == block * 2 + part
                pl.when(jnp.logical_not(here))(copy.start)
                pl.when(here)(keep_lags(unit).start)

        @pl.when(tile < half)
        def _():
            for block in reversed(range(tile_count)):
                sum_lags(block)

        @pl.when(tile >= half)
        def _():
            for block in range(tile_count):
                sum_lags(block)

    for unit in unit_order:
        if unit < base_units:
            correlate(unit)
        else:
            pl.when(spares_at[0][0])(functools.partial(correlate, unit))

    for unit in range(base_units):
        wait_for(
            gathered[unit].at[pl.ds(0, (peer_count - 1) * energy_dev)], first_send.at[unit]
        )
        wait_for(arrived.at[pl.ds(0, owner_count - 1)], second_send.at[unit])
        wait_for(arrived.at[pl.ds(0, owner_count - 1)], second_recv.at[unit])
        keep_lags(unit).wait()
    if has_spare:
        spare_units = unit_count % owner_count
        spares = spare_units * rep_count

        @pl.when(spares_at[0][0])
        def _():
            if spares > 1:
                wait_for(
                    gathered[base_units].at[pl.ds(0, (spares - 1) * energy_dev)],
                    first_send.at[base_units],
                )
            wait_for(arrived.at[pl.ds(0, owner_count - 1)], second_send.at[base_units])
            keep_lags(base_units).wait()
            if spare_units > 1:
                wait_for(arrived.at[pl.ds(0, spare_units - 1)], second_recv.at[base_units])

        @pl.when(jnp.logical_not(spares_at[0][0]))
        def _():
            wait_for(
                gathered[base_units].at[pl.ds(0, spares * energy_dev)], first_send.at[base_units]
            )
            wait_for(arrived.at[pl.ds(0, spare_units)], second_recv.at[base_units])


def unpack_kernel(arrived, polar, packed, unpacked, load_sem, store_sem):
    unit_count, lag_count = arrived.shape[:2]
    row_count = polar.shape[3]
    low_units = row_count // ROWS
    load = pltpu.make_async_copy(arrived, packed, load_sem)
    stores = [
        pltpu.make_async_copy(unpacked.at[lag], polar.at[0, lag], store_sem.at[lag])
        for lag in range(lag_count)
    ]
    load.start()
    load.wait()
    for lag in range(lag_count):
        for unit in range(unit_count):
            values = packed[unit, lag].astype(jnp.float32)
            for part in range(2):
                block = values[part * ROWS : (part + 1) * ROWS]
                if unit < low_units:
                    unpacked[lag, part, unit * ROWS : (unit + 1) * ROWS, :LANES] = block
                else:
                    row = (unit - low_units) * ROWS
                    row_low = row + row_count // 2
                    unpacked[lag, part, row : row + ROWS, LANES:] = block[:, : LANES // 2]
                    unpacked[lag, part, row_low : row_low + ROWS, LANES:] = rotated(block)[
                        :, : LANES // 2
                    ]
        stores[lag].start()
    for store in stores:
        store.wait()


def fits(sizes, energy_dev, block_order):
    comp_count, tile_count, rep_count = sizes
    return (
        comp_count % 2 == 0
        and block_order == LANES + LANES // 2
        and block_order % (2 * ROWS * 2 * rep_count) == 0
        and block_order * 3 // (4 * ROWS * rep_count) >= 2 * tile_count
        and tile_count * rep_count * energy_dev <= 4 * ROWS
    )


def fused(sizes, retarded, self_energy, energy_of):
    _, tile_count, rep_count = sizes
    energy_dev, block_order = retarded.shape[1], retarded.shape[-1]
    slot_count = energy_of.shape[0]
    lag_count = slot_count // tile_count
    row_count = block_order // rep_count
    unit_count = row_count * block_order // (ROWS * LANES)
    units_held = -(-unit_count // (2 * tile_count))
    packed = (2 * ROWS, LANES)
    arrived = pl.pallas_call(
        functools.partial(polar_kernel, (tile_count, rep_count)),
        out_shape=jax.ShapeDtypeStruct((unit_count, lag_count) + packed, jnp.bfloat16),
        in_specs=[pl.BlockSpec(memory_space=pl.ANY)] * 3,
        out_specs=pl.BlockSpec(memory_space=pl.ANY),
        scratch_shapes=[
            pltpu.VMEM(retarded.shape[1:], jnp.bfloat16),
            pltpu.VMEM(self_energy.shape[1:], jnp.bfloat16),
            pltpu.SMEM((slot_count,), jnp.int32),
            pltpu.VMEM((rep_count, unit_count, energy_dev) + packed, jnp.bfloat16),
            pltpu.VMEM((2, slot_count) + packed, jnp.float32),
            pltpu.VMEM((units_held, 2, slot_count) + packed, jnp.bfloat16),
            pltpu.SemaphoreType.DMA((2 * energy_dev + 1,)),
            pltpu.SemaphoreType.DMA((units_held,)),
            pltpu.SemaphoreType.DMA((units_held,)),
            pltpu.SemaphoreType.DMA((units_held,)),
            pltpu.SemaphoreType.DMA((units_held,)),
            pltpu.SemaphoreType.DMA((units_held,)),
        ]
        + [pltpu.VMEM((2 * slot_count,) + packed, jnp.bfloat16)] * units_held,
        compiler_params=pltpu.CompilerParams(
            collective_id=0, has_side_effects=True, vmem_limit_bytes=KERNEL_BYTES
        ),
    )(retarded, self_energy, energy_of)
    return pl.pallas_call(
        unpack_kernel,
        out_shape=jax.ShapeDtypeStruct((1, lag_count, 2, row_count, block_order), jnp.float32),
        in_specs=[pl.BlockSpec(memory_space=pl.ANY)],
        out_specs=pl.BlockSpec(memory_space=pl.ANY),
        scratch_shapes=[
            pltpu.VMEM((unit_count, lag_count) + packed, jnp.bfloat16),
            pltpu.VMEM((lag_count, 2, row_count, block_order), jnp.float32),
            pltpu.SemaphoreType.DMA,
            pltpu.SemaphoreType.DMA((lag_count,)),
        ],
        compiler_params=pltpu.CompilerParams(vmem_limit_bytes=KERNEL_BYTES),
    )(arrived)


def solution(mesh):
    placed = (
        P(None, ("tile", "rep"), None, None, None),
        P("comp", ("tile", "rep"), None, None, None),
        P(),
    )
    sizes = tuple(mesh.shape[name] for name in ("comp", "tile", "rep"))

    def device_body(retarded, self_energy, energy_of):
        if fits(sizes, retarded.shape[1], retarded.shape[-1]):
            return fused(sizes, retarded, self_energy, energy_of)
        return body(retarded, self_energy, energy_of)

    return jax.shard_map(
        device_body,
        mesh=mesh,
        in_specs=placed,
        out_specs=P("comp", "tile", None, "rep", None),
        check_vma=False,
    )
```
